32 devices in a mesh: dp: 8 (over z, core), tp: 4 (over y, x).
Axes of the slice: x: 2, y: 2, z: 4, core: 2. Of those that a mesh axis runs over, the one named last changes fastest.
Arguments:
- hidden: bfloat16 [8, 1024, 1536], P('dp', 'tp'), may hold values from -6 to 6
- segments: int32 [8, 1024], P('dp'), may hold values from 0 to 3, never falling along the last dimension, each value on 1 to 512 neighbouring positions
- cotangent: bfloat16 [8, 1024, 1536], P('dp', 'tp'), may hold values from -6 to 6
- w_query: bfloat16 [1, 1536, 1536], P(None, None, 'tp'), may hold values from -0.15625 to 0.15625
- w_keyval: bfloat16 [1, 1536, 8, 192], P(None, None, 'tp'), may hold values from -0.15625 to 0.15625
- w_output: bfloat16 [1, 1536, 1536], P(None, 'tp'), may hold values from -0.625 to 0.625
- w_gate: bfloat16 [1, 1536, 4096], P(None, None, 'tp'), may hold values from -0.15625 to 0.15625
- w_up: bfloat16 [1, 1536, 4096], P(None, None, 'tp'), may hold values from -0.15625 to 0.15625
- w_down: bfloat16 [1, 4096, 1536], P(None, 'tp'), may hold values from -0.09375 to 0.09375
- gains: float32 [1, 2, 1536], replicated, may hold values from 0.5 to 1.5
Outputs:
- result: bfloat16 [8, 1024, 1536], P('dp', 'tp')
- grad_hidden: bfloat16 [8, 1024, 1536], P('dp', 'tp')
- grad_query: float32 [1, 1536, 1536], P(None, None, 'tp')
- grad_keyval: float32 [1, 1536, 8, 192], P(None, None, 'tp')
- grad_output: float32 [1, 1536, 1536], P(None, 'tp')
- grad_gate: float32 [1, 1536, 4096], P(None, None, 'tp')
- grad_up: float32 [1, 1536, 4096], P(None, None, 'tp')
- grad_down: float32 [1, 4096, 1536], P(None, 'tp')
- grad_gains: float32 [1, 2, 1536], replicated
The draws below stay inside these ranges and needn't reach their ends.
All inputs are finite; a program needn't handle non-finite values.
Results may differ from the reference program's by a relative error of at most 0.014.
Values may be sent and summed in bfloat16 or wider, within the bound.
A program may use at most 256 MiB of HBM per device.

```python
import math
import jax
import jax.numpy as jnp
import numpy as np
from jax import lax

D = 1536
HQ = 16
KVH = 8
HD = 96
FF = 4096
LAYERS = 1
LEN = 1024
SEQS = 8


def levels(key, dims, shards, least, largest):
    def one(dim, parts):
        steps = jax.random.uniform(jax.random.fold_in(jax.random.fold_in(key, 6), dim), (parts,), jnp.float32, least / len(shards), largest / len(shards))
        return jnp.repeat(jnp.exp(steps), dims[dim] // parts).reshape((-1,) + (1,) * (len(dims) - dim - 1))

    level = one(*shards[0])
    for cut in shards[1:]:
        level = level * one(*cut)
    return level


def split_up(count, total, most, skew):
    weights = [(1 << 20) // math.isqrt(standing ** skew) + 1 for standing in range(2, count + 1)]
    rest, counts = total - most - (count - 1), [1] * (count - 1)
    while rest > 0:
        movable = [i for i in range(count - 1) if counts[i] < most]
        whole, left = sum([weights[i] for i in movable]), rest
        for i in movable:
            extra = min(most - counts[i], max(1, left * weights[i] // whole), rest)
            counts[i] = counts[i] + extra
            rest = rest - extra
    return np.array([most] + counts)


def uneven_parts(own_key, count, total, limit, slope):
    if count == 2:
        one = jax.random.randint(own_key, (), max(1, total - limit), min(limit, total - 1) + 1)
        return jnp.stack([one, total - one])
    tallies = jnp.asarray(split_up(count, total, limit, slope), jnp.int32)
    twos = (count - 1) // 2
    source_of, sink = tallies[1:1 + 2 * twos:2], tallies[2:2 + 2 * twos:2]
    room = jnp.minimum(source_of - 1, limit - sink)
    moved = jax.random.randint(jax.random.fold_in(own_key, 1), (twos,), 0, 1 << 20) % (room + 1)
    tallies = tallies.at[1:1 + 2 * twos:2].set(source_of - moved).at[2:2 + 2 * twos:2].set(sink + moved)
    return tallies[jax.random.permutation(jax.random.fold_in(own_key, 2), count)]


def scatter_about(stream_key, shape, scale, reach, split=(), held_as=jnp.bfloat16):
    factor_of = levels(stream_key, shape, split, -0.22, 0.18) if split else 1.0
    values = jax.random.normal(stream_key, shape, jnp.float32) * scale * factor_of
    return jnp.minimum(jnp.maximum(values, -reach), reach).astype(held_as)


def setup_inputs(seed: int = 0) -> dict:
    streams_of = jax.random.split(jax.random.key(seed), 11)
    hidden = scatter_about(streams_of[0], (SEQS, LEN, D), 1.0, 6.0, ((0, 8), (1, 4)))
    segments = jax.vmap(lambda own: jnp.searchsorted(jnp.cumsum(uneven_parts(own, 4, LEN, LEN // 2, 1)), jnp.arange(LEN), side="right"))(jax.random.split(streams_of[1], SEQS)).reshape((SEQS, LEN)).astype(jnp.int32)
    cotangent = scatter_about(streams_of[2], (SEQS, LEN, D), 1.0, 6.0, ((0, 8), (1, 4)))
    w_query = scatter_about(streams_of[3], (LAYERS, D, HQ * HD), D ** -0.5, 0.15625, ((2, 4),))
    w_keyval = scatter_about(streams_of[4], (LAYERS, D, KVH, 2 * HD), D ** -0.5, 0.15625, ((2, 4),))
    w_output = scatter_about(streams_of[5], (LAYERS, HQ * HD, D), (HQ * HD // 16) ** -0.5, 0.625, ((1, 4),))
    w_gate = scatter_about(streams_of[6], (LAYERS, D, FF), D ** -0.5, 0.15625, ((2, 4),))
    w_up = scatter_about(streams_of[7], (LAYERS, D, FF), D ** -0.5, 0.15625, ((2, 4),))
    w_down = scatter_about(streams_of[8], (LAYERS, FF, D), FF ** -0.5, 0.09375, ((1, 4),))
    gains = jnp.clip(1.0 + 0.1 * jax.random.normal(streams_of[9], (LAYERS, 2, D), jnp.float32), 0.5, 1.5)
    return {"hidden": hidden, "segments": segments, "cotangent": cotangent, "w_query": w_query, "w_keyval": w_keyval, "w_output": w_output, "w_gate": w_gate, "w_up": w_up, "w_down": w_down, "gains": gains}


@jax.custom_vjp
def low(v):
    return lax.optimization_barrier(v.astype(jnp.bfloat16)).astype(jnp.float32)

@jax.custom_vjp
def low_back(v):
    return v

def low_keep(v):
    return (low(v), None)

def low_pass(kept, grad):
    return (grad,)

def back_keep(v):
    return (v, None)

def back_low(kept, grad):
    return (low(grad),)
low.defvjp(low_keep, low_pass)
low_back.defvjp(back_keep, back_low)
epsilon = 1e-05
rope_base = 100000.0

def rms_norm(values, gain):
    return values * lax.rsqrt(lax.optimization_barrier(jnp.mean(values * values, axis=-1, keepdims=True)) + epsilon) * gain

def rotate(values, cos_table, sin_table):
    half_size = values.shape[-1] // 2
    first_half = values[..., :half_size]
    second_half = values[..., half_size:]
    return jnp.concatenate([first_half * cos_table - second_half * sin_table, second_half * cos_table + first_half * sin_table], axis=-1)

def positions_of(seg_row):
    index_row = jnp.arange(seg_row.shape[0], dtype=jnp.int32)
    starts = jnp.concatenate([jnp.ones((1,), jnp.int32), (seg_row[1:] != seg_row[:-1]).astype(jnp.int32)])
    first_index = lax.cummax(jnp.where(starts > 0, index_row, 0).astype(jnp.int32), axis=0)
    return index_row - first_index

def layer_forward(stream, visible, cos_table, sin_table, w_query, w_keyval, w_output, w_gate, w_up, w_down, gain_pair):
    highest = lax.Precision.HIGHEST
    seq_length = stream.shape[0]
    input_a = low(rms_norm(stream, gain_pair[0]))
    query = low_back(jnp.dot(input_a, w_query, precision=highest)).reshape(seq_length, HQ, HD)
    keyval = low_back(jnp.einsum('td,dgc->tgc', input_a, w_keyval, precision=highest))
    query_rot = low(rotate(query, cos_table, sin_table)).reshape(seq_length, KVH, HQ // KVH, HD)
    key_rot = low(rotate(keyval[:, :, :HD], cos_table, sin_table))
    value_low = low(keyval[:, :, HD:])
    scores = low_back(jnp.einsum('tgrc,ugc->grtu', query_rot, key_rot, precision=highest) * HD ** (-0.5))
    scores = jnp.where(visible[None, None], scores, -1e+30)
    probs = low(jax.nn.softmax(scores, axis=-1))
    mixed = jnp.einsum('grtu,ugc->tgrc', probs, value_low, precision=highest).reshape(seq_length, HQ * HD)
    mixed = low(low_back(mixed))
    middle = stream + low_back(jnp.dot(mixed, w_output, precision=highest))
    input_b = low(rms_norm(middle, gain_pair[1]))
    gate_pre = low_back(jnp.dot(input_b, w_gate, precision=highest))
    up_pre = low_back(jnp.dot(input_b, w_up, precision=highest))
    hidden_act = low(jax.nn.silu(gate_pre) * up_pre)
    return middle + low_back(jnp.dot(hidden_act, w_down, precision=highest))

def reference(hidden, segments, cotangent, w_query, w_keyval, w_output, w_gate, w_up, w_down, gains):
    weights = tuple((w.astype(jnp.float32) for w in (w_query, w_keyval, w_output, w_gate, w_up, w_down, gains)))
    inverse = rope_base ** (-(jnp.arange(HD // 2, dtype=jnp.float32) * 2.0) / HD)
    index_row = jnp.arange(LEN, dtype=jnp.int32)
    causal = index_row[:, None] >= index_row[None, :]

    def per_sequence(running, block_item):
        hidden_seq, seg_row, cotan_seq = block_item
        position = positions_of(seg_row)
        angles = position.astype(jnp.float32)[:, None] * inverse[None, :]
        cos_table = jnp.cos(angles)[:, None, :]
        sin_table = jnp.sin(angles)[:, None, :]
        visible = causal & (seg_row[:, None] == seg_row[None, :])

        def forward(stream, layer_weights):
            for layer_index in range(LAYERS):
                stream = layer_forward(stream, visible, cos_table, sin_table, *(w[layer_index] for w in layer_weights))
            return stream
        layer_out, pullback = jax.vjp(forward, hidden_seq.astype(jnp.float32), weights)
        grad_input, grad_weights = pullback(cotan_seq.astype(jnp.float32))
        running = tuple((r + g for r, g in zip(running, grad_weights)))
        return (running, (layer_out.astype(jnp.bfloat16), grad_input.astype(jnp.bfloat16)))
    zero_grads = tuple((jnp.zeros(w.shape, jnp.float32) for w in weights))
    grad_totals, (result, grad_hidden) = lax.scan(per_sequence, zero_grads, (hidden, segments, cotangent))
    return (result, grad_hidden, grad_totals[0], grad_totals[1], grad_totals[2], grad_totals[3], grad_totals[4], grad_totals[5], grad_totals[6])
```

```python
import jax
import jax.numpy as jnp
from jax import lax
from jax.sharding import PartitionSpec as P

HD = 96


epsilon = 1e-05
rope_base = 100000.0


def rope_tables(segments):
    seq_length = segments.shape[1]
    index_row = jnp.arange(seq_length, dtype=jnp.int32)
    first_index = jnp.sum(
        (segments[:, None, :] < segments[:, :, None]).astype(jnp.int32), axis=2
    )
    position = (index_row[None, :] - first_index).astype(jnp.float32)
    half_size = HD // 2
    inverse = rope_base ** (-(jnp.arange(half_size, dtype=jnp.float32) * 2.0) / HD)
    angles = position[:, :, None] * inverse[None, None, :]
    return (jnp.cos(angles)[:, :, None, :], jnp.sin(angles)[:, :, None, :])


def rotate(values, cos_table, sin_table):
    half_size = values.shape[-1] // 2
    first_half = values[..., :half_size]
    second_half = values[..., half_size:]
    return jnp.concatenate(
        [
            first_half * cos_table - second_half * sin_table,
            second_half * cos_table + first_half * sin_table,
        ],
        axis=-1,
    )


def unrotate(values, cos_table, sin_table):
    return rotate(values, cos_table, -sin_table)


def norm_forward(stream):
    inv_rms = lax.rsqrt(jnp.mean(stream * stream, axis=-1, keepdims=True) + epsilon)
    return (stream * inv_rms, inv_rms)


def norm_backward(grad_normed, normed, inv_rms, gain):
    scaled_grad = grad_normed * gain
    grad_in = inv_rms * (
        scaled_grad - normed * jnp.mean(scaled_grad * normed, axis=-1, keepdims=True)
    )
    return (grad_in, jnp.sum(grad_normed * normed, axis=(0, 1)))


def gather_tokens(values):
    return lax.all_gather(values, "tp", axis=1, tiled=True)


def gather_grads(values):
    return lax.all_gather(values, "tp", axis=1, tiled=True)


def sum_branch(terms):
    return lax.psum_scatter(terms, "tp", scatter_dimension=1, tiled=True)


def sum_inputs(terms):
    return lax.psum_scatter(terms, "tp", scatter_dimension=1, tiled=True)


def reduce_weights(grad_q, grad_kv, grad_o, grad_g, grad_u, grad_d):
    shares = (
        lax.psum_scatter(grad_q, "dp", scatter_dimension=1, tiled=True),
        lax.psum_scatter(grad_kv, "dp", scatter_dimension=1, tiled=True),
        lax.psum_scatter(grad_o, "dp", scatter_dimension=2, tiled=True),
        lax.psum_scatter(grad_g, "dp", scatter_dimension=1, tiled=True),
        lax.psum_scatter(grad_u, "dp", scatter_dimension=1, tiled=True),
        lax.psum_scatter(grad_d, "dp", scatter_dimension=2, tiled=True),
    )
    return (
        lax.all_gather(shares[0], "dp", axis=1, tiled=True),
        lax.all_gather(shares[1], "dp", axis=1, tiled=True),
        lax.all_gather(shares[2], "dp", axis=2, tiled=True),
        lax.all_gather(shares[3], "dp", axis=1, tiled=True),
        lax.all_gather(shares[4], "dp", axis=1, tiled=True),
        lax.all_gather(shares[5], "dp", axis=2, tiled=True),
    )


def project_attention(gathered, w_query, w_keyval, cos_table, sin_table):
    seq_count, seq_length, _ = gathered.shape
    query = jnp.einsum("std,dc->stc", gathered, w_query, preferred_element_type=jnp.float32)
    keyval = jnp.einsum("std,dgc->stgc", gathered, w_keyval, preferred_element_type=jnp.float32)
    head_size = keyval.shape[-1] // 2
    query = query.reshape(seq_count, seq_length, -1, head_size)
    query_rot = rotate(query, cos_table, sin_table).astype(jnp.bfloat16)
    key_rot = rotate(keyval[..., :head_size], cos_table, sin_table).astype(jnp.bfloat16)
    value_low = keyval[..., head_size:].astype(jnp.bfloat16)
    return (query_rot, key_rot, value_low)


def attend_one(block_item):
    query_rot, key_rot, value_low, visible = block_item
    seq_length, kv_heads, head_size = key_rot.shape
    grouped = query_rot.reshape(seq_length, kv_heads, -1, head_size)
    scores = jnp.einsum(
        "tgrc,ugc->grtu", grouped, key_rot, preferred_element_type=jnp.float32
    ) * head_size ** (-0.5)
    scores = jnp.where(visible[None, None], scores, -1e30)
    row_peak = jnp.max(scores, axis=-1, keepdims=True)
    expd = jnp.exp(scores - row_peak)
    row_total = jnp.sum(expd, axis=-1, keepdims=True)
    weights = (expd / row_total).astype(jnp.bfloat16)
    mixed = jnp.einsum("grtu,ugc->tgrc", weights, value_low, preferred_element_type=jnp.float32)
    return (mixed.reshape(seq_length, -1).astype(jnp.bfloat16), row_peak + jnp.log(row_total))


def attend_back(block_item):
    query_rot, key_rot, value_low, visible, log_sum, grad_mixed = block_item
    seq_length, kv_heads, head_size = key_rot.shape
    factor = head_size ** (-0.5)
    grouped = query_rot.reshape(seq_length, kv_heads, -1, head_size)
    grad_grouped = grad_mixed.reshape(seq_length, kv_heads, -1, head_size)
    scores = (
        jnp.einsum("tgrc,ugc->grtu", grouped, key_rot, preferred_element_type=jnp.float32) * factor
    )
    weights = jnp.where(visible[None, None], jnp.exp(scores - log_sum), 0.0)
    grad_weights = jnp.einsum(
        "tgrc,ugc->grtu", grad_grouped, value_low, preferred_element_type=jnp.float32
    )
    row_delta = jnp.sum(weights * grad_weights, axis=-1, keepdims=True)
    grad_scores = (weights * (grad_weights - row_delta)).astype(jnp.bfloat16)
    grad_query = (
        jnp.einsum(
            "grtu,ugc->tgrc", grad_scores, key_rot, preferred_element_type=jnp.float32
        ).reshape(seq_length, -1, head_size)
        * factor
    )
    grad_key = (
        jnp.einsum("grtu,tgrc->ugc", grad_scores, grouped, preferred_element_type=jnp.float32)
        * factor
    )
    grad_value = jnp.einsum(
        "grtu,tgrc->ugc",
        weights.astype(jnp.bfloat16),
        grad_grouped,
        preferred_element_type=jnp.float32,
    )
    return (grad_query, grad_key, grad_value)


def local(hidden, segments, cotangent, w_query, w_keyval, w_output, w_gate, w_up, w_down, gains):
    layer_count = w_query.shape[0]
    cos_table, sin_table = rope_tables(segments)
    index_row = jnp.arange(segments.shape[1], dtype=jnp.int32)
    visible = (index_row[None, :, None] >= index_row[None, None, :]) & (
        segments[:, :, None] == segments[:, None, :]
    )
    stream = hidden.astype(jnp.float32)
    layer_index = 0
    normed_a, inv_rms_a = norm_forward(stream)
    gathered_a = gather_tokens((normed_a * gains[layer_index, 0]).astype(jnp.bfloat16))
    query_rot, key_rot, value_low = project_attention(
        gathered_a, w_query[layer_index], w_keyval[layer_index], cos_table, sin_table
    )
    mixed_low, log_sum = lax.map(attend_one, (query_rot, key_rot, value_low, visible))
    branch = jnp.einsum(
        "stc,cd->std", mixed_low, w_output[layer_index], preferred_element_type=jnp.float32
    )
    middle = stream + sum_branch(branch)
    normed_b, inv_rms_b = norm_forward(middle)
    gathered_b = gather_tokens((normed_b * gains[layer_index, 1]).astype(jnp.bfloat16))
    gate_pre = jnp.einsum(
        "std,df->stf", gathered_b, w_gate[layer_index], preferred_element_type=jnp.float32
    )
    up_pre = jnp.einsum(
        "std,df->stf", gathered_b, w_up[layer_index], preferred_element_type=jnp.float32
    )
    hidden_act = (jax.nn.silu(gate_pre) * up_pre).astype(jnp.bfloat16)
    down_out = jnp.einsum(
        "stf,fd->std", hidden_act, w_down[layer_index], preferred_element_type=jnp.float32
    )
    saved = [
        (
            normed_a,
            inv_rms_a,
            gathered_a,
            query_rot,
            key_rot,
            value_low,
            mixed_low,
            log_sum,
            normed_b,
            inv_rms_b,
            gathered_b,
            gate_pre,
            up_pre,
            hidden_act,
        )
    ]
    stream = middle + sum_branch(down_out)
    result = stream.astype(jnp.bfloat16)
    grad_stream = cotangent.astype(jnp.float32)
    attn_parts = [None] * layer_count
    mlp_parts = [None] * layer_count
    gain_grads = [None] * layer_count
    for layer_index in reversed(range(layer_count)):
        (
            normed_a,
            inv_rms_a,
            gathered_a,
            query_rot,
            key_rot,
            value_low,
            mixed_low,
            log_sum,
            normed_b,
            inv_rms_b,
            gathered_b,
            gate_pre,
            up_pre,
            hidden_act,
        ) = saved[layer_index]
        grad_down_out = gather_grads(grad_stream.astype(jnp.bfloat16))
        grad_down_w = jnp.einsum(
            "stf,std->fd", hidden_act, grad_down_out, preferred_element_type=jnp.float32
        )
        grad_act = jnp.einsum(
            "std,fd->stf", grad_down_out, w_down[layer_index], preferred_element_type=jnp.float32
        )
        sigmoid_gate = jax.nn.sigmoid(gate_pre)
        grad_gate_low = (
            grad_act * up_pre * sigmoid_gate * (1.0 + gate_pre * (1.0 - sigmoid_gate))
        ).astype(jnp.bfloat16)
        grad_up_low = (grad_act * gate_pre * sigmoid_gate).astype(jnp.bfloat16)
        grad_gate_w = jnp.einsum(
            "std,stf->df", gathered_b, grad_gate_low, preferred_element_type=jnp.float32
        )
        grad_up_w = jnp.einsum(
            "std,stf->df", gathered_b, grad_up_low, preferred_element_type=jnp.float32
        )
        mlp_parts[layer_index] = (grad_gate_w[None], grad_up_w[None], grad_down_w[None])
        grad_input_b = sum_inputs(
            jnp.einsum(
                "stf,df->std",
                grad_gate_low,
                w_gate[layer_index],
                preferred_element_type=jnp.float32,
            )
            + jnp.einsum(
                "stf,df->std", grad_up_low, w_up[layer_index], preferred_element_type=jnp.float32
            )
        )
        grad_added, gain_grad_b = norm_backward(
            grad_input_b, normed_b, inv_rms_b, gains[layer_index, 1]
        )
        grad_stream = grad_stream + grad_added
        grad_branch = gather_grads(grad_stream.astype(jnp.bfloat16))
        grad_output_w = jnp.einsum(
            "stc,std->cd", mixed_low, grad_branch, preferred_element_type=jnp.float32
        )
        grad_mixed = jnp.einsum(
            "std,cd->stc", grad_branch, w_output[layer_index], preferred_element_type=jnp.float32
        ).astype(jnp.bfloat16)
        kept_inputs = (gathered_a, query_rot, key_rot, value_low)
        gathered_use, query_use, key_use, value_use = kept_inputs
        grad_qrot, grad_krot, grad_value = lax.map(
            attend_back, (query_use, key_use, value_use, visible, log_sum, grad_mixed)
        )
        seq_count, seq_length = (grad_qrot.shape[0], grad_qrot.shape[1])
        grad_q_low = (
            unrotate(grad_qrot, cos_table, sin_table)
            .reshape(seq_count, seq_length, -1)
            .astype(jnp.bfloat16)
        )
        grad_kv_low = jnp.concatenate(
            [unrotate(grad_krot, cos_table, sin_table), grad_value], axis=-1
        ).astype(jnp.bfloat16)
        grad_query_w = jnp.einsum(
            "std,stc->dc", gathered_use, grad_q_low, preferred_element_type=jnp.float32
        )
        grad_keyval_w = jnp.einsum(
            "std,stgc->dgc", gathered_use, grad_kv_low, preferred_element_type=jnp.float32
        )
        grad_input_a = sum_inputs(
            jnp.einsum(
                "stc,dc->std", grad_q_low, w_query[layer_index], preferred_element_type=jnp.float32
            )
            + jnp.einsum(
                "stgc,dgc->std",
                grad_kv_low,
                w_keyval[layer_index],
                preferred_element_type=jnp.float32,
            )
        )
        grad_added, gain_grad_a = norm_backward(
            grad_input_a, normed_a, inv_rms_a, gains[layer_index, 0]
        )
        grad_stream = grad_stream + grad_added
        gain_grads[layer_index] = jnp.stack([gain_grad_a, gain_grad_b])
        attn_parts[layer_index] = (grad_query_w[None], grad_keyval_w[None], grad_output_w[None])
    attn_merged = tuple((attn_parts[0][member] for member in range(3)))
    mlp_merged = tuple((mlp_parts[0][member] for member in range(3)))
    merged = reduce_weights(
        attn_merged[0], attn_merged[1], attn_merged[2], mlp_merged[0], mlp_merged[1], mlp_merged[2]
    )
    gain_total = lax.psum(jnp.stack(gain_grads), ("dp", "tp"))
    grad_hidden = grad_stream.astype(jnp.bfloat16)
    return (
        result,
        grad_hidden,
        merged[0],
        merged[1],
        merged[2],
        merged[3],
        merged[4],
        merged[5],
        gain_total,
    )


def solution(mesh):
    placed = (
        P("dp", "tp", None),
        P("dp", None),
        P("dp", "tp", None),
        P(None, None, "tp"),
        P(None, None, "tp", None),
        P(None, "tp", None),
        P(None, None, "tp"),
        P(None, None, "tp"),
        P(None, "tp", None),
        P(),
    )
    return jax.shard_map(
        local,
        mesh=mesh,
        in_specs=placed,
        out_specs=(
            P("dp", "tp", None),
            P("dp", "tp", None),
            P(None, None, "tp"),
            P(None, None, "tp", None),
            P(None, "tp", None),
            P(None, None, "tp"),
            P(None, None, "tp"),
            P(None, "tp", None),
            P(),
        ),
        check_vma=False,
    )
```

```python
import functools
import jax
import jax.numpy as jnp
from jax import lax
from jax.experimental import pallas as pl
from jax.experimental.pallas import tpu as pltpu
from jax.sharding import PartitionSpec as P

MESH = pl.DeviceIdType.MESH
HD = 96
HALF = HD // 2
EPS = 1e-05
ROPE_BASE = 100000.0
SCALE = HD ** (-0.5)
BF = jnp.bfloat16
F32 = jnp.float32
QB = 256


def flip(index, mask):
    out = index
    bit = 1
    while bit <= mask:
        if mask & bit:
            out = out + bit - 2 * bit * ((index // bit) % 2)
        bit *= 2
    return out


def nn(x, y):
    return lax.dot_general(x, y, (((1,), (0,)), ((), ())), preferred_element_type=F32)


def nt(x, y):
    return lax.dot_general(x, y, (((1,), (1,)), ((), ())), preferred_element_type=F32)


def normed(stream):
    inv = lax.rsqrt(jnp.mean(stream * stream, axis=-1, keepdims=True) + EPS)
    return stream * inv, inv


def rot_rows(x, cos, sin):
    x1, x2 = x[:HALF], x[HALF:]
    return jnp.concatenate([x1 * cos - x2 * sin, x2 * cos + x1 * sin], axis=0)


def forward_kernel(
    tp, dp,
    hid, cot, wqkv, wo, wg, wu, wd, gains, segc, segr, cos_t, sin_t,
    a_out, b_out, cot_all, q_out, kt_out, k_out, v_out, lse_out, mix_out, f1_out, f2_out, act_out, down_out, mid_out,
    hid_all, mixed_all, wo_all, w_in, w_st, wqkv_t, wg_t, wu_t, wd_n, wd_t,
    a_v, b_v, q_t, k_t, k_n, v_n, v_t, mix_t, bias, lse, f1, f2, act_t, down_v, mid_v,
    load_sem, out_sem, hid_ssem, hid_rsem, cot_ssem, cot_rsem, mix_ssem, mix_rsem, wo_ssem, wo_rsem,
):
    me, md = lax.axis_index("tp"), lax.axis_index("dp")
    nz = dp // 2
    core, mz = md % 2, md // 2
    block, width = hid.shape
    length = tp * block
    hidden = wg.shape[1]
    heads, kv_heads = q_t.shape[0], k_t.shape[0]
    qcols, kvcols = heads * HD, kv_heads * 2 * HD
    pieces = length // QB
    hops = tp == 4
    rows_o = qcols // dp
    spread = qcols % (16 * dp) == 0
    half = block // 2

    loads = [
        pltpu.make_async_copy(wqkv, w_in, load_sem.at[0]),
        pltpu.make_async_copy(wd, wd_n, load_sem.at[1]),
        pltpu.make_async_copy(hid, hid_all.at[me], load_sem.at[2]),
        pltpu.make_async_copy(wg, w_st, load_sem.at[3]),
        pltpu.make_async_copy(wo, wo_all.at[me], load_sem.at[4]),
        pltpu.make_async_copy(cot, cot_all.at[me], load_sem.at[5]),
    ]
    for c in loads:
        c.start()

    barrier = pltpu.get_barrier_semaphore()
    peers = [(md, flip(me, p)) for p in range(1, tp)]
    if spread:
        peers += [(flip(md, 2 * z), me) for z in range(1, nz)] + [(flip(md, 1), me)]
    for peer in peers:
        pl.semaphore_signal(barrier, inc=1, device_id=peer, device_id_type=MESH)
    pl.semaphore_wait(barrier, len(peers))

    def remote(src, dst, ssem, rsem, peer):
        return pltpu.make_async_remote_copy(src, dst, ssem, rsem, device_id=peer, device_id_type=MESH)

    def gather_first(src, dst, ssem, rsem):
        out = []
        for p in range(1, tp):
            if hops and p == 3:
                continue
            for part in (0, 1) if p == 1 else (1, 0):
                rows = pl.ds(part * half, half)
                out.append(remote(src.at[rows], dst.at[me, rows], ssem.at[p, part], rsem.at[p, part], (md, flip(me, p))))
        return out

    def arrived(dst, ssem, rsem, p, part):
        rows = pl.ds(part * half, half)
        slot = dst.at[flip(me, p), rows]
        return remote(slot, slot, ssem.at[p, part], rsem.at[p, part], (md, flip(me, p)))

    def handed(dst, ssem, rsem, part):
        rows = pl.ds(part * half, half)
        came, goes = (1, 2) if part == 0 else (2, 1)
        slot = dst.at[flip(me, came), rows]
        return remote(slot, slot, ssem.at[3, part], rsem.at[3, part], (md, flip(me, goes)))

    hid_first = gather_first(hid, hid_all, hid_ssem, hid_rsem)
    cot_first = gather_first(cot, cot_all, cot_ssem, cot_rsem)

    piece = pl.ds((core * nz + mz) * rows_o, rows_o) if spread else pl.ds(0, qcols)
    wo_tp = [
        remote(wo.at[piece], wo_all.at[me, piece], wo_ssem.at[0, p], wo_rsem.at[0, p], (md, flip(me, p)))
        for p in range(1, tp)
    ]
    for c in wo_tp:
        c.start()
    for c in hid_first:
        c.start()
    wo_z, wo_core = [], []
    if spread:
        for z in range(1, nz):
            for p in range(1, tp):
                slot = wo_all.at[flip(me, p), piece]
                wo_z.append(remote(slot, slot, wo_ssem.at[z, p], wo_rsem.at[z, p], (flip(md, 2 * z), me)))
        both = pl.ds(core * nz * rows_o, nz * rows_o)
        for p in range(1, tp):
            slot = wo_all.at[flip(me, p), both]
            wo_core.append(remote(slot, slot, wo_ssem.at[nz, p], wo_rsem.at[nz, p], (flip(md, 1), me)))

    def turn(dst, src, step=256):
        rows = src.shape[0]
        for r in range(0, rows, step):
            dst[:, pl.ds(r, step)] = src[pl.ds(r, step), :].T

    def project(src):
        off = pl.multiple_of(src * block, block)
        cols = pl.ds(off, block)
        base, _ = normed(hid_all[src].astype(F32))
        a = (base * gains[0:1, :]).astype(BF)
        a_v[cols, :] = a
        cos, sin = cos_t[:, cols], sin_t[:, cols]
        qk = nt(wqkv_t[...], a)
        for h in range(heads):
            q_t[h, :, cols] = rot_rows(qk[h * HD : (h + 1) * HD], cos, sin).astype(BF)
        pad = jnp.zeros((128 - HD, block), F32)
        for g in range(kv_heads):
            at = qcols + g * 2 * HD
            kr = rot_rows(qk[at : at + HD], cos, sin)
            vr = qk[at + HD : at + 2 * HD]
            k_t[g, :, cols] = kr.astype(BF)
            v_t[g, :, cols] = vr.astype(BF)
            k_n[g, cols, :] = jnp.concatenate([kr, pad], axis=0).T.astype(BF)
            v_n[g, cols, :] = jnp.concatenate([vr, pad], axis=0).T.astype(BF)

    loads[0].wait()
    turn(wqkv_t, w_in)
    loads[2].wait()
    project(me)
    for c in wo_tp:
        c.wait()
    for c in wo_z:
        c.start()
    loads[3].wait()
    turn(wg_t, w_st)
    wu_load = pltpu.make_async_copy(wu, w_st, load_sem.at[3])
    wu_load.start()
    wu_load.wait()
    turn(wu_t, w_st)
    loads[1].wait()
    turn(wd_t, wd_n)
    loads[4].wait()
    loads[5].wait()

    if hops:
        for p, part in ((1, 0), (2, 1)):
            arrived(hid_all, hid_ssem, hid_rsem, p, part).wait_recv()
            handed(hid_all, hid_ssem, hid_rsem, part).start()
        for p, part in ((1, 1), (2, 0)):
            arrived(hid_all, hid_ssem, hid_rsem, p, part).wait_recv()
            project(flip(me, p))
        for part in (0, 1):
            rows = pl.ds(part * half, half)
            slot = hid_all.at[flip(me, 3), rows]
            remote(slot, slot, hid_ssem.at[3, part], hid_rsem.at[3, part], (md, flip(me, 2))).wait_recv()
        project(flip(me, 3))
    else:
        for p in range(1, tp):
            for part in (0, 1):
                arrived(hid_all, hid_ssem, hid_rsem, p, part).wait_recv()
            project(flip(me, p))

    outs = []

    def put(src, dst):
        c = pltpu.make_async_copy(src, dst, out_sem.at[len(outs)])
        c.start()
        outs.append(c)

    for src, dst in ((a_v, a_out), (q_t, q_out), (k_t, kt_out), (k_n, k_out), (v_n, v_out)):
        put(src, dst)

    def mix_slot(who, i):
        return mixed_all.at[who, pl.ds(i * QB, QB)]

    def mix_copy(i, p):
        return remote(mix_slot(me, i), mix_slot(me, i), mix_ssem.at[p, i], mix_rsem.at[p, i], (md, flip(me, p)))

    def mix_arrived(i, p):
        slot = mix_slot(flip(me, p), i)
        return remote(slot, slot, mix_ssem.at[p, i], mix_rsem.at[p, i], (md, flip(me, p)))

    def mix_handed(i):
        came, goes = (1, 2) if i % 2 == 0 else (2, 1)
        slot = mix_slot(flip(me, came), i)
        return remote(slot, slot, mix_ssem.at[3, i], mix_rsem.at[3, i], (md, flip(me, goes)))

    def hand_on(i):
        if not hops:
            return
        mix_arrived(i, 1 if i % 2 == 0 else 2).wait_recv()
        mix_handed(i).start()

    for i in range(pieces):
        reach = (i + 1) * QB
        cols = pl.ds(i * QB, QB)
        same = segc[pl.ds(0, reach), :] == segr[:, cols]
        later = lax.broadcasted_iota(jnp.int32, (reach, QB), 0) <= lax.broadcasted_iota(jnp.int32, (reach, QB), 1) + i * QB
        bias[pl.ds(0, reach), :] = jnp.where(same & later, 0.0, -1e30)

        def head(h, _, reach=reach, cols=cols):
            g = h // (heads // kv_heads)
            s = nn(k_n[g, pl.ds(0, reach), :][:, :HD], q_t[h, :, cols]) * SCALE + bias[pl.ds(0, reach), :]
            top = jnp.max(s, axis=0, keepdims=True)
            e = jnp.exp(s - top)
            total = jnp.sum(e, axis=0, keepdims=True)
            p = (e * (1.0 / total)).astype(BF)
            mix_t[h, :, cols] = nn(v_t[g, :, pl.ds(0, reach)], p).astype(BF)
            lse[h, :, cols] = top + jnp.log(total)
            return 0

        lax.fori_loop(0, heads, head, 0)
        mixed_all[me, cols, :] = mix_t[:, :, cols].reshape(qcols, QB).T
        for p in range(1, tp):
            if not (hops and p == 3):
                mix_copy(i, p).start()
        if i:
            hand_on(i - 1)
    put(lse, lse_out)
    put(mix_t, mix_out)
    hand_on(pieces - 1)

    for c in wo_z:
        c.wait()
    for c in wo_core:
        c.start()
    for i in range(pieces):
        for p in range(1, tp):
            if not (hops and p == 3):
                mix_copy(i, p).wait_send()
    for c in cot_first:
        c.start()
    for c in wo_core:
        c.wait()

    def middle(i):
        rows = pl.ds(i * QB, QB)
        for p in range(1, tp):
            if hops and p == 3:
                slot = mix_slot(flip(me, 3), i)
                remote(slot, slot, mix_ssem.at[3, i], mix_rsem.at[3, i], (md, flip(me, 1))).wait_recv()
            elif not (hops and p == (1 if i % 2 == 0 else 2)):
                mix_arrived(i, p).wait_recv()
        per = QB // block if QB >= block else 1
        stream = jnp.concatenate([hid_all[i * per + n] for n in range(per)], axis=0).astype(F32)
        total = stream
        for s in range(tp):
            total = total + nn(mixed_all[s, rows, :], wo_all[s])
        base, _ = normed(total)
        b_v[rows, :] = (base * gains[1:2, :]).astype(BF)
        for n in range(per):
            @pl.when(me == i * per + n)
            def _(n=n):
                mid_v[...] = total[n * block : (n + 1) * block]

    def feed(i):
        rows = pl.ds(i * QB, QB)
        b = b_v[rows, :]
        step = 256
        for f in range(0, hidden, step):
            units = pl.ds(f, step)
            gate = nt(wg_t[units, :], b)
            up = nt(wu_t[units, :], b)
            sig = jax.nn.sigmoid(gate)
            silu = gate * sig
            f1[units, rows] = (up * sig * (1.0 + gate * (1.0 - sig))).astype(BF)
            f2[units, rows] = silu.astype(BF)
            act_t[units, rows] = (silu * up).astype(BF)
        for d in range(0, width, 512):
            down_v[pl.ds(d, 512), rows] = nn(wd_t[pl.ds(d, 512), :], act_t[:, rows]).astype(BF)

    for i in range(pieces):
        middle(i)
    for i in range(pieces):
        feed(i)
    for src, dst in ((b_v, b_out), (mid_v, mid_out), (f1, f1_out), (f2, f2_out), (act_t, act_out), (down_v, down_out)):
        put(src, dst)

    if hops:
        for p, part in ((1, 0), (2, 1)):
            arrived(cot_all, cot_ssem, cot_rsem, p, part).wait_recv()
            handed(cot_all, cot_ssem, cot_rsem, part).start()
        for p, part in ((1, 1), (2, 0)):
            arrived(cot_all, cot_ssem, cot_rsem, p, part).wait_recv()
        for part in (0, 1):
            rows = pl.ds(part * half, half)
            slot = cot_all.at[flip(me, 3), rows]
            remote(slot, slot, cot_ssem.at[3, part], cot_rsem.at[3, part], (md, flip(me, 2))).wait_recv()
    else:
        for p in range(1, tp):
            for part in (0, 1):
                arrived(cot_all, cot_ssem, cot_rsem, p, part).wait_recv()
    for c in hid_first + cot_first:
        c.wait_send()
    if hops:
        for part in (0, 1):
            handed(hid_all, hid_ssem, hid_rsem, part).wait_send()
            handed(cot_all, cot_ssem, cot_rsem, part).wait_send()
        for i in range(pieces):
            mix_handed(i).wait_send()
    for c in outs:
        c.wait()


def forward(mesh, hid, cot, wqkv, wo, wg, wu, wd, gains, segc, segr, cos_t, sin_t):
    tp, dp = mesh.shape["tp"], mesh.shape["dp"]
    block, width = hid.shape
    length = tp * block
    hidden = wg.shape[1]
    heads = wo.shape[0] // HD
    kv_heads = (wqkv.shape[1] - heads * HD) // (2 * HD)
    nz = dp // 2
    pieces = length // QB
    sds = jax.ShapeDtypeStruct
    outs = [
        sds((length, width), BF),
        sds((length, width), BF),
        sds((tp, block, width), BF),
        sds((heads, HD, length), BF),
        sds((kv_heads, HD, length), BF),
        sds((kv_heads, length, 128), BF),
        sds((kv_heads, length, 128), BF),
        sds((heads, 1, length), F32),
        sds((heads, HD, length), BF),
        sds((hidden, length), BF),
        sds((hidden, length), BF),
        sds((hidden, length), BF),
        sds((width, length), BF),
        sds((block, width), F32),
    ]
    dma = pltpu.SemaphoreType.DMA
    scratch = [
        pltpu.VMEM((tp, block, width), BF),
        pltpu.VMEM((tp, length, heads * HD), BF),
        pltpu.VMEM((tp, heads * HD, width), BF),
        pltpu.VMEM((width, heads * HD + kv_heads * 2 * HD), BF),
        pltpu.VMEM((width, hidden), BF),
        pltpu.VMEM((heads * HD + kv_heads * 2 * HD, width), BF),
        pltpu.VMEM((hidden, width), BF),
        pltpu.VMEM((hidden, width), BF),
        pltpu.VMEM((hidden, width), BF),
        pltpu.VMEM((width, hidden), BF),
        pltpu.VMEM((length, width), BF),
        pltpu.VMEM((length, width), BF),
        pltpu.VMEM((heads, HD, length), BF),
        pltpu.VMEM((kv_heads, HD, length), BF),
        pltpu.VMEM((kv_heads, length, 128), BF),
        pltpu.VMEM((kv_heads, length, 128), BF),
        pltpu.VMEM((kv_heads, HD, length), BF),
        pltpu.VMEM((heads, HD, length), BF),
        pltpu.VMEM((length, QB), F32),
        pltpu.VMEM((heads, 1, length), F32),
        pltpu.VMEM((hidden, length), BF),
        pltpu.VMEM((hidden, length), BF),
        pltpu.VMEM((hidden, length), BF),
        pltpu.VMEM((width, length), BF),
        pltpu.VMEM((block, width), F32),
        dma((6,)),
        dma((13,)),
        dma((tp, 2)),
        dma((tp, 2)),
        dma((tp, 2)),
        dma((tp, 2)),
        dma((tp, pieces)),
        dma((tp, pieces)),
        dma((nz + 1, tp)),
        dma((nz + 1, tp)),
    ]
    any_ = pl.BlockSpec(memory_space=pl.ANY)
    vmem = pl.BlockSpec(memory_space=pltpu.VMEM)
    return pl.pallas_call(
        functools.partial(forward_kernel, tp, dp),
        out_shape=outs,
        in_specs=[any_] * 7 + [vmem] * 5,
        out_specs=[any_] * len(outs),
        scratch_shapes=scratch,
        compiler_params=pltpu.CompilerParams(collective_id=0, has_side_effects=True, vmem_limit_bytes=62 * 2**20),
        name="forward",
    )(hid, cot, wqkv, wo, wg, wu, wd, gains, segc, segr, cos_t, sin_t)


RING = 8
PAIR = 16


def unrot_rows(d, cos, sin):
    d1, d2 = d[:HALF], d[HALF:]
    return jnp.concatenate([d1 * cos + d2 * sin, d2 * cos - d1 * sin], axis=0)


def norm_back(grad, base, inv, gain):
    e = grad * gain
    back = inv * (e - base * jnp.mean(e * base, axis=-1, keepdims=True))
    return back, jnp.sum(grad * base, axis=0, keepdims=True)


def backward_kernel(
    tp, dp,
    cot_all, a_in, b_in, q_in, kt_in, k_in, v_in, lse_in, mix_in, f1_in, f2_in, act_in, down_in, mid_in, hid_in,
    wqkv, wo, wg, wu, wd, gains, segc, segr, cos_t, sin_t,
    res_out, hid_out, sums_out, gain_out,
    tok, act, wd_v, f1, f2, wg_v, wu_v, ab, snd, rcv, acc, pair, up_ring, dn_ring,
    q_t, k_t, k_n, v_n, lse, mix, gm_t, gqkv, dk, dv, bias, mid, hid, gs, own, gb, wo_v, stage, gsum, gland,
    load_sem, out_sem, pair_ssem, pair_rsem, part_ssem, up_rsem, dn_rsem, tot_ssem, sib_ssem, sib_rsem, fin_sem,
    rs_ssem, rs_rsem, gb_ssem, gb_rsem, gain_ssem, gain_rsem, cr_pair, cr_dn, cr_up, cr_rs,
):
    me, md = lax.axis_index("tp"), lax.axis_index("dp")
    nz = dp // 2
    core, mz = md % 2, md // 2
    length, width = tok.shape
    block = length // tp
    half = block // 2
    hidden = act.shape[0]
    heads, kv_heads = q_t.shape[0], k_t.shape[0]
    group = heads // kv_heads
    qcols, kvcols = heads * HD, kv_heads * 2 * HD
    hops = tp == 4
    r = hidden // PAIR
    parts = [hidden, hidden, hidden, qcols, qcols, kvcols]
    first = [sum(p // 2 for p in parts[:n]) // r for n in range(6)]
    chunks = sum(parts) // 2 // r
    own_rows = pl.ds(pl.multiple_of(me * block, block), block)

    def load(n, src, dst):
        return pltpu.make_async_copy(src, dst, load_sem.at[n])

    early = [load(0, act_in, act)] + [load(1 + s, cot_all.at[s], tok.at[pl.ds(s * block, block)]) for s in range(tp)]
    n0 = 1 + tp
    then = [load(n0, wd.at[pl.ds(hidden // 2, hidden // 2)], wd_v.at[pl.ds(hidden // 2, hidden // 2)]), load(n0 + 1, f1_in, f1), load(n0 + 2, f2_in, f2)]
    late = [
        load(n0 + 3 + n, s, d)
        for n, (s, d) in enumerate(
            (
                (wg, wg_v), (wu, wu_v), (b_in, ab), (q_in, q_t), (kt_in, k_t), (k_in, k_n), (v_in, v_n), (lse_in, lse),
                (mix_in, mix), (mid_in, mid), (hid_in, hid), (wo, wo_v),
            )
        )
    ]
    n1 = n0 + 3 + len(late)
    for c in early:
        c.start()

    barrier = pltpu.get_barrier_semaphore()
    peers = [(md, flip(me, p)) for p in range(1, tp)] + [(flip(md, p), me) for p in range(1, dp)]
    for peer in peers:
        pl.semaphore_signal(barrier, inc=1, device_id=peer, device_id_type=MESH)
    pl.semaphore_wait(barrier, len(peers))

    def remote(src, dst, ssem, rsem, peer):
        return pltpu.make_async_remote_copy(src, dst, ssem, rsem, device_id=peer, device_id_type=MESH)

    def signal(sem, peer):
        pl.semaphore_signal(sem, inc=1, device_id=peer, device_id_type=MESH)

    left = mz < nz // 2
    step_in = jnp.where(left, 1, -1)
    is_mid = (mz == nz // 2 - 1) | (mz == nz // 2)
    has_up = (mz != 0) & (mz != nz - 1)
    not_mid, no_up = jnp.logical_not(is_mid), jnp.logical_not(has_up)
    sibling = (md + 1 - 2 * core, me)
    down_dev = (md + 2 * step_in, me)
    up_dev = (md - 2 * step_in, me)

    def rows_of(c):
        return pl.ds(c * r, r)

    def pair_copy(c):
        slot = pl.ds((c % PAIR) * r, r)
        return remote(wd_v.at[slot], pair.at[slot], pair_ssem.at[c], pair_rsem.at[c], sibling)

    def part_copy(c, dst, rsem):
        return remote(acc.at[rows_of(c)], dst.at[c % RING], part_ssem.at[c], rsem.at[c], down_dev)

    def total_copy(c):
        return remote(dn_ring.at[c % RING], dn_ring.at[c % RING], tot_ssem.at[c], dn_rsem.at[c], up_dev)

    def sib_copy(c):
        return remote(dn_ring.at[c % RING], sums_out.at[core, rows_of(c)], sib_ssem.at[c], sib_rsem.at[c], sibling)

    def fin_copy(c):
        return pltpu.make_async_copy(dn_ring.at[c % RING], sums_out.at[core, rows_of(c)], fin_sem.at[c])

    def gather_part(c):
        pair_copy(c).wait_recv()
        total = acc[rows_of(c), :].astype(F32) + pair[pl.ds((c % PAIR) * r, r), :].astype(F32)
        acc[rows_of(c), :] = total.astype(BF)

        @pl.when(has_up)
        def _():
            remote(up_ring.at[c % RING], up_ring.at[c % RING], part_ssem.at[c], up_rsem.at[c], up_dev).wait_recv()
            acc[rows_of(c), :] = (acc[rows_of(c), :].astype(F32) + up_ring[c % RING].astype(F32)).astype(BF)
            if c + RING < chunks:
                signal(cr_dn, up_dev)

        if c + PAIR < chunks:
            signal(cr_pair, sibling)
        if c >= RING:
            pl.semaphore_wait(cr_dn, 1)

        @pl.when(is_mid)
        def _():
            part_copy(c, dn_ring, dn_rsem).start()

        @pl.when(not_mid)
        def _():
            part_copy(c, up_ring, up_rsem).start()

    def spread_total(c):
        remote(dn_ring.at[c % RING], dn_ring.at[c % RING], tot_ssem.at[c], dn_rsem.at[c], down_dev).wait_recv()

        @pl.when(is_mid)
        def _():
            dn_ring[c % RING] = (acc[rows_of(c), :].astype(F32) + dn_ring[c % RING].astype(F32)).astype(BF)

        @pl.when(has_up)
        def _():
            if c >= RING:
                pl.semaphore_wait(cr_up, 1)
            total_copy(c).start()

        sib_copy(c).start()
        fin_copy(c).start()

    def retire(c):
        @pl.when(has_up)
        def _():
            total_copy(c).wait_send()

        sib_copy(c).wait_send()
        fin_copy(c).wait()
        if c + RING < chunks:

            @pl.when(is_mid)
            def _():
                signal(cr_dn, down_dev)

            @pl.when(not_mid)
            def _():
                signal(cr_up, down_dev)

    slot_now = [0]
    lag = 2

    def when_chunk(cond, fn, c):
        if 0 <= c < chunks:

            @pl.when(cond)
            def _():
                fn(c)

    def z(count=1):
        for _ in range(count):
            k = slot_now[0]
            slot_now[0] += 1
            when_chunk(no_up, gather_part, k)
            when_chunk(has_up, gather_part, k - lag)
            when_chunk(is_mid, retire, k - 2 * lag - 2)
            when_chunk(not_mid, retire, k - 3 * lag - 2)
            when_chunk(is_mid, spread_total, k - 2 * lag)
            when_chunk(not_mid, spread_total, k - 3 * lag)

    sent = set()

    def pair_done(c):
        if c not in sent:
            sent.add(c)
            pair_copy(c).wait_send()

    def weight_grad(n, lhs, rhs, mine, piece=None):
        hr = parts[n] // 2
        pr = min(256, hr)
        which = core if mine else 1 - core
        for p in range(hr // pr) if piece is None else (piece,):
            value = nn(lhs[pl.ds(pl.multiple_of(which * hr + p * pr, 16), pr), :], rhs[...]).astype(BF)
            at = first[n] + p * pr // r
            if mine:
                acc[pl.ds(at * r, pr), :] = value
                continue
            for c in range(pr // r):
                if at + c >= PAIR:
                    pair_done(at + c - PAIR)
                    pl.semaphore_wait(cr_pair, 1)
                wd_v[pl.ds(((at + c) % PAIR) * r, r), :] = value[c * r : (c + 1) * r]
                pair_copy(at + c).start()

    first_half, second_half = pl.ds(0, width // 2), pl.ds(width // 2, width // 2)
    halves = (first_half, second_half)

    def rs_copy(u, slot, part, p, ahead=False):
        return remote(
            snd.at[slot, halves[part]], rcv.at[slot, halves[part]], rs_ssem.at[u, slot, part], rs_rsem.at[u, slot, part], (md, flip(me, p))
        )

    def rs_send(u, p):
        if hops and p == 3:
            rs_copy(u, 2, 0, 1).start()
            rs_copy(u, 2, 1, 2).start()
        elif hops:
            rs_copy(u, p - 1, p - 1, p).start()
        else:
            for part in (0, 1):
                rs_copy(u, p - 1, part, p).start()

    def rs_merge(u, p):
        if not hops:
            return
        part = 2 - p
        rs_copy(u, 2, part, 3 - p).wait_recv()
        h = halves[part]
        snd[p - 1, h, :] = (snd[p - 1, h, :].astype(F32) + rcv[2, h, :].astype(F32)).astype(BF)
        rs_copy(u, p - 1, part, p).start()

    def rs_finish(u):
        for p in range(1, tp):
            if hops and p == 3:
                continue
            for part in (0, 1):
                rs_copy(u, p - 1, part, p).wait_recv()
        for p in range(1, tp):
            for part in (0, 1):
                rs_copy(u, p - 1, part, (1 if part == 0 else 2) if hops and p == 3 else p).wait_send()
        total = own[...]
        for p in range(1, tp):
            if not (hops and p == 3):
                total = total + rcv[p - 1].astype(F32)
        return total.T

    order = range(tp - 1, 0, -1) if not hops else (3, 1, 2)

    def gib_into(put, p):
        cols = pl.ds(pl.multiple_of(flip(me, p) * block, block), block)
        for d in range(0, width, 512):
            rows = pl.ds(d, 512)
            put(rows, nn(wg_v[rows, :], f1[:, cols]) + nn(wu_v[rows, :], f2[:, cols]))

    def gia_into(put, p):
        cols = pl.ds(pl.multiple_of(flip(me, p) * block, block), block)
        for d in range(0, width, 512):
            rows = pl.ds(d, 512)
            put(rows, nn(wg_v[rows, 0 : qcols + kvcols], gqkv[:, cols]))

    def to_snd(p):
        def put(rows, value):
            snd[p - 1, rows, :] = value.astype(BF)

        return put

    def to_own(rows, value):
        own[rows, :] = value

    for c in early:
        c.wait()
    for c in then:
        c.start()
    gsum[...] = jnp.zeros_like(gsum)
    mid_rows = hidden // 2
    down_pieces = max(1, mid_rows // 256)

    def gate_grads(start):
        step = min(512, mid_rows)
        for i in range(length // QB):
            cols = pl.ds(i * QB, QB)
            for f in range(start, start + mid_rows, step):
                units = pl.ds(f, step)
                grad_act = nt(wd_v[units, :], tok[cols, :])
                f1[units, cols] = (grad_act * f1[units, cols].astype(F32)).astype(BF)
                f2[units, cols] = (grad_act * f2[units, cols].astype(F32)).astype(BF)

    weight_grad(0, act, tok, False, 0)
    weight_grad(0, act, tok, True, 0)
    z()
    for p in range(1, down_pieces):
        weight_grad(0, act, tok, False, p)
        weight_grad(0, act, tok, True, p)
    for c in then:
        c.wait()
    for c in late:
        c.start()
    gate_grads(mid_rows)
    z()
    for c in range(PAIR // 2):
        pair_done(c)
    rest = load(n1 + 3 + tp, wd.at[pl.ds(0, mid_rows)], wd_v.at[pl.ds(0, mid_rows)])
    rest.start()
    rest.wait()
    gate_grads(0)
    z()
    for c in late[:2]:
        c.wait()
    for n, p in enumerate(order):
        gib_into(to_snd(p), p)
        rs_send(0, p)
        if n == 1:
            z()
    z()
    late[2].wait()
    weight_grad(1, f1, ab, False)
    z()
    weight_grad(1, f1, ab, True)
    z()
    if hops:
        rs_merge(0, 1)
        rs_merge(0, 2)
    gib_into(to_own, 0)
    z(3)
    for c in late[3:]:
        c.wait()
    qkv_load = load(n1, wqkv, wg_v.at[:, pl.ds(0, qcols + kvcols)])
    qkv_load.start()

    grad_in = rs_finish(0)
    base_b, inv_b = normed(mid[...])
    back, gain_b = norm_back(grad_in, base_b, inv_b, gains[1:2, :])
    gs[...] = tok[own_rows, :].astype(F32) + back
    gsum[1:2, :] = gain_b
    gb[...] = gs[...].astype(BF)
    tok[own_rows, :] = gb[...]

    def gb_rows(p, part):
        return tok.at[pl.ds(pl.multiple_of(flip(me, p) * block + part * half, half), half)]

    def gb_copy(p, part):
        return remote(gb.at[pl.ds(part * half, half)], gb_rows(0, part), gb_ssem.at[p, part], gb_rsem.at[p, part], (md, flip(me, p)))

    def gb_arrived(p, part):
        return remote(gb_rows(p, part), gb_rows(p, part), gb_ssem.at[p, part], gb_rsem.at[p, part], (md, flip(me, p)))

    def gb_handed(part):
        came, goes = (1, 2) if part == 0 else (2, 1)
        return remote(gb_rows(came, part), gb_rows(came, part), gb_ssem.at[3, part], gb_rsem.at[3, part], (md, flip(me, goes)))

    direct = [p for p in range(1, tp) if not (hops and p == 3)]
    for p in direct:
        for part in (0, 1) if p == 1 else (1, 0):
            gb_copy(p, part).start()
    z()
    weight_grad(2, f2, ab, False)
    z()
    weight_grad(2, f2, ab, True)
    z(2)
    a_load = load(n1 + 2, a_in, ab)
    a_load.start()
    if hops:
        for part in (0, 1):
            gb_arrived(1 if part == 0 else 2, part).wait_recv()
            gb_handed(part).start()
        for part in (0, 1):
            gb_arrived(2 if part == 0 else 1, part).wait_recv()
    z(2)
    for p in range(1, tp):
        if hops and p != 3:
            continue
        for part in (0, 1):
            gb_arrived(p, part).wait_recv()
    for p in direct:
        for part in (0, 1):
            gb_copy(p, part).wait_send()
    if hops:
        for part in (0, 1):
            gb_handed(part).wait_send()

    weight_grad(3, mix, tok, False)
    weight_grad(3, mix, tok, True)
    down_loads = []
    for n, p in enumerate((*order, 0)):
        cols = pl.ds(pl.multiple_of(flip(me, p) * block, block), block)
        down_loads.append(load(n1 + 3 + n, down_in.at[:, cols], snd.at[p - 1] if p else stage))
    for c in down_loads:
        c.start()
    for n in range(0, length, QB):
        cols = pl.ds(n, QB)
        gm_t[:, :, cols] = nt(wo_v[...], tok[cols, :]).astype(BF).reshape(heads, HD, QB)
    for c in down_loads:
        c.wait()
    for p in order:
        rs_send(1, p)
    own[...] = stage[...].astype(F32)
    z()

    dk[...] = jnp.zeros_like(dk)
    dv[...] = jnp.zeros_like(dv)
    for i in range(length // QB - 1, -1, -1):
        reach = (i + 1) * QB
        cols = pl.ds(i * QB, QB)
        same = segc[pl.ds(0, reach), :] == segr[:, cols]
        later = lax.broadcasted_iota(jnp.int32, (reach, QB), 0) <= lax.broadcasted_iota(jnp.int32, (reach, QB), 1) + i * QB
        bias[pl.ds(0, reach), :] = jnp.where(same & later, 0.0, -1e30)

        def head(h, _, reach=reach, cols=cols):
            g = h // group
            s = nn(k_n[g, pl.ds(0, reach), :][:, :HD], q_t[h, :, cols]) * SCALE + bias[pl.ds(0, reach), :]
            p = jnp.exp(s - lse[h, :, cols])
            grad_p = nn(v_n[g, pl.ds(0, reach), :][:, :HD], gm_t[h, :, cols])
            delta = jnp.sum(p * grad_p, axis=0, keepdims=True)
            ds = (p * (grad_p - delta)).astype(BF)
            dq = nn(k_t[g, :, pl.ds(0, reach)], ds) * SCALE
            gqkv[pl.ds(pl.multiple_of(h * HD, 16), HD), cols] = unrot_rows(dq, cos_t[:, cols], sin_t[:, cols]).astype(BF)
            dk[g, :, pl.ds(0, reach)] += nt(q_t[h, :, cols], ds)
            dv[g, :, pl.ds(0, reach)] += nt(gm_t[h, :, cols], p.astype(BF))
            return 0

        lax.fori_loop(0, heads, head, 0)
        z()
        if i == length // QB - 2 and hops:
            rs_merge(1, 1)
            rs_merge(1, 2)
    for g in range(kv_heads):
        at = qcols + g * 2 * HD
        gqkv[pl.ds(at, HD), :] = unrot_rows(dk[g] * SCALE, cos_t[...], sin_t[...]).astype(BF)
        gqkv[pl.ds(at + HD, HD), :] = dv[g].astype(BF)
    a_load.wait()
    weight_grad(4, gqkv.at[pl.ds(0, qcols)], ab, False)
    weight_grad(4, gqkv.at[pl.ds(0, qcols)], ab, True)
    weight_grad(5, gqkv.at[pl.ds(qcols, kvcols)], ab, False)
    weight_grad(5, gqkv.at[pl.ds(qcols, kvcols)], ab, True)
    z()
    stage_res = rs_finish(1)
    gb[...] = (mid[...] + stage_res).astype(BF)
    res_copy = pltpu.make_async_copy(gb, res_out, out_sem.at[0])
    res_copy.start()
    for p in range(1, tp):
        signal(cr_rs, (md, flip(me, p)))
    pl.semaphore_wait(cr_rs, tp - 1)
    z()
    qkv_load.wait()
    for p in order:
        gia_into(to_snd(p), p)
        rs_send(2, p)
    gia_into(to_own, 0)
    z(2)
    if hops:
        rs_merge(2, 1)
        rs_merge(2, 2)
    z(3)
    grad_in = rs_finish(2)
    base_a, inv_a = normed(hid[...].astype(F32))
    back, gain_a = norm_back(grad_in, base_a, inv_a, gains[0:1, :])
    hid[...] = (gs[...] + back).astype(BF)
    hid_copy = pltpu.make_async_copy(hid, hid_out, out_sem.at[1])
    hid_copy.start()
    gsum[0:1, :] = gain_a

    stages = []
    bit = 1
    while bit < dp:
        stages.append((flip(md, bit), me))
        bit *= 2
    bit = 1
    while bit < tp:
        stages.append((md, flip(me, bit)))
        bit *= 2
    for n, peer in enumerate(stages):
        c = remote(gsum, gland.at[n], gain_ssem.at[n], gain_rsem.at[n], peer)
        c.start()
        z()
        c.wait()
        gsum[...] = gsum[...] + gland[n]
    gain_copy = pltpu.make_async_copy(gsum.at[pl.ds(0, 8)], gain_out, out_sem.at[2])
    gain_copy.start()

    last = chunks + 3 * lag + 2
    z(last - slot_now[0])
    for c in (res_copy, hid_copy, gain_copy):
        c.wait()
    for c in range(chunks):
        remote(dn_ring.at[0], sums_out.at[1 - core, rows_of(c)], sib_ssem.at[c], sib_rsem.at[c], sibling).wait_recv()

        @pl.when(is_mid)
        def _(c=c):
            part_copy(c, dn_ring, dn_rsem).wait_send()

        @pl.when(not_mid)
        def _(c=c):
            part_copy(c, up_ring, up_rsem).wait_send()

        pair_done(c)


def backward(mesh, cot_all, a, b, q, kt, k, v, lse, mix, f1, f2, act, down, mid, hid, wqkv, wo, wg, wu, wd, gains, segc, segr, cos_t, sin_t):
    tp, dp = mesh.shape["tp"], mesh.shape["dp"]
    block, width = hid.shape
    length = tp * block
    hidden = wg.shape[1]
    heads = wo.shape[0] // HD
    kv_heads = (wqkv.shape[1] - heads * HD) // (2 * HD)
    qcols, kvcols = heads * HD, kv_heads * 2 * HD
    r = hidden // PAIR
    half_rows = (3 * hidden + 2 * qcols + kvcols) // 2
    chunks = half_rows // r
    steps = (dp - 1).bit_length() + (tp - 1).bit_length()
    sds = jax.ShapeDtypeStruct
    outs = [
        sds((block, width), BF),
        sds((block, width), BF),
        sds((2, half_rows, width), BF),
        sds((8, width), F32),
    ]
    dma = pltpu.SemaphoreType.DMA
    reg = pltpu.SemaphoreType.REGULAR
    scratch = [
        pltpu.VMEM((length, width), BF),
        pltpu.VMEM((hidden, length), BF),
        pltpu.VMEM((hidden, width), BF),
        pltpu.VMEM((hidden, length), BF),
        pltpu.VMEM((hidden, length), BF),
        pltpu.VMEM((width, hidden), BF),
        pltpu.VMEM((width, hidden), BF),
        pltpu.VMEM((length, width), BF),
        pltpu.VMEM((tp - 1, width, block), BF),
        pltpu.VMEM((tp - 1, width, block), BF),
        pltpu.VMEM((half_rows, width), BF),
        pltpu.VMEM((PAIR * r, width), BF),
        pltpu.VMEM((RING, r, width), BF),
        pltpu.VMEM((RING, r, width), BF),
        pltpu.VMEM((heads, HD, length), BF),
        pltpu.VMEM((kv_heads, HD, length), BF),
        pltpu.VMEM((kv_heads, length, 128), BF),
        pltpu.VMEM((kv_heads, length, 128), BF),
        pltpu.VMEM((heads, 1, length), F32),
        pltpu.VMEM((qcols, length), BF),
        pltpu.VMEM((heads, HD, length), BF),
        pltpu.VMEM((qcols + kvcols, length), BF),
        pltpu.VMEM((kv_heads, HD, length), F32),
        pltpu.VMEM((kv_heads, HD, length), F32),
        pltpu.VMEM((length, QB), F32),
        pltpu.VMEM((block, width), F32),
        pltpu.VMEM((block, width), BF),
        pltpu.VMEM((block, width), F32),
        pltpu.VMEM((width, block), F32),
        pltpu.VMEM((block, width), BF),
        pltpu.VMEM((qcols, width), BF),
        pltpu.VMEM((width, block), BF),
        pltpu.VMEM((8, width), F32),
        pltpu.VMEM((steps, 8, width), F32),
        dma((4 + 2 * tp + 20,)),
        dma((3,)),
        dma((chunks,)), dma((chunks,)), dma((chunks,)), dma((chunks,)), dma((chunks,)), dma((chunks,)), dma((chunks,)), dma((chunks,)), dma((chunks,)),
        dma((3, tp - 1, 2)), dma((3, tp - 1, 2)),
        dma((tp, 2)), dma((tp, 2)),
        dma((steps,)), dma((steps,)),
        reg, reg, reg, reg,
    ]
    any_ = pl.BlockSpec(memory_space=pl.ANY)
    vmem = pl.BlockSpec(memory_space=pltpu.VMEM)
    return pl.pallas_call(
        functools.partial(backward_kernel, tp, dp),
        out_shape=outs,
        in_specs=[any_] * 20 + [vmem] * 5,
        out_specs=[any_] * len(outs),
        scratch_shapes=scratch,
        compiler_params=pltpu.CompilerParams(collective_id=1, has_side_effects=True, vmem_limit_bytes=62 * 2**20),
        name="backward",
    )(cot_all, a, b, q, kt, k, v, lse, mix.reshape(qcols, length), f1, f2, act, down, mid, hid, wqkv, wo, wg, wu, wd, gains, segc, segr, cos_t, sin_t)


def rope_tables(segments):
    seg = segments[0]
    start = jnp.sum((seg[None, :] < seg[:, None]).astype(jnp.int32), axis=1)
    position = (jnp.arange(seg.shape[0], dtype=jnp.int32) - start).astype(F32)
    inverse = ROPE_BASE ** (-(jnp.arange(HALF, dtype=F32) * 2.0) / HD)
    angles = inverse[:, None] * position[None, :]
    return jnp.cos(angles), jnp.sin(angles)


def local(mesh, hidden, segments, cotangent, w_query, w_keyval, w_output, w_gate, w_up, w_down, gains):
    width = hidden.shape[2]
    cos_t, sin_t = rope_tables(segments)
    hid, cot = hidden[0], cotangent[0]
    wo = w_output[0]
    wqkv = jnp.concatenate([w_query[0], w_keyval[0].reshape(width, -1)], axis=1)
    wg, wu, wd = w_gate[0], w_up[0], w_down[0]
    segc, segr = segments.reshape(-1, 1), segments
    a, b, cot_all, q, kt, k, v, lse, mix, f1, f2, act, down, mid = forward(
        mesh, hid, cot, wqkv, wo, wg, wu, wd, gains[0], segc, segr, cos_t, sin_t
    )
    result, grad_hidden, sums, gain = backward(
        mesh, cot_all, a, b, q, kt, k, v, lse, mix, f1, f2, act, down, mid, hid,
        wqkv, wo, wg, wu, wd, gains[0], segc, segr, cos_t, sin_t,
    )
    rows = [wd.shape[0], wd.shape[0], wd.shape[0], wo.shape[0], wo.shape[0], wqkv.shape[1] - wo.shape[0]]
    at, grads = 0, []
    for n in rows:
        grads.append(sums[:, at : at + n // 2].reshape(n, width).astype(F32))
        at += n // 2
    down_g, gate_g, up_g, out_g, query_g, keyval_g = grads
    return (
        result[None],
        grad_hidden[None],
        query_g.T[None],
        keyval_g.T.reshape(1, width, *w_keyval.shape[2:]),
        out_g[None],
        gate_g.T[None],
        up_g.T[None],
        down_g[None],
        gain[None, :2],
    )


def solution(mesh):
    split = P("dp", "tp", None)
    columns, rows = P(None, None, "tp"), P(None, "tp", None)
    heads = P(None, None, "tp", None)
    return jax.shard_map(
        functools.partial(local, mesh),
        mesh=mesh,
        in_specs=(split, P("dp", None), split, columns, heads, rows, columns, columns, rows, P()),
        out_specs=(split, split, columns, heads, rows, columns, columns, rows, P()),
        check_vma=False,
    )
```

```python
import functools
import jax
import jax.numpy as jnp
from jax import lax
from jax.experimental import pallas as pl
from jax.experimental.pallas import tpu as pltpu
from jax.sharding import PartitionSpec as P

MESH = pl.DeviceIdType.MESH
HD = 96
HALF = HD // 2
EPS = 1e-05
ROPE_BASE = 100000.0
SCALE = HD ** (-0.5)
BF = jnp.bfloat16
F32 = jnp.float32
QB = 256


def flip(index, mask):
    out = index
    bit = 1
    while bit <= mask:
        if mask & bit:
            out = out + bit - 2 * bit * ((index // bit) % 2)
        bit *= 2
    return out


def nn(x, y):
    return lax.dot_general(x, y, (((1,), (0,)), ((), ())), preferred_element_type=F32)


def nt(x, y):
    return lax.dot_general(x, y, (((1,), (1,)), ((), ())), preferred_element_type=F32)


def normed(stream):
    inv = lax.rsqrt(jnp.mean(stream * stream, axis=-1, keepdims=True) + EPS)
    return stream * inv, inv


def rot_rows(x, cos, sin):
    x1, x2 = x[:HALF], x[HALF:]
    return jnp.concatenate([x1 * cos - x2 * sin, x2 * cos + x1 * sin], axis=0)


def forward_kernel(
    tp, dp,
    hid, cot, wq, wkv_t, wo, wg, wu, wd, gains, segr, inverse,
    wqkv_out, seg_out, cos_out, sin_out, a_out, b_out, cot_all, q_out, kt_out, k_out, v_out, lse_out, mix_out, f1_out, f2_out, act_out, down_out, mid_out,
    hid_all, mixed_all, wo_all, wq_in, w_in, w_st, wqkv_t, wg_t, wu_t, wd_n, wd_t,
    a_v, b_v, q_t, k_t, k_n, v_n, v_t, mix_t, bias, lse, f1, f2, act_t, down_v, mid_v, mid_w, segc, cos_t, sin_t,
    load_sem, out_sem, hid_ssem, hid_rsem, cot_ssem, cot_rsem, mix_ssem, mix_rsem, wo_ssem, wo_rsem,
):
    me, md = lax.axis_index("tp"), lax.axis_index("dp")
    nz = dp // 2
    core, mz = md % 2, md // 2
    block, width = hid.shape
    length = tp * block
    hidden = wg.shape[1]
    heads, kv_heads = q_t.shape[0], k_t.shape[0]
    qcols, kvcols = heads * HD, kv_heads * 2 * HD
    pieces = length // QB
    hops = tp == 4
    rows_o = qcols // dp
    spread = qcols % (16 * dp) == 0
    half = block // 2

    loads = [
        pltpu.make_async_copy(wq, wq_in, load_sem.at[0]),
        pltpu.make_async_copy(wd, wd_n, load_sem.at[1]),
        pltpu.make_async_copy(hid, hid_all.at[me], load_sem.at[2]),
        pltpu.make_async_copy(wg, w_st, load_sem.at[3]),
        pltpu.make_async_copy(wo, wo_all.at[me], load_sem.at[4]),
        pltpu.make_async_copy(wkv_t, wqkv_t.at[pl.ds(qcols, kvcols)], load_sem.at[5]),
    ]
    for c in loads:
        c.start()

    barrier = pltpu.get_barrier_semaphore()
    peers = [(md, flip(me, p)) for p in range(1, tp)]
    if spread:
        peers += [(flip(md, 2 * z), me) for z in range(1, nz)] + [(flip(md, 1), me)]
    for peer in peers:
        pl.semaphore_signal(barrier, inc=1, device_id=peer, device_id_type=MESH)
    pl.semaphore_wait(barrier, len(peers))

    def remote(src, dst, ssem, rsem, peer):
        return pltpu.make_async_remote_copy(src, dst, ssem, rsem, device_id=peer, device_id_type=MESH)

    def gather_first(src, dst, ssem, rsem, cols=pl.ds(0, width)):
        out = []
        for p in range(1, tp):
            if hops and p == 3:
                continue
            for part in (0, 1) if p == 1 else (1, 0):
                rows = pl.ds(part * half, half)
                out.append(remote(src.at[rows, cols], dst.at[me, rows], ssem.at[p, part], rsem.at[p, part], (md, flip(me, p))))
        return out

    def arrived(dst, ssem, rsem, p, part):
        rows = pl.ds(part * half, half)
        slot = dst.at[flip(me, p), rows]
        return remote(slot, slot, ssem.at[p, part], rsem.at[p, part], (md, flip(me, p)))

    def handed(dst, ssem, rsem, part):
        rows = pl.ds(part * half, half)
        came, goes = (1, 2) if part == 0 else (2, 1)
        slot = dst.at[flip(me, came), rows]
        return remote(slot, slot, ssem.at[3, part], rsem.at[3, part], (md, flip(me, goes)))

    hid_first = gather_first(hid, hid_all, hid_ssem, hid_rsem)
    cot_first = gather_first(cot, cot_all, cot_ssem, cot_rsem, pl.ds(0, width // 2))

    piece = pl.ds((core * nz + mz) * rows_o, rows_o) if spread else pl.ds(0, qcols)
    wo_tp = [
        remote(wo.at[piece], wo_all.at[me, piece], wo_ssem.at[0, p], wo_rsem.at[0, p], (md, flip(me, p)))
        for p in range(1, tp)
    ]
    for c in wo_tp:
        c.start()
    for c in hid_first:
        c.start()
    wo_z, wo_core = [], []
    if spread:
        for z in range(1, nz):
            for p in range(1, tp):
                slot = wo_all.at[flip(me, p), piece]
                wo_z.append(remote(slot, slot, wo_ssem.at[z, p], wo_rsem.at[z, p], (flip(md, 2 * z), me)))
        both = pl.ds(core * nz * rows_o, nz * rows_o)
        for p in range(1, tp):
            slot = wo_all.at[flip(me, p), both]
            wo_core.append(remote(slot, slot, wo_ssem.at[nz, p], wo_rsem.at[nz, p], (flip(md, 1), me)))

    def turn(dst, src, step=256):
        rows = src.shape[0]
        for r in range(0, rows, step):
            dst[:, pl.ds(r, step)] = src[pl.ds(r, step), :].T

    def project(src):
        off = pl.multiple_of(src * block, block)
        cols = pl.ds(off, block)
        base, _ = normed(hid_all[src].astype(F32))
        a = (base * gains[0:1, :]).astype(BF)
        a_v[cols, :] = a
        cos, sin = cos_t[:, cols], sin_t[:, cols]
        qk = nt(wqkv_t[...], a)
        for h in range(heads):
            q_t[h, :, cols] = rot_rows(qk[h * HD : (h + 1) * HD], cos, sin).astype(BF)
        pad = jnp.zeros((128 - HD, block), F32)
        for g in range(kv_heads):
            at = qcols + g * 2 * HD
            kr = rot_rows(qk[at : at + HD], cos, sin)
            vr = qk[at + HD : at + 2 * HD]
            k_t[g, :, cols] = kr.astype(BF)
            v_t[g, :, cols] = vr.astype(BF)
            k_n[g, cols, :] = jnp.concatenate([kr, pad], axis=0).T.astype(BF)
            v_n[g, cols, :] = jnp.concatenate([vr, pad], axis=0).T.astype(BF)

    segc[...] = jnp.broadcast_to(segr[...].astype(F32), (128, length)).T[:, :8].astype(jnp.int32)
    start = jnp.sum((segc[:, 0:1] < segr[...]).astype(F32), axis=0, keepdims=True)
    place = lax.broadcasted_iota(jnp.int32, (1, length), 1).astype(F32) - start
    angles = inverse[...] * place
    cos_t[...] = jnp.cos(angles)
    sin_t[...] = jnp.sin(angles)
    loads[0].wait()
    turn(wqkv_t.at[pl.ds(0, qcols)], wq_in)
    w_in[:, 0:qcols] = wq_in[...]
    loads[5].wait()
    w_in[:, qcols : qcols + kvcols] = wqkv_t[qcols : qcols + kvcols, :].T
    loads[2].wait()
    project(me)
    for c in wo_tp:
        c.wait()
    for c in wo_z:
        c.start()
    loads[3].wait()
    turn(wg_t, w_st)
    wu_load = pltpu.make_async_copy(wu, w_st, load_sem.at[3])
    wu_load.start()
    wu_load.wait()
    turn(wu_t, w_st)
    loads[1].wait()
    turn(wd_t, wd_n)
    loads[4].wait()

    if hops:
        for p, part in ((1, 0), (2, 1)):
            arrived(hid_all, hid_ssem, hid_rsem, p, part).wait_recv()
            handed(hid_all, hid_ssem, hid_rsem, part).start()
        for p, part in ((1, 1), (2, 0)):
            arrived(hid_all, hid_ssem, hid_rsem, p, part).wait_recv()
            project(flip(me, p))
        for part in (0, 1):
            rows = pl.ds(part * half, half)
            slot = hid_all.at[flip(me, 3), rows]
            remote(slot, slot, hid_ssem.at[3, part], hid_rsem.at[3, part], (md, flip(me, 2))).wait_recv()
        project(flip(me, 3))
    else:
        for p in range(1, tp):
            for part in (0, 1):
                arrived(hid_all, hid_ssem, hid_rsem, p, part).wait_recv()
            project(flip(me, p))

    outs = []

    def put(src, dst):
        c = pltpu.make_async_copy(src, dst, out_sem.at[len(outs)])
        c.start()
        outs.append(c)

    for src, dst in ((w_in, wqkv_out), (segc, seg_out), (cos_t, cos_out), (sin_t, sin_out), (a_v, a_out), (q_t, q_out), (k_t, kt_out), (k_n, k_out), (v_n, v_out)):
        put(src, dst)

    def mix_slot(who, i):
        return mixed_all.at[who, pl.ds(i * QB, QB)]

    def mix_copy(i, p):
        return remote(mix_slot(me, i), mix_slot(me, i), mix_ssem.at[p, i], mix_rsem.at[p, i], (md, flip(me, p)))

    def mix_arrived(i, p):
        slot = mix_slot(flip(me, p), i)
        return remote(slot, slot, mix_ssem.at[p, i], mix_rsem.at[p, i], (md, flip(me, p)))

    def mix_handed(i):
        came, goes = (1, 2) if i % 2 == 0 else (2, 1)
        slot = mix_slot(flip(me, came), i)
        return remote(slot, slot, mix_ssem.at[3, i], mix_rsem.at[3, i], (md, flip(me, goes)))

    def hand_on(i):
        if not hops:
            return
        mix_arrived(i, 1 if i % 2 == 0 else 2).wait_recv()
        mix_handed(i).start()

    for i in range(pieces):
        reach = (i + 1) * QB
        cols = pl.ds(i * QB, QB)
        same = segc[pl.ds(0, reach), 0:1] == segr[:, cols]
        later = lax.broadcasted_iota(jnp.int32, (reach, QB), 0) <= lax.broadcasted_iota(jnp.int32, (reach, QB), 1) + i * QB
        bias[pl.ds(0, reach), :] = jnp.where(same & later, 0.0, -1e30)

        def head(h, _, reach=reach, cols=cols):
            g = h // (heads // kv_heads)
            s = nn(k_n[g, pl.ds(0, reach), :][:, :HD], q_t[h, :, cols]) * SCALE + bias[pl.ds(0, reach), :]
            top = jnp.max(s, axis=0, keepdims=True)
            e = jnp.exp(s - top)
            total = jnp.sum(e, axis=0, keepdims=True)
            p = (e * (1.0 / total)).astype(BF)
            mix_t[h, :, cols] = nn(v_t[g, :, pl.ds(0, reach)], p).astype(BF)
            lse[h, :, cols] = top + jnp.log(total)
            return 0

        lax.fori_loop(0, heads, head, 0)
        mixed_all[me, cols, :] = mix_t[:, :, cols].reshape(qcols, QB).T
        for p in range(1, tp):
            if not (hops and p == 3):
                mix_copy(i, p).start()
        if i:
            hand_on(i - 1)
    put(lse, lse_out)
    put(mix_t, mix_out)
    for c in wo_z:
        c.wait()
    for c in wo_core:
        c.start()

    def middle(i):
        rows = pl.ds(i * QB, QB)
        for p in range(1, tp):
            if hops and p == 3:
                slot = mix_slot(flip(me, 3), i)
                remote(slot, slot, mix_ssem.at[3, i], mix_rsem.at[3, i], (md, flip(me, 1))).wait_recv()
            elif not (hops and p == (1 if i % 2 == 0 else 2)):
                mix_arrived(i, p).wait_recv()
        per = QB // block if QB >= block else 1
        mixed = jnp.concatenate([mixed_all[s, rows, :] for s in range(tp)], axis=1)
        for d in range(0, width, 512):
            cols = pl.ds(d, 512)
            stream = jnp.concatenate([hid_all[i * per + n, :, cols] for n in range(per)], axis=0).astype(F32)
            mid_w[:, cols] = stream + nn(mixed, wo_all[:, :, cols].reshape(tp * qcols, 512))
        total = mid_w[...]
        base, _ = normed(total)
        b_v[rows, :] = (base * gains[1:2, :]).astype(BF)
        for n in range(per):
            @pl.when(me == i * per + n)
            def _(n=n):
                mid_v[...] = total[n * block : (n + 1) * block]

    def feed(i):
        rows = pl.ds(i * QB, QB)
        b = b_v[rows, :]
        step = 256
        for f in range(0, hidden, step):
            units = pl.ds(f, step)
            gate = nt(wg_t[units, :], b)
            up = nt(wu_t[units, :], b)
            sig = jax.nn.sigmoid(gate)
            silu = gate * sig
            f1[units, rows] = (up * sig * (1.0 + gate * (1.0 - sig))).astype(BF)
            f2[units, rows] = silu.astype(BF)
            act_t[units, rows] = (silu * up).astype(BF)
        down_v[:, rows] = nn(wd_t[...], act_t[:, rows]).astype(BF)
        put(b_v.at[rows], b_out.at[rows])
        for src, dst in ((f1, f1_out), (f2, f2_out), (act_t, act_out), (down_v, down_out)):
            put(src.at[:, rows], dst.at[:, rows])

    for c in wo_core:
        c.wait()
    for i in range(pieces):
        middle(i)
        if i == min(1, pieces - 1):
            hand_on(pieces - 1)
            for n in range(pieces):
                for p in range(1, tp):
                    if not (hops and p == 3):
                        mix_copy(n, p).wait_send()
            for c in cot_first:
                c.start()
        feed(i)
    put(mid_v, mid_out)

    if hops:
        for p, part in ((1, 0), (2, 1)):
            arrived(cot_all, cot_ssem, cot_rsem, p, part).wait_recv()
            handed(cot_all, cot_ssem, cot_rsem, part).start()
        for p, part in ((1, 1), (2, 0)):
            arrived(cot_all, cot_ssem, cot_rsem, p, part).wait_recv()
        for part in (0, 1):
            rows = pl.ds(part * half, half)
            slot = cot_all.at[flip(me, 3), rows]
            remote(slot, slot, cot_ssem.at[3, part], cot_rsem.at[3, part], (md, flip(me, 2))).wait_recv()
    else:
        for p in range(1, tp):
            for part in (0, 1):
                arrived(cot_all, cot_ssem, cot_rsem, p, part).wait_recv()
    for c in hid_first + cot_first:
        c.wait_send()
    if hops:
        for part in (0, 1):
            handed(hid_all, hid_ssem, hid_rsem, part).wait_send()
            handed(cot_all, cot_ssem, cot_rsem, part).wait_send()
        for i in range(pieces):
            mix_handed(i).wait_send()
    for c in outs:
        c.wait()


def forward(mesh, hid, cot, wq, wkv_t, wo, wg, wu, wd, gains, segr, inverse):
    tp, dp = mesh.shape["tp"], mesh.shape["dp"]
    block, width = hid.shape
    length = tp * block
    hidden = wg.shape[1]
    heads = wo.shape[0] // HD
    kv_heads = wkv_t.shape[0] // (2 * HD)
    nz = dp // 2
    pieces = length // QB
    sds = jax.ShapeDtypeStruct
    outs = [
        sds((width, (heads + 2 * kv_heads) * HD), BF),
        sds((length, 8), jnp.int32),
        sds((HALF, length), F32),
        sds((HALF, length), F32),
        sds((length, width), BF),
        sds((length, width), BF),
        sds((tp, block, width // 2), BF),
        sds((heads, HD, length), BF),
        sds((kv_heads, HD, length), BF),
        sds((kv_heads, length, 128), BF),
        sds((kv_heads, length, 128), BF),
        sds((heads, 1, length), F32),
        sds((heads, HD, length), BF),
        sds((hidden, length), BF),
        sds((hidden, length), BF),
        sds((hidden, length), BF),
        sds((width, length), BF),
        sds((block, width), F32),
    ]
    dma = pltpu.SemaphoreType.DMA
    scratch = [
        pltpu.VMEM((tp, block, width), BF),
        pltpu.VMEM((tp, length, heads * HD), BF),
        pltpu.VMEM((tp, heads * HD, width), BF),
        pltpu.VMEM((width, heads * HD), BF),
        pltpu.VMEM((width, heads * HD + kv_heads * 2 * HD), BF),
        pltpu.VMEM((width, hidden), BF),
        pltpu.VMEM((heads * HD + kv_heads * 2 * HD, width), BF),
        pltpu.VMEM((hidden, width), BF),
        pltpu.VMEM((hidden, width), BF),
        pltpu.VMEM((hidden, width), BF),
        pltpu.VMEM((width, hidden), BF),
        pltpu.VMEM((length, width), BF),
        pltpu.VMEM((length, width), BF),
        pltpu.VMEM((heads, HD, length), BF),
        pltpu.VMEM((kv_heads, HD, length), BF),
        pltpu.VMEM((kv_heads, length, 128), BF),
        pltpu.VMEM((kv_heads, length, 128), BF),
        pltpu.VMEM((kv_heads, HD, length), BF),
        pltpu.VMEM((heads, HD, length), BF),
        pltpu.VMEM((length, QB), F32),
        pltpu.VMEM((heads, 1, length), F32),
        pltpu.VMEM((hidden, length), BF),
        pltpu.VMEM((hidden, length), BF),
        pltpu.VMEM((hidden, length), BF),
        pltpu.VMEM((width, length), BF),
        pltpu.VMEM((block, width), F32),
        pltpu.VMEM((QB, width), F32),
        pltpu.VMEM((length, 8), jnp.int32),
        pltpu.VMEM((HALF, length), F32),
        pltpu.VMEM((HALF, length), F32),
        dma((6,)),
        dma((12 + 5 * pieces,)),
        dma((tp, 2)),
        dma((tp, 2)),
        dma((tp, 2)),
        dma((tp, 2)),
        dma((tp, pieces)),
        dma((tp, pieces)),
        dma((nz + 1, tp)),
        dma((nz + 1, tp)),
    ]
    any_ = pl.BlockSpec(memory_space=pl.ANY)
    vmem = pl.BlockSpec(memory_space=pltpu.VMEM)
    return pl.pallas_call(
        functools.partial(forward_kernel, tp, dp),
        out_shape=outs,
        in_specs=[any_] * 8 + [vmem] * 3,
        out_specs=[any_] * len(outs),
        scratch_shapes=scratch,
        compiler_params=pltpu.CompilerParams(collective_id=0, has_side_effects=True, vmem_limit_bytes=62 * 2**20),
        name="forward",
    )(hid, cot, wq, wkv_t, wo, wg, wu, wd, gains, segr, inverse)


RING = 8
AHEAD = 1
PAIR = 16


def unrot_rows(d, cos, sin):
    d1, d2 = d[:HALF], d[HALF:]
    return jnp.concatenate([d1 * cos + d2 * sin, d2 * cos - d1 * sin], axis=0)


def norm_back(grad, base, inv, gain):
    e = grad * gain
    back = inv * (e - base * jnp.mean(e * base, axis=-1, keepdims=True))
    return back, jnp.sum(grad * base, axis=0, keepdims=True)


def backward_kernel(
    tp, dp,
    cot, cot_all, a_in, b_in, q_in, kt_in, k_in, v_in, lse_in, mix_in, f1_in, f2_in, act_in, down_in, mid_in, hid_in,
    wqkv, wo, wg, wu, wd, gains, segc, segr, cos_t, sin_t,
    res_out, hid_out, sums_out, gain_out,
    tok, act, wd_v, f1, f2, wg_v, wu_v, ab, snd, rcv, acc, pair, up_ring, dn_ring,
    q_t, k_t, k_n, v_n, lse, mix, gm_t, gqkv, dk, dv, bias, mid, hid, gs, own, gb, wo_v, stage, gsum, gland,
    load_sem, out_sem, pair_ssem, pair_rsem, part_ssem, up_rsem, dn_rsem, tot_ssem, sib_ssem, sib_rsem, fin_sem,
    rs_ssem, rs_rsem, tok_ssem, tok_rsem, gain_ssem, gain_rsem, cr_pair, cr_dn, cr_up, cr_rs,
):
    me, md = lax.axis_index("tp"), lax.axis_index("dp")
    nz = dp // 2
    core, mz = md % 2, md // 2
    length, width = tok.shape
    block = length // tp
    half = block // 2
    hidden = act.shape[0]
    heads, kv_heads = q_t.shape[0], k_t.shape[0]
    group = heads // kv_heads
    qcols, kvcols = heads * HD, kv_heads * 2 * HD
    hops = tp == 4
    r = hidden // PAIR
    parts = [hidden, hidden, hidden, qcols, qcols, kvcols]
    first = [sum(p // 2 for p in parts[:n]) // r for n in range(6)]
    chunks = sum(parts) // 2 // r
    own_rows = pl.ds(pl.multiple_of(me * block, block), block)

    def load(n, src, dst):
        return pltpu.make_async_copy(src, dst, load_sem.at[n])

    early = [load(0, act_in, act)] + [
        load(
            1 + p,
            cot_all.at[flip(me, p)] if p else cot,
            tok.at[pl.ds(pl.multiple_of(flip(me, p) * block, block), block), pl.ds(0, width // 2 if p else width)],
        )
        for p in range(tp)
    ]
    n0 = 1 + tp
    then = [load(n0, wd.at[pl.ds(hidden // 2, hidden // 2)], wd_v.at[pl.ds(hidden // 2, hidden // 2)]), load(n0 + 1, f1_in, f1), load(n0 + 2, f2_in, f2)]
    late = [
        load(n0 + 3 + n, s, d)
        for n, (s, d) in enumerate(
            (
                (wg, wg_v), (wu, wu_v), (b_in, ab), (q_in, q_t), (kt_in, k_t), (k_in, k_n), (v_in, v_n), (lse_in, lse),
                (mix_in, mix), (mid_in, mid), (hid_in, hid), (wo, wo_v),
            )
        )
    ]
    n1 = n0 + 3 + len(late)
    for c in early:
        c.start()

    barrier = pltpu.get_barrier_semaphore()
    peers = [(md, flip(me, p)) for p in range(1, tp)] + [(flip(md, p), me) for p in range(1, dp)]
    for peer in peers:
        pl.semaphore_signal(barrier, inc=1, device_id=peer, device_id_type=MESH)
    pl.semaphore_wait(barrier, len(peers))

    def remote(src, dst, ssem, rsem, peer):
        return pltpu.make_async_remote_copy(src, dst, ssem, rsem, device_id=peer, device_id_type=MESH)

    def signal(sem, peer):
        pl.semaphore_signal(sem, inc=1, device_id=peer, device_id_type=MESH)

    left = mz < nz // 2
    step_in = jnp.where(left, 1, -1)
    is_mid = (mz == nz // 2 - 1) | (mz == nz // 2)
    has_up = (mz != 0) & (mz != nz - 1)
    not_mid, no_up = jnp.logical_not(is_mid), jnp.logical_not(has_up)
    sibling = (md + 1 - 2 * core, me)
    down_dev = (md + 2 * step_in, me)
    up_dev = (md - 2 * step_in, me)

    def rows_of(c):
        return pl.ds(c * r, r)

    def pair_copy(c):
        slot = pl.ds((c % PAIR) * r, r)
        return remote(wd_v.at[slot], pair.at[slot], pair_ssem.at[c], pair_rsem.at[c], sibling)

    def part_copy(c, dst, rsem):
        return remote(acc.at[rows_of(c)], dst.at[c % RING], part_ssem.at[c], rsem.at[c], down_dev)

    def total_copy(c):
        return remote(dn_ring.at[c % RING], dn_ring.at[c % RING], tot_ssem.at[c], dn_rsem.at[c], up_dev)

    def sib_copy(c):
        return remote(dn_ring.at[c % RING], sums_out.at[core, rows_of(c)], sib_ssem.at[c], sib_rsem.at[c], sibling)

    def fin_copy(c):
        return pltpu.make_async_copy(dn_ring.at[c % RING], sums_out.at[core, rows_of(c)], fin_sem.at[c])

    def gather_part(c):
        pair_copy(c).wait_recv()
        total = acc[rows_of(c), :].astype(F32) + pair[pl.ds((c % PAIR) * r, r), :].astype(F32)
        acc[rows_of(c), :] = total.astype(BF)

        @pl.when(has_up)
        def _():
            remote(up_ring.at[c % RING], up_ring.at[c % RING], part_ssem.at[c], up_rsem.at[c], up_dev).wait_recv()
            acc[rows_of(c), :] = (acc[rows_of(c), :].astype(F32) + up_ring[c % RING].astype(F32)).astype(BF)
            if c + RING < chunks:
                signal(cr_dn, up_dev)

        if c + PAIR < chunks:
            signal(cr_pair, sibling)
        if c >= RING:
            pl.semaphore_wait(cr_dn, 1)

        @pl.when(is_mid)
        def _():
            part_copy(c, dn_ring, dn_rsem).start()

        @pl.when(not_mid)
        def _():
            part_copy(c, up_ring, up_rsem).start()

    def spread_total(c):
        remote(dn_ring.at[c % RING], dn_ring.at[c % RING], tot_ssem.at[c], dn_rsem.at[c], down_dev).wait_recv()

        @pl.when(is_mid)
        def _():
            dn_ring[c % RING] = (acc[rows_of(c), :].astype(F32) + dn_ring[c % RING].astype(F32)).astype(BF)

        @pl.when(has_up)
        def _():
            if c >= RING:
                pl.semaphore_wait(cr_up, 1)
            total_copy(c).start()

        sib_copy(c).start()
        fin_copy(c).start()

    def retire(c):
        @pl.when(has_up)
        def _():
            total_copy(c).wait_send()

        sib_copy(c).wait_send()
        fin_copy(c).wait()
        if c + RING < chunks:

            @pl.when(is_mid)
            def _():
                signal(cr_dn, down_dev)

            @pl.when(not_mid)
            def _():
                signal(cr_up, down_dev)

    slot_now = [0]
    ready, given = set(), set()
    lag = 2

    def when_chunk(cond, fn, c):
        if 0 <= c < chunks:

            @pl.when(cond)
            def _():
                fn(c)

    def z(count=1):
        for _ in range(count):
            k = slot_now[0]
            slot_now[0] += 1
            assert set(range(min(chunks, k + AHEAD + 1))) <= ready & given
            if k == 0:
                for c in range(AHEAD):
                    when_chunk(no_up, gather_part, c)
            when_chunk(no_up, gather_part, k + AHEAD)
            when_chunk(has_up, gather_part, k - lag)
            when_chunk(is_mid, retire, k - 2 * lag - 2)
            when_chunk(not_mid, retire, k - 3 * lag - 2)
            when_chunk(is_mid, spread_total, k - 2 * lag)
            when_chunk(not_mid, spread_total, k - 3 * lag)

    sent = set()

    def pair_done(c):
        if c not in sent:
            sent.add(c)
            pair_copy(c).wait_send()

    def down_grad(side, mine):
        hr = parts[0] // 2
        pr = min(256, hr)
        which = core if mine else 1 - core
        cols = pl.ds(side * (width // 2), width // 2)
        for p in range(hr // pr):
            value = nn(act[pl.ds(pl.multiple_of(which * hr + p * pr, 16), pr), :], tok[:, cols]).astype(BF)
            for j in range(pr // (2 * r)):
                c = side * (hr // (2 * r)) + p * (pr // (2 * r)) + j
                packed = jnp.concatenate([value[2 * r * j : 2 * r * j + r], value[2 * r * j + r : 2 * r * (j + 1)]], axis=1)
                (ready if mine else given).add(c)
                if mine:
                    acc[rows_of(c), :] = packed
                else:
                    wd_v[rows_of(c), :] = packed
                    pair_copy(c).start()

    def weight_grad(n, lhs, rhs, mine):
        hr = parts[n] // 2
        pr = min(256, hr)
        which = core if mine else 1 - core
        for p in range(hr // pr):
            value = nn(lhs[pl.ds(pl.multiple_of(which * hr + p * pr, 16), pr), :], rhs[...]).astype(BF)
            at = first[n] + p * pr // r
            (ready if mine else given).update(range(at, at + pr // r))
            assert mine or at + pr // r - PAIR <= slot_now[0] - lag
            if mine:
                acc[pl.ds(at * r, pr), :] = value
                continue
            for c in range(pr // r):
                if at + c >= PAIR:
                    pair_done(at + c - PAIR)
                    pl.semaphore_wait(cr_pair, 1)
                wd_v[pl.ds(((at + c) % PAIR) * r, r), :] = value[c * r : (c + 1) * r]
                pair_copy(at + c).start()

    direct = [p for p in range(1, tp) if not (hops and p == 3)]
    columns = (pl.ds(width // 2, width // 2), pl.ds(0, width))
    sources = (cot, gb)

    def tok_rows(u, p, part):
        return tok.at[pl.ds(pl.multiple_of(flip(me, p) * block + part * half, half), half), columns[u]]

    def tok_copy(u, p, part):
        src = sources[u].at[pl.ds(part * half, half), columns[u]]
        return remote(src, tok_rows(u, 0, part), tok_ssem.at[u, p, part], tok_rsem.at[u, p, part], (md, flip(me, p)))

    def tok_arrived(u, p, part):
        return remote(tok_rows(u, p, part), tok_rows(u, p, part), tok_ssem.at[u, p, part], tok_rsem.at[u, p, part], (md, flip(me, p)))

    def tok_handed(u, part):
        came, goes = (1, 2) if part == 0 else (2, 1)
        return remote(
            tok_rows(u, came, part), tok_rows(u, came, part), tok_ssem.at[u, 3, part], tok_rsem.at[u, 3, part], (md, flip(me, goes))
        )

    def tok_start(u):
        for p in direct:
            for part in (0, 1) if p == 1 else (1, 0):
                tok_copy(u, p, part).start()

    def tok_hand_on(u):
        if hops:
            for part in (0, 1):
                tok_arrived(u, 1 if part == 0 else 2, part).wait_recv()
                tok_handed(u, part).start()
            for part in (0, 1):
                tok_arrived(u, 2 if part == 0 else 1, part).wait_recv()

    def tok_finish(u):
        for p in range(1, tp):
            if hops and p != 3:
                continue
            for part in (0, 1):
                tok_arrived(u, p, part).wait_recv()
        for p in direct:
            for part in (0, 1):
                tok_copy(u, p, part).wait_send()
        if hops:
            for part in (0, 1):
                tok_handed(u, part).wait_send()

    first_half, second_half = pl.ds(0, width // 2), pl.ds(width // 2, width // 2)
    halves = (first_half, second_half)

    def rs_copy(u, slot, part, p, ahead=False):
        return remote(
            snd.at[slot, halves[part]], rcv.at[slot, halves[part]], rs_ssem.at[u, slot, part], rs_rsem.at[u, slot, part], (md, flip(me, p))
        )

    def rs_send(u, p):
        if hops and p == 3:
            rs_copy(u, 2, 0, 1).start()
            rs_copy(u, 2, 1, 2).start()
        elif hops:
            rs_copy(u, p - 1, p - 1, p).start()
        else:
            for part in (0, 1):
                rs_copy(u, p - 1, part, p).start()

    def rs_merge(u, p):
        if not hops:
            return
        part = 2 - p
        rs_copy(u, 2, part, 3 - p).wait_recv()
        h = halves[part]
        snd[p - 1, h, :] = (snd[p - 1, h, :].astype(F32) + rcv[2, h, :].astype(F32)).astype(BF)
        rs_copy(u, p - 1, part, p).start()

    def rs_finish(u):
        for p in range(1, tp):
            if hops and p == 3:
                continue
            for part in (0, 1):
                rs_copy(u, p - 1, part, p).wait_recv()
        for p in range(1, tp):
            for part in (0, 1):
                rs_copy(u, p - 1, part, (1 if part == 0 else 2) if hops and p == 3 else p).wait_send()
        total = own[...]
        for p in range(1, tp):
            if not (hops and p == 3):
                total = total + rcv[p - 1].astype(F32)
        return total.T

    order = range(tp - 1, 0, -1) if not hops else (3, 1, 2)

    def gib_into(put, p):
        cols = pl.ds(pl.multiple_of(flip(me, p) * block, block), block)
        for d in range(0, width, 512):
            rows = pl.ds(d, 512)
            put(rows, nn(wg_v[rows, :], f1[:, cols]) + nn(wu_v[rows, :], f2[:, cols]))

    def gia_into(put, p):
        cols = pl.ds(pl.multiple_of(flip(me, p) * block, block), block)
        for d in range(0, width, 512):
            rows = pl.ds(d, 512)
            put(rows, nn(wg_v[rows, 0 : qcols + kvcols], gqkv[:, cols]))

    def to_snd(p):
        def put(rows, value):
            snd[p - 1, rows, :] = value.astype(BF)

        return put

    def to_own(rows, value):
        own[rows, :] = value

    tok_start(0)
    for c in early:
        c.wait()
    for c in then:
        c.start()
    gsum[...] = jnp.zeros_like(gsum)
    mid_rows = hidden // 2
    def gate_grads(start):
        step = min(512, mid_rows)
        for i in range(length // QB):
            cols = pl.ds(i * QB, QB)
            for f in range(start, start + mid_rows, step):
                units = pl.ds(f, step)
                grad_act = nt(wd_v[units, :], tok[cols, :])
                f1[units, cols] = (grad_act * f1[units, cols].astype(F32)).astype(BF)
                f2[units, cols] = (grad_act * f2[units, cols].astype(F32)).astype(BF)

    down_grad(0, False)
    down_grad(0, True)
    z()
    for c in then:
        c.wait()
    for c in late:
        c.start()
    z()
    tok_hand_on(0)
    z()
    tok_finish(0)
    down_grad(1, False)
    down_grad(1, True)
    z()
    gate_grads(mid_rows)
    z()
    for c in range(PAIR // 2):
        pair_done(c)
    rest = load(n1 + 3 + tp, wd.at[pl.ds(0, mid_rows)], wd_v.at[pl.ds(0, mid_rows)])
    rest.start()
    rest.wait()
    gate_grads(0)
    z()
    for c in late[:2]:
        c.wait()
    for n, p in enumerate(order):
        gib_into(to_snd(p), p)
        rs_send(0, p)
        if n == 1:
            z()
    late[2].wait()
    weight_grad(1, f1, ab, False)
    weight_grad(1, f1, ab, True)
    z(2)
    if hops:
        rs_merge(0, 1)
        rs_merge(0, 2)
    gib_into(to_own, 0)
    z(3)
    for c in late[3:]:
        c.wait()
    qkv_load = load(n1, wqkv, wg_v.at[:, pl.ds(0, qcols + kvcols)])
    qkv_load.start()

    grad_in = rs_finish(0)
    base_b, inv_b = normed(mid[...])
    back, gain_b = norm_back(grad_in, base_b, inv_b, gains[1:2, :])
    gs[...] = tok[own_rows, :].astype(F32) + back
    gsum[1:2, :] = gain_b
    gb[...] = gs[...].astype(BF)
    tok[own_rows, :] = gb[...]

    tok_start(1)
    z()
    weight_grad(2, f2, ab, False)
    z()
    weight_grad(2, f2, ab, True)
    z(2)
    a_load = load(n1 + 2, a_in, ab)
    a_load.start()
    tok_hand_on(1)
    z(2)
    tok_finish(1)

    weight_grad(3, mix, tok, False)
    weight_grad(3, mix, tok, True)
    down_loads = []
    for n, p in enumerate((*order, 0)):
        cols = pl.ds(pl.multiple_of(flip(me, p) * block, block), block)
        down_loads.append(load(n1 + 3 + n, down_in.at[:, cols], snd.at[p - 1] if p else stage))
    for c in down_loads:
        c.start()
    for n in range(0, length, QB):
        cols = pl.ds(n, QB)
        gm_t[:, :, cols] = nt(wo_v[...], tok[cols, :]).astype(BF).reshape(heads, HD, QB)
    for c in down_loads:
        c.wait()
    for p in order:
        rs_send(1, p)
    own[...] = stage[...].astype(F32)
    z()

    dk[...] = jnp.zeros_like(dk)
    dv[...] = jnp.zeros_like(dv)
    for i in range(length // QB - 1, -1, -1):
        reach = (i + 1) * QB
        cols = pl.ds(i * QB, QB)
        same = segc[pl.ds(0, reach), 0:1] == segr[:, cols]
        later = lax.broadcasted_iota(jnp.int32, (reach, QB), 0) <= lax.broadcasted_iota(jnp.int32, (reach, QB), 1) + i * QB
        bias[pl.ds(0, reach), :] = jnp.where(same & later, 0.0, -1e30)

        def head(h, _, reach=reach, cols=cols):
            g = h // group
            s = nn(k_n[g, pl.ds(0, reach), :][:, :HD], q_t[h, :, cols]) * SCALE + bias[pl.ds(0, reach), :]
            p = jnp.exp(s - lse[h, :, cols])
            grad_p = nn(v_n[g, pl.ds(0, reach), :][:, :HD], gm_t[h, :, cols])
            delta = jnp.sum(p * grad_p, axis=0, keepdims=True)
            ds = (p * (grad_p - delta)).astype(BF)
            dq = nn(k_t[g, :, pl.ds(0, reach)], ds) * SCALE
            gqkv[pl.ds(pl.multiple_of(h * HD, 16), HD), cols] = unrot_rows(dq, cos_t[:, cols], sin_t[:, cols]).astype(BF)
            dk[g, :, pl.ds(0, reach)] += nt(q_t[h, :, cols], ds)
            dv[g, :, pl.ds(0, reach)] += nt(gm_t[h, :, cols], p.astype(BF))
            return 0

        lax.fori_loop(0, heads, head, 0)
        z()
        if i == length // QB - 2 and hops:
            rs_merge(1, 1)
            rs_merge(1, 2)
    for g in range(kv_heads):
        at = qcols + g * 2 * HD
        gqkv[pl.ds(at, HD), :] = unrot_rows(dk[g] * SCALE, cos_t[...], sin_t[...]).astype(BF)
        gqkv[pl.ds(at + HD, HD), :] = dv[g].astype(BF)
    a_load.wait()
    weight_grad(4, gqkv.at[pl.ds(0, qcols)], ab, False)
    weight_grad(4, gqkv.at[pl.ds(0, qcols)], ab, True)
    weight_grad(5, gqkv.at[pl.ds(qcols, kvcols)], ab, False)
    weight_grad(5, gqkv.at[pl.ds(qcols, kvcols)], ab, True)
    z()
    stage_res = rs_finish(1)
    gb[...] = (mid[...] + stage_res).astype(BF)
    res_copy = pltpu.make_async_copy(gb, res_out, out_sem.at[0])
    res_copy.start()
    for p in range(1, tp):
        signal(cr_rs, (md, flip(me, p)))
    pl.semaphore_wait(cr_rs, tp - 1)
    z()
    qkv_load.wait()
    for p in order:
        gia_into(to_snd(p), p)
        rs_send(2, p)
    gia_into(to_own, 0)
    z(2)
    if hops:
        rs_merge(2, 1)
        rs_merge(2, 2)
    z(3)
    grad_in = rs_finish(2)
    base_a, inv_a = normed(hid[...].astype(F32))
    back, gain_a = norm_back(grad_in, base_a, inv_a, gains[0:1, :])
    hid[...] = (gs[...] + back).astype(BF)
    hid_copy = pltpu.make_async_copy(hid, hid_out, out_sem.at[1])
    hid_copy.start()
    gsum[0:1, :] = gain_a

    stages = []
    bit = 1
    while bit < dp:
        stages.append((flip(md, bit), me))
        bit *= 2
    bit = 1
    while bit < tp:
        stages.append((md, flip(me, bit)))
        bit *= 2
    for n, peer in enumerate(stages):
        c = remote(gsum, gland.at[n], gain_ssem.at[n], gain_rsem.at[n], peer)
        c.start()
        z()
        c.wait()
        gsum[...] = gsum[...] + gland[n]
    gain_copy = pltpu.make_async_copy(gsum.at[pl.ds(0, 8)], gain_out, out_sem.at[2])
    gain_copy.start()

    last = chunks + 3 * lag + 2
    z(last - slot_now[0])
    for c in (res_copy, hid_copy, gain_copy):
        c.wait()
    for c in range(chunks):
        remote(dn_ring.at[0], sums_out.at[1 - core, rows_of(c)], sib_ssem.at[c], sib_rsem.at[c], sibling).wait_recv()

        @pl.when(is_mid)
        def _(c=c):
            part_copy(c, dn_ring, dn_rsem).wait_send()

        @pl.when(not_mid)
        def _(c=c):
            part_copy(c, up_ring, up_rsem).wait_send()

        pair_done(c)


def backward(mesh, cot, cot_all, a, b, q, kt, k, v, lse, mix, f1, f2, act, down, mid, hid, wqkv, wo, wg, wu, wd, gains, segc, segr, cos_t, sin_t):
    tp, dp = mesh.shape["tp"], mesh.shape["dp"]
    block, width = hid.shape
    length = tp * block
    hidden = wg.shape[1]
    heads = wo.shape[0] // HD
    kv_heads = (wqkv.shape[1] - heads * HD) // (2 * HD)
    qcols, kvcols = heads * HD, kv_heads * 2 * HD
    r = hidden // PAIR
    half_rows = (3 * hidden + 2 * qcols + kvcols) // 2
    chunks = half_rows // r
    steps = (dp - 1).bit_length() + (tp - 1).bit_length()
    sds = jax.ShapeDtypeStruct
    outs = [
        sds((block, width), BF),
        sds((block, width), BF),
        sds((2, half_rows, width), BF),
        sds((8, width), F32),
    ]
    dma = pltpu.SemaphoreType.DMA
    reg = pltpu.SemaphoreType.REGULAR
    scratch = [
        pltpu.VMEM((length, width), BF),
        pltpu.VMEM((hidden, length), BF),
        pltpu.VMEM((hidden, width), BF),
        pltpu.VMEM((hidden, length), BF),
        pltpu.VMEM((hidden, length), BF),
        pltpu.VMEM((width, hidden), BF),
        pltpu.VMEM((width, hidden), BF),
        pltpu.VMEM((length, width), BF),
        pltpu.VMEM((tp - 1, width, block), BF),
        pltpu.VMEM((tp - 1, width, block), BF),
        pltpu.VMEM((half_rows, width), BF),
        pltpu.VMEM((PAIR * r, width), BF),
        pltpu.VMEM((RING, r, width), BF),
        pltpu.VMEM((RING, r, width), BF),
        pltpu.VMEM((heads, HD, length), BF),
        pltpu.VMEM((kv_heads, HD, length), BF),
        pltpu.VMEM((kv_heads, length, 128), BF),
        pltpu.VMEM((kv_heads, length, 128), BF),
        pltpu.VMEM((heads, 1, length), F32),
        pltpu.VMEM((qcols, length), BF),
        pltpu.VMEM((heads, HD, length), BF),
        pltpu.VMEM((qcols + kvcols, length), BF),
        pltpu.VMEM((kv_heads, HD, length), F32),
        pltpu.VMEM((kv_heads, HD, length), F32),
        pltpu.VMEM((length, QB), F32),
        pltpu.VMEM((block, width), F32),
        pltpu.VMEM((block, width), BF),
        pltpu.VMEM((block, width), F32),
        pltpu.VMEM((width, block), F32),
        pltpu.VMEM((block, width), BF),
        pltpu.VMEM((qcols, width), BF),
        pltpu.VMEM((width, block), BF),
        pltpu.VMEM((8, width), F32),
        pltpu.VMEM((steps, 8, width), F32),
        dma((4 + 2 * tp + 20,)),
        dma((3,)),
        dma((chunks,)), dma((chunks,)), dma((chunks,)), dma((chunks,)), dma((chunks,)), dma((chunks,)), dma((chunks,)), dma((chunks,)), dma((chunks,)),
        dma((3, tp - 1, 2)), dma((3, tp - 1, 2)),
        dma((2, tp, 2)), dma((2, tp, 2)),
        dma((steps,)), dma((steps,)),
        reg, reg, reg, reg,
    ]
    any_ = pl.BlockSpec(memory_space=pl.ANY)
    vmem = pl.BlockSpec(memory_space=pltpu.VMEM)
    return pl.pallas_call(
        functools.partial(backward_kernel, tp, dp),
        out_shape=outs,
        in_specs=[any_] * 21 + [vmem] * 5,
        out_specs=[any_] * len(outs),
        scratch_shapes=scratch,
        compiler_params=pltpu.CompilerParams(collective_id=1, has_side_effects=True, vmem_limit_bytes=62 * 2**20),
        name="backward",
    )(cot, cot_all, a, b, q, kt, k, v, lse, mix.reshape(qcols, length), f1, f2, act, down, mid, hid, wqkv, wo, wg, wu, wd, gains, segc, segr, cos_t, sin_t)


def finish_kernel(sums, res, hid, gain, res_out, hid_out, query_out, keyval_out, output_out, gate_out, up_out, down_out, gain_out,
                  in_v, nat_v, wide_v, turn_v, query_v, pass_v, in_sem, nat_sem, wide_sem, turn_sem, query_sem, copy_sem):
    width = sums.shape[2]
    passing = [
        pltpu.make_async_copy(res, pass_v.at[0], copy_sem.at[0]),
        pltpu.make_async_copy(hid, pass_v.at[1], copy_sem.at[1]),
    ]
    copies = [
        pltpu.make_async_copy(pass_v.at[0], res_out, copy_sem.at[0]),
        pltpu.make_async_copy(pass_v.at[1], hid_out, copy_sem.at[1]),
    ]
    outs = (down_out, gate_out, up_out, output_out, query_out, keyval_out)
    flat = (True, False, False, True, False, True)
    total = [o.shape[0] if f else o.shape[1] for o, f in zip(outs, flat)]
    tasks, at = [], 0
    for n, rows in enumerate(total):
        hr = rows // 2
        if n == 0:
            for core in (0, 1):
                for side in (0, 1):
                    tasks.append((n, [(core, at + side * (hr // 2), hr // 2)], core * hr, side))
        elif n < 3:
            step = min(256, hr)
            for core in (0, 1):
                for p in range(0, hr, step):
                    tasks.append((n, [(core, at + p, step)], core * hr + p, step))
        else:
            tasks.append((n, [(0, at, hr), (1, at, hr)], 0, rows))
        at += hr
    depth = in_v.shape[0]
    keep = nat_v.shape[0]

    def loads(i):
        _, pieces, _, _ = tasks[i]
        to, out = 0, []
        for j, (core, row, rows) in enumerate(pieces):
            out.append(pltpu.make_async_copy(sums.at[core, pl.ds(row, rows)], in_v.at[i % depth, pl.ds(to, rows)], in_sem.at[i % depth, j]))
            to += rows
        return out

    for i in range(min(depth - 1, len(tasks))):
        for c in loads(i):
            c.start()
    for c in passing:
        c.start()
    nat_busy, turn_busy, wide_busy, tail = {}, {}, {}, []
    nats = turns = wides = 0
    rows_r = total[0] // PAIR
    for i, (n, _, row, rows) in enumerate(tasks):
        if i == 2:
            for p, c in zip(passing, copies):
                p.wait()
                c.start()
        if i + depth - 1 < len(tasks):
            for c in loads(i + depth - 1):
                c.start()
        for c in loads(i):
            c.wait()
        if n == 0:
            slot = wides % 2
            wides += 1
            if slot in wide_busy:
                wide_busy.pop(slot).wait()
            r = rows_r
            for j in range(total[0] // 2 // (2 * r)):
                for k in (0, 1):
                    wide_v[slot, pl.ds((2 * j + k) * r, r), :] = in_v[
                        i % depth, pl.ds(j * r, r), pl.ds(k * (width // 2), width // 2)
                    ].astype(F32)
            c = pltpu.make_async_copy(
                wide_v.at[slot], outs[n].at[pl.ds(row, total[0] // 2), pl.ds(rows * (width // 2), width // 2)], wide_sem.at[slot]
            )
            wide_busy[slot] = c
        elif flat[n]:
            slot = nats % keep
            nats += 1
            if slot in nat_busy:
                nat_busy.pop(slot).wait()
            nat_v[slot, pl.ds(0, rows), :] = in_v[i % depth, pl.ds(0, rows), :].astype(F32)
            c = pltpu.make_async_copy(nat_v.at[slot, pl.ds(0, rows)], outs[n].at[pl.ds(row, rows)], nat_sem.at[slot])
            nat_busy[slot] = c
        elif n < 3:
            slot = turns % keep
            turns += 1
            if slot in turn_busy:
                turn_busy.pop(slot).wait()
            turn_v[slot] = in_v[i % depth, pl.ds(0, rows), :].T.astype(F32)
            c = pltpu.make_async_copy(turn_v.at[slot], outs[n].at[:, pl.ds(row, rows)], turn_sem.at[slot])
            turn_busy[slot] = c
        else:
            query_v[...] = in_v[i % depth, pl.ds(0, rows), :].T.astype(F32)
            c = pltpu.make_async_copy(query_v, outs[n], query_sem)
            tail.append(c)
        c.start()
    gain_out[...] = gain[0:2, :]
    for c in [*nat_busy.values(), *turn_busy.values(), *wide_busy.values(), *tail, *copies]:
        c.wait()


def finish(sums, res, hid, gain, hidden, qcols, kvcols):
    width = sums.shape[2]
    sds = jax.ShapeDtypeStruct
    outs = [
        sds(res.shape, BF), sds(hid.shape, BF),
        sds((width, qcols), F32), sds((kvcols, width), F32), sds((qcols, width), F32),
        sds((width, hidden), F32), sds((width, hidden), F32), sds((hidden, width), F32),
        sds((2, width), F32),
    ]
    dma = pltpu.SemaphoreType.DMA
    any_ = pl.BlockSpec(memory_space=pl.ANY)
    vmem = pl.BlockSpec(memory_space=pltpu.VMEM)
    tall = max(min(256, hidden // 2), qcols, kvcols)
    step = min(256, hidden // 2)
    return pl.pallas_call(
        finish_kernel,
        out_shape=outs,
        in_specs=[any_] * 3 + [vmem],
        out_specs=[any_] * 8 + [vmem],
        scratch_shapes=[
            pltpu.VMEM((4, tall, width), BF),
            pltpu.VMEM((3, tall, width), F32),
            pltpu.VMEM((2, hidden // 2, width // 2), F32),
            pltpu.VMEM((3, width, step), F32),
            pltpu.VMEM((width, qcols), F32),
            pltpu.VMEM((2, *res.shape), BF),
            dma((4, 2)), dma((3,)), dma((2,)), dma((3,)), dma, dma((2,)),
        ],
        compiler_params=pltpu.CompilerParams(vmem_limit_bytes=62 * 2**20),
        name="finish",
    )(sums, res, hid, gain)


def local(mesh, hidden, segments, cotangent, w_query, w_keyval, w_output, w_gate, w_up, w_down, gains):
    width = hidden.shape[2]
    hid, cot, gain = hidden[0], cotangent[0], gains[0]
    wq, wo, wg, wu, wd = w_query[0], w_output[0], w_gate[0], w_up[0], w_down[0]
    wkv_t = w_keyval[0].transpose(1, 2, 0).reshape(-1, width)
    inverse = ROPE_BASE ** (-(jnp.arange(HALF, dtype=F32) * 2.0) / HD)
    wqkv, segc, cos_t, sin_t, a, b, cot_all, q, kt, k, v, lse, mix, f1, f2, act, down, mid = forward(
        mesh, hid, cot, wq, wkv_t, wo, wg, wu, wd, gain, segments, inverse[:, None]
    )
    result, grad_hidden, sums, gain_sum = backward(
        mesh, cot, cot_all, a, b, q, kt, k, v, lse, mix, f1, f2, act, down, mid, hid,
        wqkv, wo, wg, wu, wd, gain, segc, segments, cos_t, sin_t,
    )
    result, grad_hidden, query, keyval, output, gate, up, down, gain_sum = finish(
        sums, result, grad_hidden, gain_sum, wd.shape[0], wo.shape[0], wkv_t.shape[0]
    )
    keyval = keyval.reshape(*w_keyval.shape[2:], width).transpose(2, 0, 1)
    return tuple(x[None] for x in (result, grad_hidden, query, keyval, output, gate, up, down, gain_sum))


def solution(mesh):
    split = P("dp", "tp", None)
    columns, rows = P(None, None, "tp"), P(None, "tp", None)
    heads = P(None, None, "tp", None)
    return jax.shard_map(
        functools.partial(local, mesh),
        mesh=mesh,
        in_specs=(split, P("dp", None), split, columns, heads, rows, columns, columns, rows, P()),
        out_specs=(split, split, columns, heads, rows, columns, columns, rows, P()),
        check_vma=False,
    )
```

```python
import functools
import jax
import jax.numpy as jnp
from jax import lax
from jax.experimental import pallas as pl
from jax.experimental.pallas import tpu as pltpu
from jax.sharding import PartitionSpec as P

MESH = pl.DeviceIdType.MESH
HD = 96
HALF = HD // 2
EPS = 1e-05
ROPE_BASE = 100000.0
SCALE = HD ** (-0.5)
BF = jnp.bfloat16
F32 = jnp.float32
QB = 256


def flip(index, mask):
    out = index
    bit = 1
    while bit <= mask:
        if mask & bit:
            out = out + bit - 2 * bit * ((index // bit) % 2)
        bit *= 2
    return out


def nn(x, y):
    return lax.dot_general(x, y, (((1,), (0,)), ((), ())), preferred_element_type=F32)


def nt(x, y):
    return lax.dot_general(x, y, (((1,), (1,)), ((), ())), preferred_element_type=F32)


def normed(stream):
    inv = lax.rsqrt(jnp.mean(stream * stream, axis=-1, keepdims=True) + EPS)
    return stream * inv, inv


def rot_rows(x, cos, sin):
    x1, x2 = x[:HALF], x[HALF:]
    return jnp.concatenate([x1 * cos - x2 * sin, x2 * cos + x1 * sin], axis=0)


def forward_kernel(
    tp, dp,
    hid, cot, wq, wkv_t, wo, wg, wu, wd, gains, segr, inverse,
    wqkv_out, seg_out, cos_out, sin_out, a_out, b_out, cot_all, q_out, kt_out, k_out, v_out, lse_out, mix_out, f1_out, f2_out, act_out, wdt_out, mid_out,
    hid_all, mixed_all, wo_all, wq_in, w_in, w_st, wqkv_t, wg_t, wu_t, wd_n, wd_t,
    a_v, b_v, q_t, k_t, k_n, v_n, v_t, mix_t, bias, lse, f1, f2, act_t, mid_v, mid_w, segc, cos_t, sin_t,
    load_sem, out_sem, hid_ssem, hid_rsem, cot_ssem, cot_rsem, mix_ssem, mix_rsem, wo_ssem, wo_rsem,
):
    me, md = lax.axis_index("tp"), lax.axis_index("dp")
    nz = dp // 2
    core, mz = md % 2, md // 2
    block, width = hid.shape
    length = tp * block
    hidden = wg.shape[1]
    heads, kv_heads = q_t.shape[0], k_t.shape[0]
    qcols, kvcols = heads * HD, kv_heads * 2 * HD
    pieces = length // QB
    hops = tp == 4
    rows_o = qcols // dp
    spread = qcols % (16 * dp) == 0
    half = block // 2

    loads = [
        pltpu.make_async_copy(wq, wq_in, load_sem.at[0]),
        pltpu.make_async_copy(wd, wd_n, load_sem.at[1]),
        pltpu.make_async_copy(hid, hid_all.at[me], load_sem.at[2]),
        pltpu.make_async_copy(wg, w_st, load_sem.at[3]),
        pltpu.make_async_copy(wo, wo_all.at[me], load_sem.at[4]),
        pltpu.make_async_copy(wkv_t, wqkv_t.at[pl.ds(qcols, kvcols)], load_sem.at[5]),
    ]
    for c in loads:
        c.start()

    barrier = pltpu.get_barrier_semaphore()
    peers = [(md, flip(me, p)) for p in range(1, tp)]
    if spread:
        peers += [(flip(md, 2 * z), me) for z in range(1, nz)] + [(flip(md, 1), me)]
    for peer in peers:
        pl.semaphore_signal(barrier, inc=1, device_id=peer, device_id_type=MESH)
    pl.semaphore_wait(barrier, len(peers))

    def remote(src, dst, ssem, rsem, peer):
        return pltpu.make_async_remote_copy(src, dst, ssem, rsem, device_id=peer, device_id_type=MESH)

    def gather_first(src, dst, ssem, rsem, cols=pl.ds(0, width)):
        out = []
        for p in range(1, tp):
            if hops and p == 3:
                continue
            for part in (0, 1) if p == 1 else (1, 0):
                rows = pl.ds(part * half, half)
                out.append(remote(src.at[rows, cols], dst.at[me, rows], ssem.at[p, part], rsem.at[p, part], (md, flip(me, p))))
        return out

    def arrived(dst, ssem, rsem, p, part):
        rows = pl.ds(part * half, half)
        slot = dst.at[flip(me, p), rows]
        return remote(slot, slot, ssem.at[p, part], rsem.at[p, part], (md, flip(me, p)))

    def handed(dst, ssem, rsem, part):
        rows = pl.ds(part * half, half)
        came, goes = (1, 2) if part == 0 else (2, 1)
        slot = dst.at[flip(me, came), rows]
        return remote(slot, slot, ssem.at[3, part], rsem.at[3, part], (md, flip(me, goes)))

    hid_first = gather_first(hid, hid_all, hid_ssem, hid_rsem)
    cot_first = gather_first(cot, cot_all, cot_ssem, cot_rsem, pl.ds(0, width // 2))

    piece = pl.ds((core * nz + mz) * rows_o, rows_o) if spread else pl.ds(0, qcols)
    wo_tp = [
        remote(wo.at[piece], wo_all.at[me, piece], wo_ssem.at[0, p], wo_rsem.at[0, p], (md, flip(me, p)))
        for p in range(1, tp)
    ]
    for c in wo_tp:
        c.start()
    for c in hid_first:
        c.start()
    wo_z, wo_core = [], []
    if spread:
        for z in range(1, nz):
            for p in range(1, tp):
                slot = wo_all.at[flip(me, p), piece]
                wo_z.append(remote(slot, slot, wo_ssem.at[z, p], wo_rsem.at[z, p], (flip(md, 2 * z), me)))
        both = pl.ds(core * nz * rows_o, nz * rows_o)
        for p in range(1, tp):
            slot = wo_all.at[flip(me, p), both]
            wo_core.append(remote(slot, slot, wo_ssem.at[nz, p], wo_rsem.at[nz, p], (flip(md, 1), me)))

    def turn(dst, src, step=256):
        rows = src.shape[0]
        for r in range(0, rows, step):
            dst[:, pl.ds(r, step)] = src[pl.ds(r, step), :].T

    def project(src):
        off = pl.multiple_of(src * block, block)
        cols = pl.ds(off, block)
        base, _ = normed(hid_all[src].astype(F32))
        a = (base * gains[0:1, :]).astype(BF)
        a_v[cols, :] = a
        cos, sin = cos_t[:, cols], sin_t[:, cols]
        qk = nt(wqkv_t[...], a)
        for h in range(heads):
            q_t[h, :, cols] = rot_rows(qk[h * HD : (h + 1) * HD], cos, sin).astype(BF)
        pad = jnp.zeros((128 - HD, block), F32)
        for g in range(kv_heads):
            at = qcols + g * 2 * HD
            kr = rot_rows(qk[at : at + HD], cos, sin)
            vr = qk[at + HD : at + 2 * HD]
            k_t[g, :, cols] = kr.astype(BF)
            v_t[g, :, cols] = vr.astype(BF)
            k_n[g, cols, :] = jnp.concatenate([kr, pad], axis=0).T.astype(BF)
            v_n[g, cols, :] = jnp.concatenate([vr, pad], axis=0).T.astype(BF)

    loads[0].wait()
    turn(wqkv_t.at[pl.ds(0, qcols)], wq_in)
    loads[3].wait()
    turn(wg_t, w_st)
    wu_load = pltpu.make_async_copy(wu, w_st, load_sem.at[3])
    wu_load.start()
    for c in wo_tp:
        c.wait()
    for c in wo_z:
        c.start()
    segc[...] = jnp.broadcast_to(segr[...].astype(F32), (128, length)).T[:, :8].astype(jnp.int32)
    start = jnp.sum((segc[:, 0:1] < segr[...]).astype(F32), axis=0, keepdims=True)
    place = lax.broadcasted_iota(jnp.int32, (1, length), 1).astype(F32) - start
    angles = inverse[...] * place
    cos_t[...] = jnp.cos(angles)
    sin_t[...] = jnp.sin(angles)
    w_in[:, 0:qcols] = wq_in[...]
    loads[5].wait()
    w_in[:, qcols : qcols + kvcols] = wqkv_t[qcols : qcols + kvcols, :].T
    loads[2].wait()
    project(me)
    wu_load.wait()
    turn(wu_t, w_st)
    loads[1].wait()
    turn(wd_t, wd_n)
    loads[4].wait()

    if hops:
        for p, part in ((1, 0), (2, 1)):
            arrived(hid_all, hid_ssem, hid_rsem, p, part).wait_recv()
            handed(hid_all, hid_ssem, hid_rsem, part).start()
        for p, part in ((1, 1), (2, 0)):
            arrived(hid_all, hid_ssem, hid_rsem, p, part).wait_recv()
            project(flip(me, p))
        for part in (0, 1):
            rows = pl.ds(part * half, half)
            slot = hid_all.at[flip(me, 3), rows]
            remote(slot, slot, hid_ssem.at[3, part], hid_rsem.at[3, part], (md, flip(me, 2))).wait_recv()
        project(flip(me, 3))
    else:
        for p in range(1, tp):
            for part in (0, 1):
                arrived(hid_all, hid_ssem, hid_rsem, p, part).wait_recv()
            project(flip(me, p))

    outs = []

    def put(src, dst):
        c = pltpu.make_async_copy(src, dst, out_sem.at[len(outs)])
        c.start()
        outs.append(c)

    for src, dst in ((w_in, wqkv_out), (wd_t, wdt_out), (segc, seg_out), (cos_t, cos_out), (sin_t, sin_out), (a_v, a_out), (q_t, q_out), (k_t, kt_out), (k_n, k_out), (v_n, v_out)):
        put(src, dst)

    def mix_slot(who, i):
        return mixed_all.at[who, pl.ds(i * QB, QB)]

    def mix_copy(i, p):
        return remote(mix_slot(me, i), mix_slot(me, i), mix_ssem.at[p, i], mix_rsem.at[p, i], (md, flip(me, p)))

    def mix_arrived(i, p):
        slot = mix_slot(flip(me, p), i)
        return remote(slot, slot, mix_ssem.at[p, i], mix_rsem.at[p, i], (md, flip(me, p)))

    def mix_handed(i):
        came, goes = (1, 2) if i % 2 == 0 else (2, 1)
        slot = mix_slot(flip(me, came), i)
        return remote(slot, slot, mix_ssem.at[3, i], mix_rsem.at[3, i], (md, flip(me, goes)))

    def hand_on(i):
        if not hops:
            return
        mix_arrived(i, 1 if i % 2 == 0 else 2).wait_recv()
        mix_handed(i).start()

    for i in range(pieces):
        if i == pieces - 1:
            for n in range(pieces - 3):
                hand_on(n)
        reach = (i + 1) * QB
        cols = pl.ds(i * QB, QB)
        same = segc[pl.ds(0, reach), 0:1] == segr[:, cols]
        later = lax.broadcasted_iota(jnp.int32, (reach, QB), 0) <= lax.broadcasted_iota(jnp.int32, (reach, QB), 1) + i * QB
        bias[pl.ds(0, reach), :] = jnp.where(same & later, 0.0, -1e30)

        def head(h, _, reach=reach, cols=cols):
            g = h // (heads // kv_heads)
            s = nn(k_n[g, pl.ds(0, reach), :][:, :HD], q_t[h, :, cols]) * SCALE + bias[pl.ds(0, reach), :]
            top = jnp.max(s, axis=0, keepdims=True)
            e = jnp.exp(s - top)
            total = jnp.sum(e, axis=0, keepdims=True)
            p = (e * (1.0 / total)).astype(BF)
            mix_t[h, :, cols] = nn(v_t[g, :, pl.ds(0, reach)], p).astype(BF)
            lse[h, :, cols] = top + jnp.log(total)
            return 0

        lax.fori_loop(0, heads, head, 0)
        mixed_all[me, cols, :] = mix_t[:, :, cols].reshape(qcols, QB).T
        for p in range(1, tp):
            if not (hops and p == 3):
                mix_copy(i, p).start()
    put(lse, lse_out)
    put(mix_t, mix_out)
    if pieces >= 3:
        hand_on(pieces - 3)
    for c in wo_z:
        c.wait()
    for c in wo_core:
        c.start()

    def middle(i):
        rows = pl.ds(i * QB, QB)
        for p in range(1, tp):
            if hops and p == 3:
                slot = mix_slot(flip(me, 3), i)
                remote(slot, slot, mix_ssem.at[3, i], mix_rsem.at[3, i], (md, flip(me, 1))).wait_recv()
            elif not (hops and p == (1 if i % 2 == 0 else 2)):
                mix_arrived(i, p).wait_recv()
        per = QB // block if QB >= block else 1
        mixed = jnp.concatenate([mixed_all[s, rows, :] for s in range(tp)], axis=1)
        for d in range(0, width, 512):
            cols = pl.ds(d, 512)
            stream = jnp.concatenate([hid_all[i * per + n, :, cols] for n in range(per)], axis=0).astype(F32)
            mid_w[:, cols] = stream + nn(mixed, wo_all[:, :, cols].reshape(tp * qcols, 512))
        total = mid_w[...]
        base, _ = normed(total)
        b_v[rows, :] = (base * gains[1:2, :]).astype(BF)
        for n in range(per):
            @pl.when(me == i * per + n)
            def _(n=n):
                mid_v[...] = total[n * block : (n + 1) * block]

    def feed(i):
        rows = pl.ds(i * QB, QB)
        b = b_v[rows, :]
        step = 256
        for f in range(0, hidden, step):
            units = pl.ds(f, step)
            gate = nt(wg_t[units, :], b)
            up = nt(wu_t[units, :], b)
            sig = jax.nn.sigmoid(gate)
            silu = gate * sig
            f1[units, rows] = (up * sig * (1.0 + gate * (1.0 - sig))).astype(BF)
            f2[units, rows] = silu.astype(BF)
            act_t[units, rows] = (silu * up).astype(BF)
        put(b_v.at[rows], b_out.at[rows])
        for src, dst in ((f1, f1_out), (f2, f2_out), (act_t, act_out)):
            put(src.at[:, rows], dst.at[:, rows])

    if pieces >= 2:
        hand_on(pieces - 2)
    for c in wo_core:
        c.wait()
    for i in range(pieces):
        if i == min(1, pieces - 1):
            hand_on(pieces - 1)
            for c in cot_first:
                c.start()
        middle(i)
        feed(i)
    put(mid_v, mid_out)

    if hops:
        for p, part in ((1, 0), (2, 1)):
            arrived(cot_all, cot_ssem, cot_rsem, p, part).wait_recv()
            handed(cot_all, cot_ssem, cot_rsem, part).start()
        for p, part in ((1, 1), (2, 0)):
            arrived(cot_all, cot_ssem, cot_rsem, p, part).wait_recv()
        for part in (0, 1):
            rows = pl.ds(part * half, half)
            slot = cot_all.at[flip(me, 3), rows]
            remote(slot, slot, cot_ssem.at[3, part], cot_rsem.at[3, part], (md, flip(me, 2))).wait_recv()
    else:
        for p in range(1, tp):
            for part in (0, 1):
                arrived(cot_all, cot_ssem, cot_rsem, p, part).wait_recv()
    for c in hid_first + cot_first:
        c.wait_send()
    if hops:
        for part in (0, 1):
            handed(hid_all, hid_ssem, hid_rsem, part).wait_send()
            handed(cot_all, cot_ssem, cot_rsem, part).wait_send()
        for i in range(pieces):
            mix_handed(i).wait_send()
    for n in range(pieces):
        for p in range(1, tp):
            if not (hops and p == 3):
                mix_copy(n, p).wait_send()
    for c in outs:
        c.wait()


def forward(mesh, hid, cot, wq, wkv_t, wo, wg, wu, wd, gains, segr, inverse):
    tp, dp = mesh.shape["tp"], mesh.shape["dp"]
    block, width = hid.shape
    length = tp * block
    hidden = wg.shape[1]
    heads = wo.shape[0] // HD
    kv_heads = wkv_t.shape[0] // (2 * HD)
    nz = dp // 2
    pieces = length // QB
    sds = jax.ShapeDtypeStruct
    outs = [
        sds((width, (heads + 2 * kv_heads) * HD), BF),
        sds((length, 8), jnp.int32),
        sds((HALF, length), F32),
        sds((HALF, length), F32),
        sds((length, width), BF),
        sds((length, width), BF),
        sds((tp, block, width // 2), BF),
        sds((heads, HD, length), BF),
        sds((kv_heads, HD, length), BF),
        sds((kv_heads, length, 128), BF),
        sds((kv_heads, length, 128), BF),
        sds((heads, 1, length), F32),
        sds((heads, HD, length), BF),
        sds((hidden, length), BF),
        sds((hidden, length), BF),
        sds((hidden, length), BF),
        sds((width, hidden), BF),
        sds((block, width), F32),
    ]
    dma = pltpu.SemaphoreType.DMA
    scratch = [
        pltpu.VMEM((tp, block, width), BF),
        pltpu.VMEM((tp, length, heads * HD), BF),
        pltpu.VMEM((tp, heads * HD, width), BF),
        pltpu.VMEM((width, heads * HD), BF),
        pltpu.VMEM((width, heads * HD + kv_heads * 2 * HD), BF),
        pltpu.VMEM((width, hidden), BF),
        pltpu.VMEM((heads * HD + kv_heads * 2 * HD, width), BF),
        pltpu.VMEM((hidden, width), BF),
        pltpu.VMEM((hidden, width), BF),
        pltpu.VMEM((hidden, width), BF),
        pltpu.VMEM((width, hidden), BF),
        pltpu.VMEM((length, width), BF),
        pltpu.VMEM((length, width), BF),
        pltpu.VMEM((heads, HD, length), BF),
        pltpu.VMEM((kv_heads, HD, length), BF),
        pltpu.VMEM((kv_heads, length, 128), BF),
        pltpu.VMEM((kv_heads, length, 128), BF),
        pltpu.VMEM((kv_heads, HD, length), BF),
        pltpu.VMEM((heads, HD, length), BF),
        pltpu.VMEM((length, QB), F32),
        pltpu.VMEM((heads, 1, length), F32),
        pltpu.VMEM((hidden, length), BF),
        pltpu.VMEM((hidden, length), BF),
        pltpu.VMEM((hidden, length), BF),
        pltpu.VMEM((block, width), F32),
        pltpu.VMEM((QB, width), F32),
        pltpu.VMEM((length, 8), jnp.int32),
        pltpu.VMEM((HALF, length), F32),
        pltpu.VMEM((HALF, length), F32),
        dma((6,)),
        dma((13 + 4 * pieces,)),
        dma((tp, 2)),
        dma((tp, 2)),
        dma((tp, 2)),
        dma((tp, 2)),
        dma((tp, pieces)),
        dma((tp, pieces)),
        dma((nz + 1, tp)),
        dma((nz + 1, tp)),
    ]
    any_ = pl.BlockSpec(memory_space=pl.ANY)
    vmem = pl.BlockSpec(memory_space=pltpu.VMEM)
    return pl.pallas_call(
        functools.partial(forward_kernel, tp, dp),
        out_shape=outs,
        in_specs=[any_] * 8 + [vmem] * 3,
        out_specs=[any_] * len(outs),
        scratch_shapes=scratch,
        compiler_params=pltpu.CompilerParams(collective_id=0, has_side_effects=True, vmem_limit_bytes=62 * 2**20),
        name="forward",
    )(hid, cot, wq, wkv_t, wo, wg, wu, wd, gains, segr, inverse)


RING = 8
AHEAD = 1
FINE = 2
PAIR = 16


def unrot_rows(d, cos, sin):
    d1, d2 = d[:HALF], d[HALF:]
    return jnp.concatenate([d1 * cos + d2 * sin, d2 * cos - d1 * sin], axis=0)


def norm_back(grad, base, inv, gain):
    e = grad * gain
    back = inv * (e - base * jnp.mean(e * base, axis=-1, keepdims=True))
    return back, jnp.sum(grad * base, axis=0, keepdims=True)


def backward_kernel(
    tp, dp,
    cot, cot_all, a_in, b_in, q_in, kt_in, k_in, v_in, lse_in, mix_in, f1_in, f2_in, act_in, wdt, mid_in, hid_in,
    wqkv, wo, wg, wu, wd, gains, segc, segr, cos_t, sin_t,
    res_out, hid_out, sums_out, gain_out,
    tok, act, wd_v, f1, f2, wg_v, wu_v, ab, snd, rcv, acc, pair, up_ring, dn_ring,
    q_t, k_t, k_n, v_n, lse, mix, gm_t, gqkv, dk, dv, bias, mid, hid, gs, own, gb, wo_v, gsum, gland,
    load_sem, out_sem, pair_ssem, pair_rsem, part_ssem, up_rsem, dn_rsem, tot_ssem, sib_ssem, sib_rsem, fin_sem,
    rs_ssem, rs_rsem, tok_ssem, tok_rsem, gain_ssem, gain_rsem, cr_pair, cr_dn, cr_up, cr_rs,
):
    me, md = lax.axis_index("tp"), lax.axis_index("dp")
    nz = dp // 2
    core, mz = md % 2, md // 2
    length, width = tok.shape
    block = length // tp
    half = block // 2
    hidden = act.shape[0]
    heads, kv_heads = q_t.shape[0], k_t.shape[0]
    group = heads // kv_heads
    qcols, kvcols = heads * HD, kv_heads * 2 * HD
    hops = tp == 4
    r = hidden // PAIR
    parts = [hidden, hidden, hidden, qcols, qcols, kvcols]
    sizes = [r] * (sum(parts[:5]) // 2 // r) + [r // FINE] * (parts[5] // 2 // (r // FINE))
    chunks = len(sizes)
    starts = [sum(sizes[:c]) for c in range(chunks)]
    own_rows = pl.ds(pl.multiple_of(me * block, block), block)

    def load(n, src, dst):
        return pltpu.make_async_copy(src, dst, load_sem.at[n])

    early = [load(0, act_in, act)] + [
        load(
            1 + p,
            cot_all.at[flip(me, p)] if p else cot,
            tok.at[pl.ds(pl.multiple_of(flip(me, p) * block, block), block), pl.ds(0, width // 2 if p else width)],
        )
        for p in range(tp)
    ]
    n0 = 1 + tp
    then = [load(n0, wd.at[pl.ds(hidden // 2, hidden // 2)], wd_v.at[pl.ds(hidden // 2, hidden // 2)]), load(n0 + 1, f1_in, f1), load(n0 + 2, f2_in, f2)]
    late = [
        load(n0 + 3 + n, s, d)
        for n, (s, d) in enumerate(
            (
                (wg, wg_v), (wu, wu_v), (b_in, ab), (q_in, q_t), (kt_in, k_t), (k_in, k_n), (v_in, v_n), (lse_in, lse),
                (mix_in, mix), (mid_in, mid), (hid_in, hid), (wo, wo_v),
            )
        )
    ]
    n1 = n0 + 3 + len(late)
    for c in early:
        c.start()

    barrier = pltpu.get_barrier_semaphore()
    peers = [(md, flip(me, p)) for p in range(1, tp)] + [(flip(md, p), me) for p in range(1, dp)]
    for peer in peers:
        pl.semaphore_signal(barrier, inc=1, device_id=peer, device_id_type=MESH)
    pl.semaphore_wait(barrier, len(peers))

    def remote(src, dst, ssem, rsem, peer):
        return pltpu.make_async_remote_copy(src, dst, ssem, rsem, device_id=peer, device_id_type=MESH)

    def signal(sem, peer):
        pl.semaphore_signal(sem, inc=1, device_id=peer, device_id_type=MESH)

    left = mz < nz // 2
    step_in = jnp.where(left, 1, -1)
    is_mid = (mz == nz // 2 - 1) | (mz == nz // 2)
    has_up = (mz != 0) & (mz != nz - 1)
    not_mid, no_up = jnp.logical_not(is_mid), jnp.logical_not(has_up)
    sibling = (md + 1 - 2 * core, me)
    down_dev = (md + 2 * step_in, me)
    up_dev = (md - 2 * step_in, me)

    def rows_of(c):
        return pl.ds(starts[c], sizes[c])

    def pair_rows(c):
        return pl.ds((c % PAIR) * r, sizes[c])

    def in_ring(ring, c):
        return ring.at[c % RING, pl.ds(0, sizes[c])]

    def pair_copy(c):
        slot = pair_rows(c)
        return remote(wd_v.at[slot], pair.at[slot], pair_ssem.at[c], pair_rsem.at[c], sibling)

    def part_copy(c, dst, rsem):
        return remote(acc.at[rows_of(c)], in_ring(dst, c), part_ssem.at[c], rsem.at[c], down_dev)

    def total_copy(c):
        return remote(in_ring(dn_ring, c), in_ring(dn_ring, c), tot_ssem.at[c], dn_rsem.at[c], up_dev)

    def sib_copy(c):
        return remote(in_ring(dn_ring, c), sums_out.at[core, rows_of(c)], sib_ssem.at[c], sib_rsem.at[c], sibling)

    def fin_copy(c):
        return pltpu.make_async_copy(in_ring(dn_ring, c), sums_out.at[core, rows_of(c)], fin_sem.at[c])

    def gather_part(c):
        pair_copy(c).wait_recv()
        total = acc[rows_of(c), :].astype(F32) + pair[pair_rows(c), :].astype(F32)
        acc[rows_of(c), :] = total.astype(BF)

        @pl.when(has_up)
        def _():
            remote(in_ring(up_ring, c), in_ring(up_ring, c), part_ssem.at[c], up_rsem.at[c], up_dev).wait_recv()
            acc[rows_of(c), :] = (acc[rows_of(c), :].astype(F32) + up_ring[c % RING, 0 : sizes[c]].astype(F32)).astype(BF)
            if c + RING < chunks:
                signal(cr_dn, up_dev)

        if c + PAIR < chunks:
            signal(cr_pair, sibling)
        if c >= RING:
            pl.semaphore_wait(cr_dn, 1)

        @pl.when(is_mid)
        def _():
            part_copy(c, dn_ring, dn_rsem).start()

        @pl.when(not_mid)
        def _():
            part_copy(c, up_ring, up_rsem).start()

    def spread_total(c):
        remote(in_ring(dn_ring, c), in_ring(dn_ring, c), tot_ssem.at[c], dn_rsem.at[c], down_dev).wait_recv()

        @pl.when(is_mid)
        def _():
            dn_ring[c % RING, 0 : sizes[c]] = (acc[rows_of(c), :].astype(F32) + dn_ring[c % RING, 0 : sizes[c]].astype(F32)).astype(BF)

        @pl.when(has_up)
        def _():
            if c >= RING:
                pl.semaphore_wait(cr_up, 1)
            total_copy(c).start()

        sib_copy(c).start()
        fin_copy(c).start()

    def retire(c):
        @pl.when(has_up)
        def _():
            total_copy(c).wait_send()

        sib_copy(c).wait_send()
        fin_copy(c).wait()
        if c + RING < chunks:

            @pl.when(is_mid)
            def _():
                signal(cr_dn, down_dev)

            @pl.when(not_mid)
            def _():
                signal(cr_up, down_dev)

    slot_now = [0]
    ready, given = set(), set()
    lag = 2

    def when_chunk(cond, fn, c):
        if 0 <= c < chunks:

            @pl.when(cond)
            def _():
                fn(c)

    def z(count=1):
        for _ in range(count):
            k = slot_now[0]
            slot_now[0] += 1
            assert set(range(min(chunks, k + AHEAD + 1))) <= ready & given
            if k == 0:
                for c in range(AHEAD):
                    when_chunk(no_up, gather_part, c)
            when_chunk(no_up, gather_part, k + AHEAD)
            when_chunk(has_up, gather_part, k - lag)
            when_chunk(is_mid, retire, k - 2 * lag - 2)
            when_chunk(not_mid, retire, k - 3 * lag - 2)
            when_chunk(is_mid, spread_total, k - 2 * lag)
            when_chunk(not_mid, spread_total, k - 3 * lag)

    sent = set()

    def pair_done(c):
        if c not in sent:
            sent.add(c)
            pair_copy(c).wait_send()

    def down_grad(side, mine, only=None):
        hr = parts[0] // 2
        pr = min(256, hr)
        which = core if mine else 1 - core
        cols = pl.ds(side * (width // 2), width // 2)
        for p in range(hr // pr) if only is None else (only,):
            value = nn(act[pl.ds(pl.multiple_of(which * hr + p * pr, 16), pr), :], tok[:, cols]).astype(BF)
            for j in range(pr // (2 * r)):
                c = side * (hr // (2 * r)) + p * (pr // (2 * r)) + j
                packed = jnp.concatenate([value[2 * r * j : 2 * r * j + r], value[2 * r * j + r : 2 * r * (j + 1)]], axis=1)
                (ready if mine else given).add(c)
                if mine:
                    acc[rows_of(c), :] = packed
                else:
                    wd_v[rows_of(c), :] = packed
                    pair_copy(c).start()

    def weight_grad(n, lhs, rhs, mine):
        hr = parts[n] // 2
        pr = min(256, hr)
        which = core if mine else 1 - core
        for p in range(hr // pr):
            value = nn(lhs[pl.ds(pl.multiple_of(which * hr + p * pr, 16), pr), :], rhs[...]).astype(BF)
            begin = sum(parts[:n]) // 2 + p * pr
            held = [c for c in range(chunks) if begin <= starts[c] < begin + pr]
            (ready if mine else given).update(held)
            assert mine or held[-1] - PAIR < slot_now[0] - lag
            if mine:
                acc[pl.ds(begin, pr), :] = value
                continue
            for c in held:
                if c >= PAIR:
                    pair_done(c - PAIR)
                    pl.semaphore_wait(cr_pair, 1)
                wd_v[pair_rows(c), :] = value[starts[c] - begin : starts[c] - begin + sizes[c]]
                pair_copy(c).start()

    direct = [p for p in range(1, tp) if not (hops and p == 3)]
    columns = (pl.ds(width // 2, width // 2), pl.ds(0, width))
    sources = (cot, gb)

    def tok_rows(u, p, part):
        return tok.at[pl.ds(pl.multiple_of(flip(me, p) * block + part * half, half), half), columns[u]]

    def tok_copy(u, p, part):
        src = sources[u].at[pl.ds(part * half, half), columns[u]]
        return remote(src, tok_rows(u, 0, part), tok_ssem.at[u, p, part], tok_rsem.at[u, p, part], (md, flip(me, p)))

    def tok_arrived(u, p, part):
        return remote(tok_rows(u, p, part), tok_rows(u, p, part), tok_ssem.at[u, p, part], tok_rsem.at[u, p, part], (md, flip(me, p)))

    def tok_handed(u, part):
        came, goes = (1, 2) if part == 0 else (2, 1)
        return remote(
            tok_rows(u, came, part), tok_rows(u, came, part), tok_ssem.at[u, 3, part], tok_rsem.at[u, 3, part], (md, flip(me, goes))
        )

    def tok_start(u):
        for p in direct:
            for part in (0, 1) if p == 1 else (1, 0):
                tok_copy(u, p, part).start()

    def tok_hand_on(u):
        if hops:
            for part in (0, 1):
                tok_arrived(u, 1 if part == 0 else 2, part).wait_recv()
                tok_handed(u, part).start()
            for part in (0, 1):
                tok_arrived(u, 2 if part == 0 else 1, part).wait_recv()

    def tok_finish(u):
        for p in range(1, tp):
            if hops and p != 3:
                continue
            for part in (0, 1):
                tok_arrived(u, p, part).wait_recv()
        for p in direct:
            for part in (0, 1):
                tok_copy(u, p, part).wait_send()
        if hops:
            for part in (0, 1):
                tok_handed(u, part).wait_send()

    first_half, second_half = pl.ds(0, width // 2), pl.ds(width // 2, width // 2)
    halves = (first_half, second_half)

    def rs_copy(u, slot, part, p, ahead=False):
        return remote(
            snd.at[slot, halves[part]], rcv.at[slot, halves[part]], rs_ssem.at[u, slot, part], rs_rsem.at[u, slot, part], (md, flip(me, p))
        )

    def rs_send(u, p):
        if hops and p == 3:
            rs_copy(u, 2, 0, 1).start()
            rs_copy(u, 2, 1, 2).start()
        elif hops:
            rs_copy(u, p - 1, p - 1, p).start()
        else:
            for part in (0, 1):
                rs_copy(u, p - 1, part, p).start()

    def rs_merge(u, p):
        if not hops:
            return
        part = 2 - p
        rs_copy(u, 2, part, 3 - p).wait_recv()
        h = halves[part]
        snd[p - 1, h, :] = (snd[p - 1, h, :].astype(F32) + rcv[2, h, :].astype(F32)).astype(BF)
        rs_copy(u, p - 1, part, p).start()

    def rs_finish(u):
        for p in range(1, tp):
            if hops and p == 3:
                continue
            for part in (0, 1):
                rs_copy(u, p - 1, part, p).wait_recv()
        for p in range(1, tp):
            for part in (0, 1):
                rs_copy(u, p - 1, part, (1 if part == 0 else 2) if hops and p == 3 else p).wait_send()
        total = own[...]
        for p in range(1, tp):
            if not (hops and p == 3):
                total = total + rcv[p - 1].astype(F32)
        return total.T

    order = range(tp - 1, 0, -1) if not hops else (3, 1, 2)

    def gib_into(put, p):
        cols = pl.ds(pl.multiple_of(flip(me, p) * block, block), block)
        for d in range(0, width, 512):
            rows = pl.ds(d, 512)
            put(rows, nn(wg_v[rows, :], f1[:, cols]) + nn(wu_v[rows, :], f2[:, cols]))

    def down_into(put, p):
        cols = pl.ds(pl.multiple_of(flip(me, p) * block, block), block)
        for d in range(0, width, 512):
            rows = pl.ds(d, 512)
            put(rows, nn(wu_v[rows, :], act[:, cols]))

    def gia_into(put, p):
        cols = pl.ds(pl.multiple_of(flip(me, p) * block, block), block)
        for d in range(0, width, 512):
            rows = pl.ds(d, 512)
            put(rows, nn(wg_v[rows, 0 : qcols + kvcols], gqkv[:, cols]))

    def to_snd(p):
        def put(rows, value):
            snd[p - 1, rows, :] = value.astype(BF)

        return put

    def to_own(rows, value):
        own[rows, :] = value

    tok_start(0)
    for c in early:
        c.wait()
    for c in then:
        c.start()
    gsum[...] = jnp.zeros_like(gsum)
    mid_rows = hidden // 2
    def gate_grads(start):
        step = min(512, mid_rows)
        for i in range(length // QB):
            cols = pl.ds(i * QB, QB)
            for f in range(start, start + mid_rows, step):
                units = pl.ds(f, step)
                grad_act = nt(wd_v[units, :], tok[cols, :])
                f1[units, cols] = (grad_act * f1[units, cols].astype(F32)).astype(BF)
                f2[units, cols] = (grad_act * f2[units, cols].astype(F32)).astype(BF)

    down_grad(0, False, 0)
    down_grad(0, True, 0)
    z()
    for p in range(1, max(1, mid_rows // 256)):
        down_grad(0, False, p)
        down_grad(0, True, p)
    for c in then:
        c.wait()
    for c in late:
        c.start()
    z()
    tok_hand_on(0)
    z()
    tok_finish(0)
    down_grad(1, False)
    down_grad(1, True)
    z()
    gate_grads(mid_rows)
    z()
    for c in range(PAIR // 2):
        pair_done(c)
    rest = load(n1 + 3 + tp, wd.at[pl.ds(0, mid_rows)], wd_v.at[pl.ds(0, mid_rows)])
    rest.start()
    rest.wait()
    gate_grads(0)
    z()
    for c in late[:2]:
        c.wait()
    for n, p in enumerate(order):
        gib_into(to_snd(p), p)
        rs_send(0, p)
        if n == 1:
            z()
    late[2].wait()
    weight_grad(1, f1, ab, False)
    weight_grad(1, f1, ab, True)
    z(2)
    if hops:
        rs_merge(0, 1)
        rs_merge(0, 2)
    gib_into(to_own, 0)
    z(3)
    for c in late[3:]:
        c.wait()
    qkv_load = load(n1, wqkv, wg_v.at[:, pl.ds(0, qcols + kvcols)])
    qkv_load.start()
    down_load = load(n1 + 1, wdt, wu_v)
    down_load.start()

    grad_in = rs_finish(0)
    base_b, inv_b = normed(mid[...])
    back, gain_b = norm_back(grad_in, base_b, inv_b, gains[1:2, :])
    gs[...] = tok[own_rows, :].astype(F32) + back
    gsum[1:2, :] = gain_b
    gb[...] = gs[...].astype(BF)
    tok[own_rows, :] = gb[...]

    tok_start(1)
    z()
    weight_grad(2, f2, ab, False)
    z()
    weight_grad(2, f2, ab, True)
    z(2)
    a_load = load(n1 + 2, a_in, ab)
    a_load.start()
    tok_hand_on(1)
    z(2)
    tok_finish(1)

    weight_grad(3, mix, tok, False)
    weight_grad(3, mix, tok, True)
    for n in range(0, length, QB):
        cols = pl.ds(n, QB)
        gm_t[:, :, cols] = nt(wo_v[...], tok[cols, :]).astype(BF).reshape(heads, HD, QB)
    z()
    down_load.wait()
    for p in order:
        down_into(to_snd(p), p)
        rs_send(1, p)
    down_into(to_own, 0)
    z()

    dk[...] = jnp.zeros_like(dk)
    dv[...] = jnp.zeros_like(dv)
    for i in range(length // QB - 1, -1, -1):
        reach = (i + 1) * QB
        cols = pl.ds(i * QB, QB)
        same = segc[pl.ds(0, reach), 0:1] == segr[:, cols]
        later = lax.broadcasted_iota(jnp.int32, (reach, QB), 0) <= lax.broadcasted_iota(jnp.int32, (reach, QB), 1) + i * QB
        bias[pl.ds(0, reach), :] = jnp.where(same & later, 0.0, -1e30)

        def head(h, _, reach=reach, cols=cols):
            g = h // group
            s = nn(k_n[g, pl.ds(0, reach), :][:, :HD], q_t[h, :, cols]) * SCALE + bias[pl.ds(0, reach), :]
            p = jnp.exp(s - lse[h, :, cols])
            grad_p = nn(v_n[g, pl.ds(0, reach), :][:, :HD], gm_t[h, :, cols])
            delta = jnp.sum(p * grad_p, axis=0, keepdims=True)
            ds = (p * (grad_p - delta)).astype(BF)
            dq = nn(k_t[g, :, pl.ds(0, reach)], ds) * SCALE
            gqkv[pl.ds(pl.multiple_of(h * HD, 16), HD), cols] = unrot_rows(dq, cos_t[:, cols], sin_t[:, cols]).astype(BF)
            dk[g, :, pl.ds(0, reach)] += nt(q_t[h, :, cols], ds)
            dv[g, :, pl.ds(0, reach)] += nt(gm_t[h, :, cols], p.astype(BF))
            return 0

        lax.fori_loop(0, heads, head, 0)
        z()
        if i == length // QB - 2 and hops:
            rs_merge(1, 1)
            rs_merge(1, 2)
    for g in range(kv_heads):
        at = qcols + g * 2 * HD
        gqkv[pl.ds(at, HD), :] = unrot_rows(dk[g] * SCALE, cos_t[...], sin_t[...]).astype(BF)
        gqkv[pl.ds(at + HD, HD), :] = dv[g].astype(BF)
    a_load.wait()
    weight_grad(4, gqkv.at[pl.ds(0, qcols)], ab, False)
    weight_grad(4, gqkv.at[pl.ds(0, qcols)], ab, True)
    weight_grad(5, gqkv.at[pl.ds(qcols, kvcols)], ab, False)
    weight_grad(5, gqkv.at[pl.ds(qcols, kvcols)], ab, True)
    z()
    stage_res = rs_finish(1)
    gb[...] = (mid[...] + stage_res).astype(BF)
    res_copy = pltpu.make_async_copy(gb, res_out, out_sem.at[0])
    res_copy.start()
    for p in range(1, tp):
        signal(cr_rs, (md, flip(me, p)))
    pl.semaphore_wait(cr_rs, tp - 1)
    z()
    qkv_load.wait()
    for p in order:
        gia_into(to_snd(p), p)
        rs_send(2, p)
    gia_into(to_own, 0)
    z(2)
    if hops:
        rs_merge(2, 1)
        rs_merge(2, 2)
    z(3)
    grad_in = rs_finish(2)
    base_a, inv_a = normed(hid[...].astype(F32))
    back, gain_a = norm_back(grad_in, base_a, inv_a, gains[0:1, :])
    hid[...] = (gs[...] + back).astype(BF)
    hid_copy = pltpu.make_async_copy(hid, hid_out, out_sem.at[1])
    hid_copy.start()
    gsum[0:1, :] = gain_a

    stages = []
    bit = 1
    while bit < dp:
        stages.append((flip(md, bit), me))
        bit *= 2
    bit = 1
    while bit < tp:
        stages.append((md, flip(me, bit)))
        bit *= 2
    for n, peer in enumerate(stages):
        c = remote(gsum, gland.at[n], gain_ssem.at[n], gain_rsem.at[n], peer)
        c.start()
        z()
        c.wait()
        gsum[...] = gsum[...] + gland[n]
    gain_copy = pltpu.make_async_copy(gsum.at[pl.ds(0, 8)], gain_out, out_sem.at[2])
    gain_copy.start()

    last = chunks + 3 * lag + 2
    z(last - slot_now[0])
    for c in (res_copy, hid_copy, gain_copy):
        c.wait()
    for c in range(chunks):
        remote(in_ring(dn_ring, c), sums_out.at[1 - core, rows_of(c)], sib_ssem.at[c], sib_rsem.at[c], sibling).wait_recv()

        @pl.when(is_mid)
        def _(c=c):
            part_copy(c, dn_ring, dn_rsem).wait_send()

        @pl.when(not_mid)
        def _(c=c):
            part_copy(c, up_ring, up_rsem).wait_send()

        pair_done(c)


def backward(mesh, cot, cot_all, a, b, q, kt, k, v, lse, mix, f1, f2, act, wdt, mid, hid, wqkv, wo, wg, wu, wd, gains, segc, segr, cos_t, sin_t):
    tp, dp = mesh.shape["tp"], mesh.shape["dp"]
    block, width = hid.shape
    length = tp * block
    hidden = wg.shape[1]
    heads = wo.shape[0] // HD
    kv_heads = (wqkv.shape[1] - heads * HD) // (2 * HD)
    qcols, kvcols = heads * HD, kv_heads * 2 * HD
    r = hidden // PAIR
    half_rows = (3 * hidden + 2 * qcols + kvcols) // 2
    chunks = (3 * hidden + 2 * qcols) // 2 // r + kvcols // 2 // (r // FINE)
    steps = (dp - 1).bit_length() + (tp - 1).bit_length()
    sds = jax.ShapeDtypeStruct
    outs = [
        sds((block, width), BF),
        sds((block, width), BF),
        sds((2, half_rows, width), BF),
        sds((8, width), F32),
    ]
    dma = pltpu.SemaphoreType.DMA
    reg = pltpu.SemaphoreType.REGULAR
    scratch = [
        pltpu.VMEM((length, width), BF),
        pltpu.VMEM((hidden, length), BF),
        pltpu.VMEM((hidden, width), BF),
        pltpu.VMEM((hidden, length), BF),
        pltpu.VMEM((hidden, length), BF),
        pltpu.VMEM((width, hidden), BF),
        pltpu.VMEM((width, hidden), BF),
        pltpu.VMEM((length, width), BF),
        pltpu.VMEM((tp - 1, width, block), BF),
        pltpu.VMEM((tp - 1, width, block), BF),
        pltpu.VMEM((half_rows, width), BF),
        pltpu.VMEM((PAIR * r, width), BF),
        pltpu.VMEM((RING, r, width), BF),
        pltpu.VMEM((RING, r, width), BF),
        pltpu.VMEM((heads, HD, length), BF),
        pltpu.VMEM((kv_heads, HD, length), BF),
        pltpu.VMEM((kv_heads, length, 128), BF),
        pltpu.VMEM((kv_heads, length, 128), BF),
        pltpu.VMEM((heads, 1, length), F32),
        pltpu.VMEM((qcols, length), BF),
        pltpu.VMEM((heads, HD, length), BF),
        pltpu.VMEM((qcols + kvcols, length), BF),
        pltpu.VMEM((kv_heads, HD, length), F32),
        pltpu.VMEM((kv_heads, HD, length), F32),
        pltpu.VMEM((length, QB), F32),
        pltpu.VMEM((block, width), F32),
        pltpu.VMEM((block, width), BF),
        pltpu.VMEM((block, width), F32),
        pltpu.VMEM((width, block), F32),
        pltpu.VMEM((block, width), BF),
        pltpu.VMEM((qcols, width), BF),
        pltpu.VMEM((8, width), F32),
        pltpu.VMEM((steps, 8, width), F32),
        dma((4 + 2 * tp + 20,)),
        dma((3,)),
        dma((chunks,)), dma((chunks,)), dma((chunks,)), dma((chunks,)), dma((chunks,)), dma((chunks,)), dma((chunks,)), dma((chunks,)), dma((chunks,)),
        dma((3, tp - 1, 2)), dma((3, tp - 1, 2)),
        dma((2, tp, 2)), dma((2, tp, 2)),
        dma((steps,)), dma((steps,)),
        reg, reg, reg, reg,
    ]
    any_ = pl.BlockSpec(memory_space=pl.ANY)
    vmem = pl.BlockSpec(memory_space=pltpu.VMEM)
    return pl.pallas_call(
        functools.partial(backward_kernel, tp, dp),
        out_shape=outs,
        in_specs=[any_] * 21 + [vmem] * 5,
        out_specs=[any_] * len(outs),
        scratch_shapes=scratch,
        compiler_params=pltpu.CompilerParams(collective_id=1, has_side_effects=True, vmem_limit_bytes=62 * 2**20),
        name="backward",
    )(cot, cot_all, a, b, q, kt, k, v, lse, mix.reshape(qcols, length), f1, f2, act, wdt, mid, hid, wqkv, wo, wg, wu, wd, gains, segc, segr, cos_t, sin_t)


def finish_kernel(sums, res, hid, gain, res_out, hid_out, query_out, keyval_out, output_out, gate_out, up_out, down_out, gain_out,
                  in_v, nat_v, wide_v, turn_v, query_v, pass_v, in_sem, nat_sem, wide_sem, turn_sem, query_sem, copy_sem):
    width = sums.shape[2]
    passing = [
        pltpu.make_async_copy(res, pass_v.at[0], copy_sem.at[0]),
        pltpu.make_async_copy(hid, pass_v.at[1], copy_sem.at[1]),
    ]
    copies = [
        pltpu.make_async_copy(pass_v.at[0], res_out, copy_sem.at[0]),
        pltpu.make_async_copy(pass_v.at[1], hid_out, copy_sem.at[1]),
    ]
    outs = (down_out, gate_out, up_out, output_out, query_out, keyval_out)
    flat = (True, False, False, True, False, True)
    total = [o.shape[0] if f else o.shape[1] for o, f in zip(outs, flat)]
    tasks, at = [], 0
    for n, rows in enumerate(total):
        hr = rows // 2
        if n == 0:
            for core in (0, 1):
                for side in (0, 1):
                    tasks.append((n, [(core, at + side * (hr // 2), hr // 2)], core * hr, side))
        elif n < 3:
            step = min(256, hr)
            for core in (0, 1):
                for p in range(0, hr, step):
                    tasks.append((n, [(core, at + p, step)], core * hr + p, step))
        else:
            tasks.append((n, [(0, at, hr), (1, at, hr)], 0, rows))
        at += hr
    depth = in_v.shape[0]
    keep = nat_v.shape[0]

    def loads(i):
        _, pieces, _, _ = tasks[i]
        to, out = 0, []
        for j, (core, row, rows) in enumerate(pieces):
            out.append(pltpu.make_async_copy(sums.at[core, pl.ds(row, rows)], in_v.at[i % depth, pl.ds(to, rows)], in_sem.at[i % depth, j]))
            to += rows
        return out

    for i in range(min(depth - 1, len(tasks))):
        for c in loads(i):
            c.start()
    for c in passing:
        c.start()
    nat_busy, turn_busy, wide_busy, tail = {}, {}, {}, []
    nats = turns = wides = 0
    rows_r = total[0] // PAIR
    for i, (n, _, row, rows) in enumerate(tasks):
        if i == 2:
            for p, c in zip(passing, copies):
                p.wait()
                c.start()
        if i + depth - 1 < len(tasks):
            for c in loads(i + depth - 1):
                c.start()
        for c in loads(i):
            c.wait()
        if n == 0:
            slot = wides % 2
            wides += 1
            if slot in wide_busy:
                wide_busy.pop(slot).wait()
            r = rows_r
            for j in range(total[0] // 2 // (2 * r)):
                for k in (0, 1):
                    wide_v[slot, pl.ds((2 * j + k) * r, r), :] = in_v[
                        i % depth, pl.ds(j * r, r), pl.ds(k * (width // 2), width // 2)
                    ].astype(F32)
            c = pltpu.make_async_copy(
                wide_v.at[slot], outs[n].at[pl.ds(row, total[0] // 2), pl.ds(rows * (width // 2), width // 2)], wide_sem.at[slot]
            )
            wide_busy[slot] = c
        elif flat[n]:
            slot = nats % keep
            nats += 1
            if slot in nat_busy:
                nat_busy.pop(slot).wait()
            nat_v[slot, pl.ds(0, rows), :] = in_v[i % depth, pl.ds(0, rows), :].astype(F32)
            c = pltpu.make_async_copy(nat_v.at[slot, pl.ds(0, rows)], outs[n].at[pl.ds(row, rows)], nat_sem.at[slot])
            nat_busy[slot] = c
        elif n < 3:
            slot = turns % keep
            turns += 1
            if slot in turn_busy:
                turn_busy.pop(slot).wait()
            turn_v[slot] = in_v[i % depth, pl.ds(0, rows), :].T.astype(F32)
            c = pltpu.make_async_copy(turn_v.at[slot], outs[n].at[:, pl.ds(row, rows)], turn_sem.at[slot])
            turn_busy[slot] = c
        else:
            query_v[...] = in_v[i % depth, pl.ds(0, rows), :].T.astype(F32)
            c = pltpu.make_async_copy(query_v, outs[n], query_sem)
            tail.append(c)
        c.start()
    gain_out[...] = gain[0:2, :]
    for c in [*nat_busy.values(), *turn_busy.values(), *wide_busy.values(), *tail, *copies]:
        c.wait()


def finish(sums, res, hid, gain, hidden, qcols, kvcols):
    width = sums.shape[2]
    sds = jax.ShapeDtypeStruct
    outs = [
        sds(res.shape, BF), sds(hid.shape, BF),
        sds((width, qcols), F32), sds((kvcols, width), F32), sds((qcols, width), F32),
        sds((width, hidden), F32), sds((width, hidden), F32), sds((hidden, width), F32),
        sds((2, width), F32),
    ]
    dma = pltpu.SemaphoreType.DMA
    any_ = pl.BlockSpec(memory_space=pl.ANY)
    vmem = pl.BlockSpec(memory_space=pltpu.VMEM)
    tall = max(min(256, hidden // 2), qcols, kvcols)
    step = min(256, hidden // 2)
    return pl.pallas_call(
        finish_kernel,
        out_shape=outs,
        in_specs=[any_] * 3 + [vmem],
        out_specs=[any_] * 8 + [vmem],
        scratch_shapes=[
            pltpu.VMEM((4, tall, width), BF),
            pltpu.VMEM((3, tall, width), F32),
            pltpu.VMEM((2, hidden // 2, width // 2), F32),
            pltpu.VMEM((3, width, step), F32),
            pltpu.VMEM((width, qcols), F32),
            pltpu.VMEM((2, *res.shape), BF),
            dma((4, 2)), dma((3,)), dma((2,)), dma((3,)), dma, dma((2,)),
        ],
        compiler_params=pltpu.CompilerParams(vmem_limit_bytes=62 * 2**20),
        name="finish",
    )(sums, res, hid, gain)


def local(mesh, hidden, segments, cotangent, w_query, w_keyval, w_output, w_gate, w_up, w_down, gains):
    width = hidden.shape[2]
    hid, cot, gain = hidden[0], cotangent[0], gains[0]
    wq, wo, wg, wu, wd = w_query[0], w_output[0], w_gate[0], w_up[0], w_down[0]
    wkv_t = w_keyval[0].transpose(1, 2, 0).reshape(-1, width)
    inverse = ROPE_BASE ** (-(jnp.arange(HALF, dtype=F32) * 2.0) / HD)
    wqkv, segc, cos_t, sin_t, a, b, cot_all, q, kt, k, v, lse, mix, f1, f2, act, wdt, mid = forward(
        mesh, hid, cot, wq, wkv_t, wo, wg, wu, wd, gain, segments, inverse[:, None]
    )
    result, grad_hidden, sums, gain_sum = backward(
        mesh, cot, cot_all, a, b, q, kt, k, v, lse, mix, f1, f2, act, wdt, mid, hid,
        wqkv, wo, wg, wu, wd, gain, segc, segments, cos_t, sin_t,
    )
    result, grad_hidden, query, keyval, output, gate, up, down, gain_sum = finish(
        sums, result, grad_hidden, gain_sum, wd.shape[0], wo.shape[0], wkv_t.shape[0]
    )
    keyval = keyval.reshape(*w_keyval.shape[2:], width).transpose(2, 0, 1)
    return tuple(x[None] for x in (result, grad_hidden, query, keyval, output, gate, up, down, gain_sum))


def solution(mesh):
    split = P("dp", "tp", None)
    columns, rows = P(None, None, "tp"), P(None, "tp", None)
    heads = P(None, None, "tp", None)
    return jax.shard_map(
        functools.partial(local, mesh),
        mesh=mesh,
        in_specs=(split, P("dp", None), split, columns, heads, rows, columns, columns, rows, P()),
        out_specs=(split, split, columns, heads, rows, columns, columns, rows, P()),
        check_vma=False,
    )
```

```python
import functools
import jax
import jax.numpy as jnp
from jax import lax
from jax.experimental import pallas as pl
from jax.experimental.pallas import tpu as pltpu
from jax.sharding import PartitionSpec as P

MESH = pl.DeviceIdType.MESH
HD = 96
HALF = HD // 2
EPS = 1e-05
ROPE_BASE = 100000.0
SCALE = HD ** (-0.5)
BF = jnp.bfloat16
F32 = jnp.float32
QB = 256


def flip(index, mask):
    out = index
    bit = 1
    while bit <= mask:
        if mask & bit:
            out = out + bit - 2 * bit * ((index // bit) % 2)
        bit *= 2
    return out


def nn(x, y):
    return lax.dot_general(x, y, (((1,), (0,)), ((), ())), preferred_element_type=F32)


def nt(x, y):
    return lax.dot_general(x, y, (((1,), (1,)), ((), ())), preferred_element_type=F32)


def normed(stream):
    inv = lax.rsqrt(jnp.mean(stream * stream, axis=-1, keepdims=True) + EPS)
    return stream * inv, inv


def rot_rows(x, cos, sin):
    x1, x2 = x[:HALF], x[HALF:]
    return jnp.concatenate([x1 * cos - x2 * sin, x2 * cos + x1 * sin], axis=0)


def forward_kernel(
    tp, dp,
    hid, cot, wq, wkv_t, wo, wg, wu, wd, gains, segr, inverse,
    wqkv_out, seg_out, cos_out, sin_out, a_out, b_out, cot_all, q_out, kt_out, k_out, v_out, lse_out, mix_out, f1_out, f2_out, act_out, wdt_out, mid_out,
    hid_all, mixed_all, wo_all, wq_in, w_in, w_st, wqkv_t, wg_t, wu_t, wd_n, wd_t,
    a_v, b_v, q_t, k_t, k_n, v_n, v_t, mix_t, bias, lse, f1, f2, act_t, mid_v, mid_w, segc, cos_t, sin_t,
    load_sem, out_sem, hid_ssem, hid_rsem, cot_ssem, cot_rsem, mix_ssem, mix_rsem, wo_ssem, wo_rsem,
):
    me, md = lax.axis_index("tp"), lax.axis_index("dp")
    nz = dp // 2
    core, mz = md % 2, md // 2
    block, width = hid.shape
    length = tp * block
    hidden = wg.shape[1]
    heads, kv_heads = q_t.shape[0], k_t.shape[0]
    qcols, kvcols = heads * HD, kv_heads * 2 * HD
    pieces = length // QB
    hops = tp == 4
    rows_o = qcols // dp
    spread = qcols % (16 * dp) == 0
    half = block // 2

    loads = [
        pltpu.make_async_copy(wq, wq_in, load_sem.at[0]),
        pltpu.make_async_copy(wd, wd_n, load_sem.at[1]),
        pltpu.make_async_copy(hid, hid_all.at[me], load_sem.at[2]),
        pltpu.make_async_copy(wg, w_st, load_sem.at[3]),
        pltpu.make_async_copy(wo, wo_all.at[me], load_sem.at[4]),
        pltpu.make_async_copy(wkv_t, wqkv_t.at[pl.ds(qcols, kvcols)], load_sem.at[5]),
    ]
    for c in loads:
        c.start()

    barrier = pltpu.get_barrier_semaphore()
    peers = [(md, flip(me, p)) for p in range(1, tp)]
    if spread:
        peers += [(flip(md, 2 * z), me) for z in range(1, nz)] + [(flip(md, 1), me)]
    for peer in peers:
        pl.semaphore_signal(barrier, inc=1, device_id=peer, device_id_type=MESH)
    pl.semaphore_wait(barrier, len(peers))

    def remote(src, dst, ssem, rsem, peer):
        return pltpu.make_async_remote_copy(src, dst, ssem, rsem, device_id=peer, device_id_type=MESH)

    def gather_first(src, dst, ssem, rsem, cols=pl.ds(0, width)):
        out = []
        for p in range(1, tp):
            if hops and p == 3:
                continue
            for part in (0, 1) if p == 1 else (1, 0):
                rows = pl.ds(part * half, half)
                out.append(remote(src.at[rows, cols], dst.at[me, rows], ssem.at[p, part], rsem.at[p, part], (md, flip(me, p))))
        return out

    def arrived(dst, ssem, rsem, p, part):
        rows = pl.ds(part * half, half)
        slot = dst.at[flip(me, p), rows]
        return remote(slot, slot, ssem.at[p, part], rsem.at[p, part], (md, flip(me, p)))

    def handed(dst, ssem, rsem, part):
        rows = pl.ds(part * half, half)
        came, goes = (1, 2) if part == 0 else (2, 1)
        slot = dst.at[flip(me, came), rows]
        return remote(slot, slot, ssem.at[3, part], rsem.at[3, part], (md, flip(me, goes)))

    hid_first = gather_first(hid, hid_all, hid_ssem, hid_rsem)
    cot_first = gather_first(cot, cot_all, cot_ssem, cot_rsem, pl.ds(0, width // 2))

    piece = pl.ds((core * nz + mz) * rows_o, rows_o) if spread else pl.ds(0, qcols)
    wo_tp = [
        remote(wo.at[piece], wo_all.at[me, piece], wo_ssem.at[0, p], wo_rsem.at[0, p], (md, flip(me, p)))
        for p in range(1, tp)
    ]
    for c in wo_tp:
        c.start()
    for c in hid_first:
        c.start()
    wo_z, wo_core = [], []
    if spread:
        for z in range(1, nz):
            for p in range(1, tp):
                slot = wo_all.at[flip(me, p), piece]
                wo_z.append(remote(slot, slot, wo_ssem.at[z, p], wo_rsem.at[z, p], (flip(md, 2 * z), me)))
        both = pl.ds(core * nz * rows_o, nz * rows_o)
        for p in range(1, tp):
            slot = wo_all.at[flip(me, p), both]
            wo_core.append(remote(slot, slot, wo_ssem.at[nz, p], wo_rsem.at[nz, p], (flip(md, 1), me)))

    def turn(dst, src, step=256):
        rows = src.shape[0]
        for r in range(0, rows, step):
            dst[:, pl.ds(r, step)] = src[pl.ds(r, step), :].T

    def project(src):
        off = pl.multiple_of(src * block, block)
        cols = pl.ds(off, block)
        base, _ = normed(hid_all[src].astype(F32))
        a = (base * gains[0:1, :]).astype(BF)
        a_v[cols, :] = a
        cos, sin = cos_t[:, cols], sin_t[:, cols]
        qk = nt(wqkv_t[...], a)
        for h in range(heads):
            q_t[h, :, cols] = rot_rows(qk[h * HD : (h + 1) * HD], cos, sin).astype(BF)
        pad = jnp.zeros((128 - HD, block), F32)
        for g in range(kv_heads):
            at = qcols + g * 2 * HD
            kr = rot_rows(qk[at : at + HD], cos, sin)
            vr = qk[at + HD : at + 2 * HD]
            k_t[g, :, cols] = kr.astype(BF)
            v_t[g, :, cols] = vr.astype(BF)
            k_n[g, cols, :] = jnp.concatenate([kr, pad], axis=0).T.astype(BF)
            v_n[g, cols, :] = jnp.concatenate([vr, pad], axis=0).T.astype(BF)

    loads[0].wait()
    turn(wqkv_t.at[pl.ds(0, qcols)], wq_in)
    loads[3].wait()
    turn(wg_t, w_st)
    wu_load = pltpu.make_async_copy(wu, w_st, load_sem.at[3])
    wu_load.start()
    for c in wo_tp:
        c.wait()
    for c in wo_z:
        c.start()
    segc[...] = jnp.broadcast_to(segr[...].astype(F32), (128, length)).T[:, :8].astype(jnp.int32)
    start = jnp.sum((segc[:, 0:1] < segr[...]).astype(F32), axis=0, keepdims=True)
    place = lax.broadcasted_iota(jnp.int32, (1, length), 1).astype(F32) - start
    angles = inverse[...] * place
    cos_t[...] = jnp.cos(angles)
    sin_t[...] = jnp.sin(angles)
    w_in[:, 0:qcols] = wq_in[...]
    loads[5].wait()
    w_in[:, qcols : qcols + kvcols] = wqkv_t[qcols : qcols + kvcols, :].T
    loads[2].wait()
    project(me)
    wu_load.wait()
    turn(wu_t, w_st)
    loads[1].wait()
    turn(wd_t, wd_n)
    loads[4].wait()

    if hops:
        for p, part in ((1, 0), (2, 1)):
            arrived(hid_all, hid_ssem, hid_rsem, p, part).wait_recv()
            handed(hid_all, hid_ssem, hid_rsem, part).start()
        for p, part in ((1, 1), (2, 0)):
            arrived(hid_all, hid_ssem, hid_rsem, p, part).wait_recv()
            project(flip(me, p))
        for part in (0, 1):
            rows = pl.ds(part * half, half)
            slot = hid_all.at[flip(me, 3), rows]
            remote(slot, slot, hid_ssem.at[3, part], hid_rsem.at[3, part], (md, flip(me, 2))).wait_recv()
        project(flip(me, 3))
    else:
        for p in range(1, tp):
            for part in (0, 1):
                arrived(hid_all, hid_ssem, hid_rsem, p, part).wait_recv()
            project(flip(me, p))

    outs = []

    def put(src, dst):
        c = pltpu.make_async_copy(src, dst, out_sem.at[len(outs)])
        c.start()
        outs.append(c)

    for src, dst in ((w_in, wqkv_out), (wd_t, wdt_out), (segc, seg_out), (cos_t, cos_out), (sin_t, sin_out), (a_v, a_out), (q_t, q_out), (k_t, kt_out), (k_n, k_out), (v_n, v_out)):
        put(src, dst)

    def mix_slot(who, i):
        return mixed_all.at[who, pl.ds(i * QB, QB)]

    def mix_copy(i, p):
        return remote(mix_slot(me, i), mix_slot(me, i), mix_ssem.at[p, i], mix_rsem.at[p, i], (md, flip(me, p)))

    def mix_arrived(i, p):
        slot = mix_slot(flip(me, p), i)
        return remote(slot, slot, mix_ssem.at[p, i], mix_rsem.at[p, i], (md, flip(me, p)))

    def mix_handed(i):
        came, goes = (1, 2) if i % 2 == 0 else (2, 1)
        slot = mix_slot(flip(me, came), i)
        return remote(slot, slot, mix_ssem.at[3, i], mix_rsem.at[3, i], (md, flip(me, goes)))

    def hand_on(i):
        if not hops:
            return
        mix_arrived(i, 1 if i % 2 == 0 else 2).wait_recv()
        mix_handed(i).start()

    for i in range(pieces):
        if i == pieces - 1:
            for n in range(pieces - 3):
                hand_on(n)
        reach = (i + 1) * QB
        cols = pl.ds(i * QB, QB)
        same = segc[pl.ds(0, reach), 0:1] == segr[:, cols]
        later = lax.broadcasted_iota(jnp.int32, (reach, QB), 0) <= lax.broadcasted_iota(jnp.int32, (reach, QB), 1) + i * QB
        bias[pl.ds(0, reach), :] = jnp.where(same & later, 0.0, -1e30)

        def head(h, _, reach=reach, cols=cols):
            g = h // (heads // kv_heads)
            s = nn(k_n[g, pl.ds(0, reach), :][:, :HD], q_t[h, :, cols]) * SCALE + bias[pl.ds(0, reach), :]
            top = jnp.max(s, axis=0, keepdims=True)
            e = jnp.exp(s - top)
            total = jnp.sum(e, axis=0, keepdims=True)
            p = (e * (1.0 / total)).astype(BF)
            mix_t[h, :, cols] = nn(v_t[g, :, pl.ds(0, reach)], p).astype(BF)
            lse[h, :, cols] = top + jnp.log(total)
            return 0

        lax.fori_loop(0, heads, head, 0)
        mixed_all[me, cols, :] = mix_t[:, :, cols].reshape(qcols, QB).T
        for p in range(1, tp):
            if not (hops and p == 3):
                mix_copy(i, p).start()
    put(lse, lse_out)
    put(mix_t, mix_out)
    if pieces >= 3:
        hand_on(pieces - 3)
    for c in wo_z:
        c.wait()
    for c in wo_core:
        c.start()

    def middle(i):
        rows = pl.ds(i * QB, QB)
        for p in range(1, tp):
            if hops and p == 3:
                slot = mix_slot(flip(me, 3), i)
                remote(slot, slot, mix_ssem.at[3, i], mix_rsem.at[3, i], (md, flip(me, 1))).wait_recv()
            elif not (hops and p == (1 if i % 2 == 0 else 2)):
                mix_arrived(i, p).wait_recv()
        per = QB // block if QB >= block else 1
        mixed = jnp.concatenate([mixed_all[s, rows, :] for s in range(tp)], axis=1)
        for d in range(0, width, 512):
            cols = pl.ds(d, 512)
            stream = jnp.concatenate([hid_all[i * per + n, :, cols] for n in range(per)], axis=0).astype(F32)
            mid_w[:, cols] = stream + nn(mixed, wo_all[:, :, cols].reshape(tp * qcols, 512))
        total = mid_w[...]
        base, _ = normed(total)
        b_v[rows, :] = (base * gains[1:2, :]).astype(BF)
        for n in range(per):
            @pl.when(me == i * per + n)
            def _(n=n):
                mid_v[...] = total[n * block : (n + 1) * block]

    def feed(i):
        rows = pl.ds(i * QB, QB)
        b = b_v[rows, :]
        step = 256
        for f in range(0, hidden, step):
            units = pl.ds(f, step)
            gate = nt(wg_t[units, :], b)
            up = nt(wu_t[units, :], b)
            sig = jax.nn.sigmoid(gate)
            silu = gate * sig
            f1[units, rows] = (up * sig * (1.0 + gate * (1.0 - sig))).astype(BF)
            f2[units, rows] = silu.astype(BF)
            act_t[units, rows] = (silu * up).astype(BF)
        put(b_v.at[rows], b_out.at[rows])
        for src, dst in ((f1, f1_out), (f2, f2_out), (act_t, act_out)):
            put(src.at[:, rows], dst.at[:, rows])

    if pieces >= 2:
        hand_on(pieces - 2)
    for c in wo_core:
        c.wait()
    for i in range(pieces):
        if i == min(1, pieces - 1):
            hand_on(pieces - 1)
            for c in cot_first:
                c.start()
        middle(i)
        feed(i)
    put(mid_v, mid_out)

    if hops:
        for p, part in ((1, 0), (2, 1)):
            arrived(cot_all, cot_ssem, cot_rsem, p, part).wait_recv()
            handed(cot_all, cot_ssem, cot_rsem, part).start()
        for p, part in ((1, 1), (2, 0)):
            arrived(cot_all, cot_ssem, cot_rsem, p, part).wait_recv()
        for part in (0, 1):
            rows = pl.ds(part * half, half)
            slot = cot_all.at[flip(me, 3), rows]
            remote(slot, slot, cot_ssem.at[3, part], cot_rsem.at[3, part], (md, flip(me, 2))).wait_recv()
    else:
        for p in range(1, tp):
            for part in (0, 1):
                arrived(cot_all, cot_ssem, cot_rsem, p, part).wait_recv()
    for c in hid_first + cot_first:
        c.wait_send()
    if hops:
        for part in (0, 1):
            handed(hid_all, hid_ssem, hid_rsem, part).wait_send()
            handed(cot_all, cot_ssem, cot_rsem, part).wait_send()
        for i in range(pieces):
            mix_handed(i).wait_send()
    for n in range(pieces):
        for p in range(1, tp):
            if not (hops and p == 3):
                mix_copy(n, p).wait_send()
    for c in outs:
        c.wait()


def forward(mesh, hid, cot, wq, wkv_t, wo, wg, wu, wd, gains, segr, inverse):
    tp, dp = mesh.shape["tp"], mesh.shape["dp"]
    block, width = hid.shape
    length = tp * block
    hidden = wg.shape[1]
    heads = wo.shape[0] // HD
    kv_heads = wkv_t.shape[0] // (2 * HD)
    nz = dp // 2
    pieces = length // QB
    sds = jax.ShapeDtypeStruct
    outs = [
        sds((width, (heads + 2 * kv_heads) * HD), BF),
        sds((length, 8), jnp.int32),
        sds((HALF, length), F32),
        sds((HALF, length), F32),
        sds((length, width), BF),
        sds((length, width), BF),
        sds((tp, block, width // 2), BF),
        sds((heads, HD, length), BF),
        sds((kv_heads, HD, length), BF),
        sds((kv_heads, length, 128), BF),
        sds((kv_heads, length, 128), BF),
        sds((heads, 1, length), F32),
        sds((heads, HD, length), BF),
        sds((hidden, length), BF),
        sds((hidden, length), BF),
        sds((hidden, length), BF),
        sds((width, hidden), BF),
        sds((block, width), F32),
    ]
    dma = pltpu.SemaphoreType.DMA
    scratch = [
        pltpu.VMEM((tp, block, width), BF),
        pltpu.VMEM((tp, length, heads * HD), BF),
        pltpu.VMEM((tp, heads * HD, width), BF),
        pltpu.VMEM((width, heads * HD), BF),
        pltpu.VMEM((width, heads * HD + kv_heads * 2 * HD), BF),
        pltpu.VMEM((width, hidden), BF),
        pltpu.VMEM((heads * HD + kv_heads * 2 * HD, width), BF),
        pltpu.VMEM((hidden, width), BF),
        pltpu.VMEM((hidden, width), BF),
        pltpu.VMEM((hidden, width), BF),
        pltpu.VMEM((width, hidden), BF),
        pltpu.VMEM((length, width), BF),
        pltpu.VMEM((length, width), BF),
        pltpu.VMEM((heads, HD, length), BF),
        pltpu.VMEM((kv_heads, HD, length), BF),
        pltpu.VMEM((kv_heads, length, 128), BF),
        pltpu.VMEM((kv_heads, length, 128), BF),
        pltpu.VMEM((kv_heads, HD, length), BF),
        pltpu.VMEM((heads, HD, length), BF),
        pltpu.VMEM((length, QB), F32),
        pltpu.VMEM((heads, 1, length), F32),
        pltpu.VMEM((hidden, length), BF),
        pltpu.VMEM((hidden, length), BF),
        pltpu.VMEM((hidden, length), BF),
        pltpu.VMEM((block, width), F32),
        pltpu.VMEM((QB, width), F32),
        pltpu.VMEM((length, 8), jnp.int32),
        pltpu.VMEM((HALF, length), F32),
        pltpu.VMEM((HALF, length), F32),
        dma((6,)),
        dma((13 + 4 * pieces,)),
        dma((tp, 2)),
        dma((tp, 2)),
        dma((tp, 2)),
        dma((tp, 2)),
        dma((tp, pieces)),
        dma((tp, pieces)),
        dma((nz + 1, tp)),
        dma((nz + 1, tp)),
    ]
    any_ = pl.BlockSpec(memory_space=pl.ANY)
    vmem = pl.BlockSpec(memory_space=pltpu.VMEM)
    return pl.pallas_call(
        functools.partial(forward_kernel, tp, dp),
        out_shape=outs,
        in_specs=[any_] * 8 + [vmem] * 3,
        out_specs=[any_] * len(outs),
        scratch_shapes=scratch,
        compiler_params=pltpu.CompilerParams(collective_id=0, has_side_effects=True, vmem_limit_bytes=62 * 2**20),
        name="forward",
    )(hid, cot, wq, wkv_t, wo, wg, wu, wd, gains, segr, inverse)


RING = 8
AHEAD = 1
FINE = 2
PAIR = 16


def unrot_rows(d, cos, sin):
    d1, d2 = d[:HALF], d[HALF:]
    return jnp.concatenate([d1 * cos + d2 * sin, d2 * cos - d1 * sin], axis=0)


def norm_back(grad, base, inv, gain):
    e = grad * gain
    back = inv * (e - base * jnp.mean(e * base, axis=-1, keepdims=True))
    return back, jnp.sum(grad * base, axis=0, keepdims=True)


def backward_kernel(
    tp, dp,
    cot, cot_all, a_in, b_in, q_in, kt_in, k_in, v_in, lse_in, mix_in, f1_in, f2_in, act_in, wdt, mid_in, hid_in,
    wqkv, wo, wg, wu, wd, gains, segc, segr, cos_t, sin_t,
    res_out, hid_out, sums_out, gain_out,
    tok, act, wd_v, f1, f2, wg_v, wu_v, ab, snd, rcv, acc, pair, up_ring, dn_ring,
    q_t, k_t, k_n, v_n, lse, mix, gm_t, gqkv, dk, dv, bias, mid, hid, gs, own, gb, wo_v, gsum, gland,
    load_sem, out_sem, pair_ssem, pair_rsem, part_ssem, up_rsem, dn_rsem, tot_ssem, sib_ssem, sib_rsem, fin_sem,
    rs_ssem, rs_rsem, tok_ssem, tok_rsem, gain_ssem, gain_rsem, cr_pair, cr_dn, cr_up, cr_rs,
):
    me, md = lax.axis_index("tp"), lax.axis_index("dp")
    nz = dp // 2
    core, mz = md % 2, md // 2
    length, width = tok.shape
    block = length // tp
    half = block // 2
    hidden = act.shape[0]
    heads, kv_heads = q_t.shape[0], k_t.shape[0]
    group = heads // kv_heads
    qcols, kvcols = heads * HD, kv_heads * 2 * HD
    hops = tp == 4
    r = hidden // PAIR
    parts = [hidden, hidden, hidden, qcols, qcols, kvcols]
    sizes = [r] * (sum(parts[:5]) // 2 // r) + [r // FINE] * (parts[5] // 2 // (r // FINE))
    chunks = len(sizes)
    starts = [sum(sizes[:c]) for c in range(chunks)]
    own_rows = pl.ds(pl.multiple_of(me * block, block), block)

    def load(n, src, dst):
        return pltpu.make_async_copy(src, dst, load_sem.at[n])

    early = [load(0, act_in, act)] + [
        load(
            1 + p,
            cot_all.at[flip(me, p)] if p else cot,
            tok.at[pl.ds(pl.multiple_of(flip(me, p) * block, block), block), pl.ds(0, width // 2 if p else width)],
        )
        for p in range(tp)
    ]
    n0 = 1 + tp
    then = [load(n0, wd.at[pl.ds(hidden // 2, hidden // 2)], wd_v.at[pl.ds(hidden // 2, hidden // 2)]), load(n0 + 1, f1_in, f1), load(n0 + 2, f2_in, f2)]
    late = [
        load(n0 + 3 + n, s, d)
        for n, (s, d) in enumerate(
            (
                (wg, wg_v), (wu, wu_v), (b_in, ab), (q_in, q_t), (kt_in, k_t), (k_in, k_n), (v_in, v_n), (lse_in, lse),
                (mix_in, mix), (mid_in, mid), (hid_in, hid), (wo, wo_v),
            )
        )
    ]
    n1 = n0 + 3 + len(late)
    for c in early:
        c.start()

    barrier = pltpu.get_barrier_semaphore()
    peers = [(md, flip(me, p)) for p in range(1, tp)] + [(flip(md, p), me) for p in range(1, dp)]
    for peer in peers:
        pl.semaphore_signal(barrier, inc=1, device_id=peer, device_id_type=MESH)
    pl.semaphore_wait(barrier, len(peers))

    def remote(src, dst, ssem, rsem, peer):
        return pltpu.make_async_remote_copy(src, dst, ssem, rsem, device_id=peer, device_id_type=MESH)

    def signal(sem, peer):
        pl.semaphore_signal(sem, inc=1, device_id=peer, device_id_type=MESH)

    left = mz < nz // 2
    step_in = jnp.where(left, 1, -1)
    is_mid = (mz == nz // 2 - 1) | (mz == nz // 2)
    has_up = (mz != 0) & (mz != nz - 1)
    not_mid, no_up = jnp.logical_not(is_mid), jnp.logical_not(has_up)
    sibling = (md + 1 - 2 * core, me)
    down_dev = (md + 2 * step_in, me)
    up_dev = (md - 2 * step_in, me)

    def rows_of(c):
        return pl.ds(starts[c], sizes[c])

    def pair_rows(c):
        return pl.ds((c % PAIR) * r, sizes[c])

    def in_ring(ring, c):
        return ring.at[c % RING, pl.ds(0, sizes[c])]

    def pair_copy(c):
        slot = pair_rows(c)
        return remote(wd_v.at[slot], pair.at[slot], pair_ssem.at[c], pair_rsem.at[c], sibling)

    def part_copy(c, dst, rsem):
        return remote(acc.at[rows_of(c)], in_ring(dst, c), part_ssem.at[c], rsem.at[c], down_dev)

    def total_copy(c):
        return remote(in_ring(dn_ring, c), in_ring(dn_ring, c), tot_ssem.at[c], dn_rsem.at[c], up_dev)

    def sib_copy(c):
        return remote(in_ring(dn_ring, c), sums_out.at[core, rows_of(c)], sib_ssem.at[c], sib_rsem.at[c], sibling)

    def fin_copy(c):
        return pltpu.make_async_copy(in_ring(dn_ring, c), sums_out.at[core, rows_of(c)], fin_sem.at[c])

    def gather_part(c):
        pair_copy(c).wait_recv()
        total = acc[rows_of(c), :].astype(F32) + pair[pair_rows(c), :].astype(F32)
        acc[rows_of(c), :] = total.astype(BF)

        @pl.when(has_up)
        def _():
            remote(in_ring(up_ring, c), in_ring(up_ring, c), part_ssem.at[c], up_rsem.at[c], up_dev).wait_recv()
            acc[rows_of(c), :] = (acc[rows_of(c), :].astype(F32) + up_ring[c % RING, 0 : sizes[c]].astype(F32)).astype(BF)
            if c + RING < chunks:
                signal(cr_dn, up_dev)

        if c + PAIR < chunks:
            signal(cr_pair, sibling)
        if c >= RING:
            pl.semaphore_wait(cr_dn, 1)

        @pl.when(is_mid)
        def _():
            part_copy(c, dn_ring, dn_rsem).start()

        @pl.when(not_mid)
        def _():
            part_copy(c, up_ring, up_rsem).start()

    def spread_total(c):
        remote(in_ring(dn_ring, c), in_ring(dn_ring, c), tot_ssem.at[c], dn_rsem.at[c], down_dev).wait_recv()

        @pl.when(is_mid)
        def _():
            dn_ring[c % RING, 0 : sizes[c]] = (acc[rows_of(c), :].astype(F32) + dn_ring[c % RING, 0 : sizes[c]].astype(F32)).astype(BF)

        @pl.when(has_up)
        def _():
            if c >= RING:
                pl.semaphore_wait(cr_up, 1)
            total_copy(c).start()

        sib_copy(c).start()
        fin_copy(c).start()

    def retire(c):
        @pl.when(has_up)
        def _():
            total_copy(c).wait_send()

        sib_copy(c).wait_send()
        fin_copy(c).wait()
        if c + RING < chunks:

            @pl.when(is_mid)
            def _():
                signal(cr_dn, down_dev)

            @pl.when(not_mid)
            def _():
                signal(cr_up, down_dev)

    slot_now = [0]
    ready, given = set(), set()
    lag = 2

    def when_chunk(cond, fn, c):
        if 0 <= c < chunks:

            @pl.when(cond)
            def _():
                fn(c)

    def z(count=1):
        for _ in range(count):
            k = slot_now[0]
            slot_now[0] += 1
            assert set(range(min(chunks, k + AHEAD + 1))) <= ready & given
            if k == 0:
                for c in range(AHEAD):
                    when_chunk(no_up, gather_part, c)
            when_chunk(no_up, gather_part, k + AHEAD)
            when_chunk(has_up, gather_part, k - lag)
            when_chunk(is_mid, retire, k - 2 * lag - 2)
            when_chunk(not_mid, retire, k - 3 * lag - 2)
            when_chunk(is_mid, spread_total, k - 2 * lag)
            when_chunk(not_mid, spread_total, k - 3 * lag)

    sent = set()

    def pair_done(c):
        if c not in sent:
            sent.add(c)
            pair_copy(c).wait_send()

    def down_grad(side, mine, only=None):
        hr = parts[0] // 2
        pr = min(256, hr)
        which = core if mine else 1 - core
        cols = pl.ds(side * (width // 2), width // 2)
        for p in range(hr // pr) if only is None else (only,):
            value = nn(act[pl.ds(pl.multiple_of(which * hr + p * pr, 16), pr), :], tok[:, cols]).astype(BF)
            for j in range(pr // (2 * r)):
                c = side * (hr // (2 * r)) + p * (pr // (2 * r)) + j
                packed = jnp.concatenate([value[2 * r * j : 2 * r * j + r], value[2 * r * j + r : 2 * r * (j + 1)]], axis=1)
                (ready if mine else given).add(c)
                if mine:
                    acc[rows_of(c), :] = packed
                else:
                    wd_v[rows_of(c), :] = packed
                    pair_copy(c).start()

    def weight_grad(n, lhs, rhs, mine):
        hr = parts[n] // 2
        pr = min(256, hr)
        which = core if mine else 1 - core
        for p in range(hr // pr):
            value = nn(lhs[pl.ds(pl.multiple_of(which * hr + p * pr, 16), pr), :], rhs[...]).astype(BF)
            begin = sum(parts[:n]) // 2 + p * pr
            held = [c for c in range(chunks) if begin <= starts[c] < begin + pr]
            (ready if mine else given).update(held)
            assert mine or held[-1] - PAIR < slot_now[0] - lag
            if mine:
                acc[pl.ds(begin, pr), :] = value
                continue
            for c in held:
                if c >= PAIR:
                    pair_done(c - PAIR)
                    pl.semaphore_wait(cr_pair, 1)
                wd_v[pair_rows(c), :] = value[starts[c] - begin : starts[c] - begin + sizes[c]]
                pair_copy(c).start()

    direct = [p for p in range(1, tp) if not (hops and p == 3)]
    columns = (pl.ds(width // 2, width // 2), pl.ds(0, width))
    sources = (cot, gb)

    def tok_rows(u, p, part):
        return tok.at[pl.ds(pl.multiple_of(flip(me, p) * block + part * half, half), half), columns[u]]

    def tok_copy(u, p, part):
        src = sources[u].at[pl.ds(part * half, half), columns[u]]
        return remote(src, tok_rows(u, 0, part), tok_ssem.at[u, p, part], tok_rsem.at[u, p, part], (md, flip(me, p)))

    def tok_arrived(u, p, part):
        return remote(tok_rows(u, p, part), tok_rows(u, p, part), tok_ssem.at[u, p, part], tok_rsem.at[u, p, part], (md, flip(me, p)))

    def tok_handed(u, part):
        came, goes = (1, 2) if part == 0 else (2, 1)
        return remote(
            tok_rows(u, came, part), tok_rows(u, came, part), tok_ssem.at[u, 3, part], tok_rsem.at[u, 3, part], (md, flip(me, goes))
        )

    def tok_start(u):
        for p in direct:
            for part in (0, 1) if p == 1 else (1, 0):
                tok_copy(u, p, part).start()

    def tok_hand_on(u):
        if hops:
            for part in (0, 1):
                tok_arrived(u, 1 if part == 0 else 2, part).wait_recv()
                tok_handed(u, part).start()
            for part in (0, 1):
                tok_arrived(u, 2 if part == 0 else 1, part).wait_recv()

    def tok_finish(u):
        for p in range(1, tp):
            if hops and p != 3:
                continue
            for part in (0, 1):
                tok_arrived(u, p, part).wait_recv()
        for p in direct:
            for part in (0, 1):
                tok_copy(u, p, part).wait_send()
        if hops:
            for part in (0, 1):
                tok_handed(u, part).wait_send()

    first_half, second_half = pl.ds(0, width // 2), pl.ds(width // 2, width // 2)
    halves = (first_half, second_half)

    def rs_copy(u, slot, part, p, ahead=False):
        return remote(
            snd.at[slot, halves[part]], rcv.at[slot, halves[part]], rs_ssem.at[u, slot, part], rs_rsem.at[u, slot, part], (md, flip(me, p))
        )

    def rs_send(u, p):
        if hops and p == 3:
            rs_copy(u, 2, 0, 1).start()
            rs_copy(u, 2, 1, 2).start()
        elif hops:
            rs_copy(u, p - 1, p - 1, p).start()
        else:
            for part in (0, 1):
                rs_copy(u, p - 1, part, p).start()

    def rs_merge(u, p):
        if not hops:
            return
        part = 2 - p
        rs_copy(u, 2, part, 3 - p).wait_recv()
        h = halves[part]
        snd[p - 1, h, :] = (snd[p - 1, h, :].astype(F32) + rcv[2, h, :].astype(F32)).astype(BF)
        rs_copy(u, p - 1, part, p).start()

    def rs_finish(u):
        for p in range(1, tp):
            if hops and p == 3:
                continue
            for part in (0, 1):
                rs_copy(u, p - 1, part, p).wait_recv()
        for p in range(1, tp):
            for part in (0, 1):
                rs_copy(u, p - 1, part, (1 if part == 0 else 2) if hops and p == 3 else p).wait_send()
        total = own[...]
        for p in range(1, tp):
            if not (hops and p == 3):
                total = total + rcv[p - 1].astype(F32)
        return total.T

    order = range(tp - 1, 0, -1) if not hops else (3, 1, 2)

    def gib_into(put, p):
        cols = pl.ds(pl.multiple_of(flip(me, p) * block, block), block)
        for d in range(0, width, 512):
            rows = pl.ds(d, 512)
            put(rows, nn(wg_v[rows, :], f1[:, cols]) + nn(wu_v[rows, :], f2[:, cols]))

    def down_into(put, p):
        cols = pl.ds(pl.multiple_of(flip(me, p) * block, block), block)
        for d in range(0, width, 512):
            rows = pl.ds(d, 512)
            put(rows, nn(wu_v[rows, :], act[:, cols]))

    def gia_into(put, p):
        cols = pl.ds(pl.multiple_of(flip(me, p) * block, block), block)
        for d in range(0, width, 512):
            rows = pl.ds(d, 512)
            put(rows, nn(wg_v[rows, 0 : qcols + kvcols], gqkv[:, cols]))

    def to_snd(p):
        def put(rows, value):
            snd[p - 1, rows, :] = value.astype(BF)

        return put

    def to_own(rows, value):
        own[rows, :] = value

    tok_start(0)
    for c in early:
        c.wait()
    for c in then:
        c.start()
    gsum[...] = jnp.zeros_like(gsum)
    mid_rows = hidden // 2
    def gate_grads(start):
        step = min(512, mid_rows)
        for i in range(length // QB):
            cols = pl.ds(i * QB, QB)
            for f in range(start, start + mid_rows, step):
                units = pl.ds(f, step)
                grad_act = nt(wd_v[units, :], tok[cols, :])
                f1[units, cols] = (grad_act * f1[units, cols].astype(F32)).astype(BF)
                f2[units, cols] = (grad_act * f2[units, cols].astype(F32)).astype(BF)

    down_grad(0, False, 0)
    down_grad(0, True, 0)
    z()
    for p in range(1, max(1, mid_rows // 256)):
        down_grad(0, False, p)
        down_grad(0, True, p)
    for c in then:
        c.wait()
    for c in late:
        c.start()
    z()
    tok_hand_on(0)
    z()
    tok_finish(0)
    down_grad(1, False)
    down_grad(1, True)
    z()
    gate_grads(mid_rows)
    z()
    for c in range(PAIR // 2):
        pair_done(c)
    rest = load(n1 + 3 + tp, wd.at[pl.ds(0, mid_rows)], wd_v.at[pl.ds(0, mid_rows)])
    rest.start()
    rest.wait()
    gate_grads(0)
    z()
    for c in late[:2]:
        c.wait()
    for n, p in enumerate(order):
        gib_into(to_snd(p), p)
        rs_send(0, p)
        if n == 1:
            z()
    late[2].wait()
    weight_grad(1, f1, ab, False)
    weight_grad(1, f1, ab, True)
    z(2)
    if hops:
        rs_merge(0, 1)
        rs_merge(0, 2)
    gib_into(to_own, 0)
    z(3)
    for c in late[3:]:
        c.wait()
    qkv_load = load(n1, wqkv, wg_v.at[:, pl.ds(0, qcols + kvcols)])
    qkv_load.start()
    down_load = load(n1 + 1, wdt, wu_v)
    down_load.start()

    grad_in = rs_finish(0)
    base_b, inv_b = normed(mid[...])
    back, gain_b = norm_back(grad_in, base_b, inv_b, gains[1:2, :])
    gs[...] = tok[own_rows, :].astype(F32) + back
    for n in range(4):
        gsum[4 + n : 5 + n, :] = gain_b[:, n * (width // 4) : (n + 1) * (width // 4)]
    gb[...] = gs[...].astype(BF)
    tok[own_rows, :] = gb[...]

    tok_start(1)
    z()
    weight_grad(2, f2, ab, False)
    z()
    weight_grad(2, f2, ab, True)
    z(2)
    a_load = load(n1 + 2, a_in, ab)
    a_load.start()
    tok_hand_on(1)
    z(2)
    tok_finish(1)

    weight_grad(3, mix, tok, False)
    weight_grad(3, mix, tok, True)
    for n in range(0, length, QB):
        cols = pl.ds(n, QB)
        gm_t[:, :, cols] = nt(wo_v[...], tok[cols, :]).astype(BF).reshape(heads, HD, QB)
    z()
    down_load.wait()
    for p in order:
        down_into(to_snd(p), p)
        rs_send(1, p)
    down_into(to_own, 0)
    z()

    dk[...] = jnp.zeros_like(dk)
    dv[...] = jnp.zeros_like(dv)
    for i in range(length // QB - 1, -1, -1):
        reach = (i + 1) * QB
        cols = pl.ds(i * QB, QB)
        same = segc[pl.ds(0, reach), 0:1] == segr[:, cols]
        later = lax.broadcasted_iota(jnp.int32, (reach, QB), 0) <= lax.broadcasted_iota(jnp.int32, (reach, QB), 1) + i * QB
        bias[pl.ds(0, reach), :] = jnp.where(same & later, 0.0, -1e30)

        def head(h, _, reach=reach, cols=cols):
            g = h // group
            s = nn(k_n[g, pl.ds(0, reach), :][:, :HD], q_t[h, :, cols]) * SCALE + bias[pl.ds(0, reach), :]
            p = jnp.exp(s - lse[h, :, cols])
            grad_p = nn(v_n[g, pl.ds(0, reach), :][:, :HD], gm_t[h, :, cols])
            delta = jnp.sum(p * grad_p, axis=0, keepdims=True)
            ds = (p * (grad_p - delta)).astype(BF)
            dq = nn(k_t[g, :, pl.ds(0, reach)], ds) * SCALE
            gqkv[pl.ds(pl.multiple_of(h * HD, 16), HD), cols] = unrot_rows(dq, cos_t[:, cols], sin_t[:, cols]).astype(BF)
            dk[g, :, pl.ds(0, reach)] += nt(q_t[h, :, cols], ds)
            dv[g, :, pl.ds(0, reach)] += nt(gm_t[h, :, cols], p.astype(BF))
            return 0

        lax.fori_loop(0, heads, head, 0)
        z()
        if i == length // QB - 2 and hops:
            rs_merge(1, 1)
            rs_merge(1, 2)
    for g in range(kv_heads):
        at = qcols + g * 2 * HD
        gqkv[pl.ds(at, HD), :] = unrot_rows(dk[g] * SCALE, cos_t[...], sin_t[...]).astype(BF)
        gqkv[pl.ds(at + HD, HD), :] = dv[g].astype(BF)
    a_load.wait()
    weight_grad(4, gqkv.at[pl.ds(0, qcols)], ab, False)
    weight_grad(4, gqkv.at[pl.ds(0, qcols)], ab, True)
    weight_grad(5, gqkv.at[pl.ds(qcols, kvcols)], ab, False)
    weight_grad(5, gqkv.at[pl.ds(qcols, kvcols)], ab, True)
    z()
    stage_res = rs_finish(1)
    gb[...] = (mid[...] + stage_res).astype(BF)
    res_copy = pltpu.make_async_copy(gb, res_out, out_sem.at[0])
    res_copy.start()
    for p in range(1, tp):
        signal(cr_rs, (md, flip(me, p)))
    pl.semaphore_wait(cr_rs, tp - 1)
    z()
    qkv_load.wait()
    for p in order:
        gia_into(to_snd(p), p)
        rs_send(2, p)
    gia_into(to_own, 0)
    z(2)
    if hops:
        rs_merge(2, 1)
        rs_merge(2, 2)
    z(3)
    grad_in = rs_finish(2)
    base_a, inv_a = normed(hid[...].astype(F32))
    back, gain_a = norm_back(grad_in, base_a, inv_a, gains[0:1, :])
    hid[...] = (gs[...] + back).astype(BF)
    hid_copy = pltpu.make_async_copy(hid, hid_out, out_sem.at[1])
    hid_copy.start()
    for n in range(4):
        gsum[n : n + 1, :] = gain_a[:, n * (width // 4) : (n + 1) * (width // 4)]

    stages = []
    bit = 1
    while bit < dp:
        stages.append((flip(md, bit), me))
        bit *= 2
    bit = 1
    while bit < tp:
        stages.append((md, flip(me, bit)))
        bit *= 2
    for n, peer in enumerate(stages):
        c = remote(gsum, gland.at[n], gain_ssem.at[n], gain_rsem.at[n], peer)
        c.start()
        z()
        c.wait()
        gsum[...] = gsum[...] + gland[n]
    gain_copy = pltpu.make_async_copy(gsum.at[pl.ds(0, 8)], gain_out, out_sem.at[2])
    gain_copy.start()

    last = chunks + 3 * lag + 2
    z(last - slot_now[0])
    for c in (res_copy, hid_copy, gain_copy):
        c.wait()
    for c in range(chunks):
        remote(in_ring(dn_ring, c), sums_out.at[1 - core, rows_of(c)], sib_ssem.at[c], sib_rsem.at[c], sibling).wait_recv()

        @pl.when(is_mid)
        def _(c=c):
            part_copy(c, dn_ring, dn_rsem).wait_send()

        @pl.when(not_mid)
        def _(c=c):
            part_copy(c, up_ring, up_rsem).wait_send()

        pair_done(c)


def backward(mesh, cot, cot_all, a, b, q, kt, k, v, lse, mix, f1, f2, act, wdt, mid, hid, wqkv, wo, wg, wu, wd, gains, segc, segr, cos_t, sin_t):
    tp, dp = mesh.shape["tp"], mesh.shape["dp"]
    block, width = hid.shape
    length = tp * block
    hidden = wg.shape[1]
    heads = wo.shape[0] // HD
    kv_heads = (wqkv.shape[1] - heads * HD) // (2 * HD)
    qcols, kvcols = heads * HD, kv_heads * 2 * HD
    r = hidden // PAIR
    half_rows = (3 * hidden + 2 * qcols + kvcols) // 2
    chunks = (3 * hidden + 2 * qcols) // 2 // r + kvcols // 2 // (r // FINE)
    steps = (dp - 1).bit_length() + (tp - 1).bit_length()
    sds = jax.ShapeDtypeStruct
    outs = [
        sds((block, width), BF),
        sds((block, width), BF),
        sds((2, half_rows, width), BF),
        sds((8, width // 4), F32),
    ]
    dma = pltpu.SemaphoreType.DMA
    reg = pltpu.SemaphoreType.REGULAR
    scratch = [
        pltpu.VMEM((length, width), BF),
        pltpu.VMEM((hidden, length), BF),
        pltpu.VMEM((hidden, width), BF),
        pltpu.VMEM((hidden, length), BF),
        pltpu.VMEM((hidden, length), BF),
        pltpu.VMEM((width, hidden), BF),
        pltpu.VMEM((width, hidden), BF),
        pltpu.VMEM((length, width), BF),
        pltpu.VMEM((tp - 1, width, block), BF),
        pltpu.VMEM((tp - 1, width, block), BF),
        pltpu.VMEM((half_rows, width), BF),
        pltpu.VMEM((PAIR * r, width), BF),
        pltpu.VMEM((RING, r, width), BF),
        pltpu.VMEM((RING, r, width), BF),
        pltpu.VMEM((heads, HD, length), BF),
        pltpu.VMEM((kv_heads, HD, length), BF),
        pltpu.VMEM((kv_heads, length, 128), BF),
        pltpu.VMEM((kv_heads, length, 128), BF),
        pltpu.VMEM((heads, 1, length), F32),
        pltpu.VMEM((qcols, length), BF),
        pltpu.VMEM((heads, HD, length), BF),
        pltpu.VMEM((qcols + kvcols, length), BF),
        pltpu.VMEM((kv_heads, HD, length), F32),
        pltpu.VMEM((kv_heads, HD, length), F32),
        pltpu.VMEM((length, QB), F32),
        pltpu.VMEM((block, width), F32),
        pltpu.VMEM((block, width), BF),
        pltpu.VMEM((block, width), F32),
        pltpu.VMEM((width, block), F32),
        pltpu.VMEM((block, width), BF),
        pltpu.VMEM((qcols, width), BF),
        pltpu.VMEM((8, width // 4), F32),
        pltpu.VMEM((steps, 8, width // 4), F32),
        dma((4 + 2 * tp + 20,)),
        dma((3,)),
        dma((chunks,)), dma((chunks,)), dma((chunks,)), dma((chunks,)), dma((chunks,)), dma((chunks,)), dma((chunks,)), dma((chunks,)), dma((chunks,)),
        dma((3, tp - 1, 2)), dma((3, tp - 1, 2)),
        dma((2, tp, 2)), dma((2, tp, 2)),
        dma((steps,)), dma((steps,)),
        reg, reg, reg, reg,
    ]
    any_ = pl.BlockSpec(memory_space=pl.ANY)
    vmem = pl.BlockSpec(memory_space=pltpu.VMEM)
    return pl.pallas_call(
        functools.partial(backward_kernel, tp, dp),
        out_shape=outs,
        in_specs=[any_] * 21 + [vmem] * 5,
        out_specs=[any_] * len(outs),
        scratch_shapes=scratch,
        compiler_params=pltpu.CompilerParams(collective_id=1, has_side_effects=True, vmem_limit_bytes=62 * 2**20),
        name="backward",
    )(cot, cot_all, a, b, q, kt, k, v, lse, mix.reshape(qcols, length), f1, f2, act, wdt, mid, hid, wqkv, wo, wg, wu, wd, gains, segc, segr, cos_t, sin_t)


def finish_kernel(sums, res, hid, gain, res_out, hid_out, query_out, keyval_out, output_out, gate_out, up_out, down_out, gain_out,
                  in_v, nat_v, wide_v, turn_v, query_v, pass_v, in_sem, nat_sem, wide_sem, turn_sem, query_sem, copy_sem):
    width = sums.shape[2]
    passing = [
        pltpu.make_async_copy(res, pass_v.at[0], copy_sem.at[0]),
        pltpu.make_async_copy(hid, pass_v.at[1], copy_sem.at[1]),
    ]
    copies = [
        pltpu.make_async_copy(pass_v.at[0], res_out, copy_sem.at[0]),
        pltpu.make_async_copy(pass_v.at[1], hid_out, copy_sem.at[1]),
    ]
    outs = (down_out, gate_out, up_out, output_out, query_out, keyval_out)
    flat = (True, False, False, True, False, True)
    total = [o.shape[0] if f else o.shape[1] for o, f in zip(outs, flat)]
    tasks, at = [], 0
    for n, rows in enumerate(total):
        hr = rows // 2
        if n == 0:
            for core in (0, 1):
                for side in (0, 1):
                    tasks.append((n, [(core, at + side * (hr // 2), hr // 2)], core * hr, side))
        elif n < 3:
            step = min(256, hr)
            for core in (0, 1):
                for p in range(0, hr, step):
                    tasks.append((n, [(core, at + p, step)], core * hr + p, step))
        else:
            tasks.append((n, [(0, at, hr), (1, at, hr)], 0, rows))
        at += hr
    depth = in_v.shape[0]
    keep = nat_v.shape[0]

    def loads(i):
        _, pieces, _, _ = tasks[i]
        to, out = 0, []
        for j, (core, row, rows) in enumerate(pieces):
            out.append(pltpu.make_async_copy(sums.at[core, pl.ds(row, rows)], in_v.at[i % depth, pl.ds(to, rows)], in_sem.at[i % depth, j]))
            to += rows
        return out

    for i in range(min(depth - 1, len(tasks))):
        for c in loads(i):
            c.start()
    for c in passing:
        c.start()
    nat_busy, turn_busy, wide_busy, tail = {}, {}, {}, []
    nats = turns = wides = 0
    rows_r = total[0] // PAIR
    for i, (n, _, row, rows) in enumerate(tasks):
        if i == 2:
            for p, c in zip(passing, copies):
                p.wait()
                c.start()
        if i + depth - 1 < len(tasks):
            for c in loads(i + depth - 1):
                c.start()
        for c in loads(i):
            c.wait()
        if n == 0:
            slot = wides % 2
            wides += 1
            if slot in wide_busy:
                wide_busy.pop(slot).wait()
            r = rows_r
            for j in range(total[0] // 2 // (2 * r)):
                for k in (0, 1):
                    wide_v[slot, pl.ds((2 * j + k) * r, r), :] = in_v[
                        i % depth, pl.ds(j * r, r), pl.ds(k * (width // 2), width // 2)
                    ].astype(F32)
            c = pltpu.make_async_copy(
                wide_v.at[slot], outs[n].at[pl.ds(row, total[0] // 2), pl.ds(rows * (width // 2), width // 2)], wide_sem.at[slot]
            )
            wide_busy[slot] = c
        elif flat[n]:
            slot = nats % keep
            nats += 1
            if slot in nat_busy:
                nat_busy.pop(slot).wait()
            nat_v[slot, pl.ds(0, rows), :] = in_v[i % depth, pl.ds(0, rows), :].astype(F32)
            c = pltpu.make_async_copy(nat_v.at[slot, pl.ds(0, rows)], outs[n].at[pl.ds(row, rows)], nat_sem.at[slot])
            nat_busy[slot] = c
        elif n < 3:
            slot = turns % keep
            turns += 1
            if slot in turn_busy:
                turn_busy.pop(slot).wait()
            turn_v[slot] = in_v[i % depth, pl.ds(0, rows), :].T.astype(F32)
            c = pltpu.make_async_copy(turn_v.at[slot], outs[n].at[:, pl.ds(row, rows)], turn_sem.at[slot])
            turn_busy[slot] = c
        else:
            query_v[...] = in_v[i % depth, pl.ds(0, rows), :].T.astype(F32)
            c = pltpu.make_async_copy(query_v, outs[n], query_sem)
            tail.append(c)
        c.start()
    for n in range(8):
        gain_out[n // 4 : n // 4 + 1, pl.ds(n % 4 * (width // 4), width // 4)] = gain[n : n + 1, :]
    for c in [*nat_busy.values(), *turn_busy.values(), *wide_busy.values(), *tail, *copies]:
        c.wait()


def finish(sums, res, hid, gain, hidden, qcols, kvcols):
    width = sums.shape[2]
    sds = jax.ShapeDtypeStruct
    outs = [
        sds(res.shape, BF), sds(hid.shape, BF),
        sds((width, qcols), F32), sds((kvcols, width), F32), sds((qcols, width), F32),
        sds((width, hidden), F32), sds((width, hidden), F32), sds((hidden, width), F32),
        sds((2, width), F32),
    ]
    dma = pltpu.SemaphoreType.DMA
    any_ = pl.BlockSpec(memory_space=pl.ANY)
    vmem = pl.BlockSpec(memory_space=pltpu.VMEM)
    tall = max(min(256, hidden // 2), qcols, kvcols)
    step = min(256, hidden // 2)
    return pl.pallas_call(
        finish_kernel,
        out_shape=outs,
        in_specs=[any_] * 3 + [vmem],
        out_specs=[any_] * 8 + [vmem],
        scratch_shapes=[
            pltpu.VMEM((4, tall, width), BF),
            pltpu.VMEM((3, tall, width), F32),
            pltpu.VMEM((2, hidden // 2, width // 2), F32),
            pltpu.VMEM((3, width, step), F32),
            pltpu.VMEM((width, qcols), F32),
            pltpu.VMEM((2, *res.shape), BF),
            dma((4, 2)), dma((3,)), dma((2,)), dma((3,)), dma, dma((2,)),
        ],
        compiler_params=pltpu.CompilerParams(vmem_limit_bytes=62 * 2**20),
        name="finish",
    )(sums, res, hid, gain)


def local(mesh, hidden, segments, cotangent, w_query, w_keyval, w_output, w_gate, w_up, w_down, gains):
    width = hidden.shape[2]
    hid, cot, gain = hidden[0], cotangent[0], gains[0]
    wq, wo, wg, wu, wd = w_query[0], w_output[0], w_gate[0], w_up[0], w_down[0]
    wkv_t = w_keyval[0].transpose(1, 2, 0).reshape(-1, width)
    inverse = ROPE_BASE ** (-(jnp.arange(HALF, dtype=F32) * 2.0) / HD)
    wqkv, segc, cos_t, sin_t, a, b, cot_all, q, kt, k, v, lse, mix, f1, f2, act, wdt, mid = forward(
        mesh, hid, cot, wq, wkv_t, wo, wg, wu, wd, gain, segments, inverse[:, None]
    )
    result, grad_hidden, sums, gain_sum = backward(
        mesh, cot, cot_all, a, b, q, kt, k, v, lse, mix, f1, f2, act, wdt, mid, hid,
        wqkv, wo, wg, wu, wd, gain, segc, segments, cos_t, sin_t,
    )
    result, grad_hidden, query, keyval, output, gate, up, down, gain_sum = finish(
        sums, result, grad_hidden, gain_sum, wd.shape[0], wo.shape[0], wkv_t.shape[0]
    )
    keyval = keyval.reshape(*w_keyval.shape[2:], width).transpose(2, 0, 1)
    return tuple(x[None] for x in (result, grad_hidden, query, keyval, output, gate, up, down, gain_sum))


def solution(mesh):
    split = P("dp", "tp", None)
    columns, rows = P(None, None, "tp"), P(None, "tp", None)
    heads = P(None, None, "tp", None)
    return jax.shard_map(
        functools.partial(local, mesh),
        mesh=mesh,
        in_specs=(split, P("dp", None), split, columns, heads, rows, columns, columns, rows, P()),
        out_specs=(split, split, columns, heads, rows, columns, columns, rows, P()),
        check_vma=False,
    )
```
